256 devices in a mesh: dp: 4 (over y), fsdp: 64 (over x, z, core).
Axes of the slice: x: 4, y: 4, z: 8, core: 2. Of those that a mesh axis runs over, the one named last changes fastest.
Arguments:
- tokens: bfloat16 [4, 16384, 768], P('dp', 'fsdp'), may hold values from -6 to 6
- image_ids: int32 [4, 16384], P('dp'), may hold values from 0 to 191, never falling along the last dimension, each value on 1 to 256 neighbouring positions
- patch_row: int32 [4, 16384], P('dp', 'fsdp'), may hold values from 0 to 31
- patch_col: int32 [4, 16384], P('dp', 'fsdp'), may hold values from 0 to 31
- cotangent: bfloat16 [4, 16384, 768], P('dp', 'fsdp'), may hold values from -6 to 6
- norm1_gain: bfloat16 [768], P('fsdp'), may hold values from 0.5 to 1.5
- norm1_bias: bfloat16 [768], P('fsdp'), may hold values from -1 to 1
- qkv_weight: bfloat16 [768, 2304], P('fsdp'), may hold values from -0.21875 to 0.21875
- qkv_bias: bfloat16 [2304], P('fsdp'), may hold values from -1 to 1
- frequencies: bfloat16 [2, 384], P(None, 'fsdp'), may hold values from -0.59765625 to 0.59765625
- out_weight: bfloat16 [768, 768], P('fsdp'), may hold values from -0.875 to 0.875
- out_bias: bfloat16 [768], P('fsdp'), may hold values from -1 to 1
- norm2_gain: bfloat16 [768], P('fsdp'), may hold values from 0.5 to 1.5
- norm2_bias: bfloat16 [768], P('fsdp'), may hold values from -1 to 1
- up_weight: bfloat16 [768, 3072], P('fsdp'), may hold values from -0.21875 to 0.21875
- up_bias: bfloat16 [3072], P('fsdp'), may hold values from -1 to 1
- down_weight: bfloat16 [3072, 768], P('fsdp'), may hold values from -0.109375 to 0.109375
- down_bias: bfloat16 [768], P('fsdp'), may hold values from -1 to 1
Outputs:
- output: bfloat16 [4, 16384, 768], P('dp', 'fsdp')
- input_grad: float32 [4, 16384, 768], P('dp', 'fsdp')
- norm1_gain_grad: float32 [768], P('fsdp')
- norm1_bias_grad: float32 [768], P('fsdp')
- qkv_weight_grad: float32 [768, 2304], P('fsdp')
- qkv_bias_grad: float32 [2304], P('fsdp')
- frequencies_grad: float32 [2, 384], P(None, 'fsdp')
- out_weight_grad: float32 [768, 768], P('fsdp')
- out_bias_grad: float32 [768], P('fsdp')
- norm2_gain_grad: float32 [768], P('fsdp')
- norm2_bias_grad: float32 [768], P('fsdp')
- up_weight_grad: float32 [768, 3072], P('fsdp')
- up_bias_grad: float32 [3072], P('fsdp')
- down_weight_grad: float32 [3072, 768], P('fsdp')
- down_bias_grad: float32 [768], P('fsdp')
The draws below stay inside these ranges and needn't reach their ends.
Inputs may be any that keep to these rules, and one draw needn't show every extreme that they name: Within a sequence image_ids never fall, and each id names 1 to 256 consecutive patches.
All inputs are finite; a program needn't handle non-finite values.
Results may differ from the reference program's by a relative error of at most 0.02.
Values may be sent and summed in bfloat16 or wider, within the bound.
No kernel may reach another device: no remote copies, remote signals or barrier semaphores. Data moves between devices by JAX's collectives and lax.ppermute only.
A program may use at most 128 MiB of HBM per device.

```python
import math
import jax
import jax.numpy as jnp
import numpy as np
from jax import lax

D = 768
HEADS = 12
HEAD_DIM = 64
FF = 3072
TOK_DEV = 256
SEQS = 4
SEQ = 16384
N_FSDP = 64


def plant(entries, stream_key, smallest, high):
    dims = entries.shape
    place = [jax.random.randint(jax.random.fold_in(stream_key, axis), (), 0, dims[axis]) for axis in range(len(dims))]
    entries = entries.at[tuple(place)].set(smallest)
    longest = dims.index(max(dims))
    place[longest] = (place[longest] + 1) % dims[longest]
    return entries.at[tuple(place)].set(high)


def block_levels(own_key, shape, cuts, low, largest):
    loudness, own = 1.0, jax.random.fold_in(own_key, 6)
    for position, blocks in cuts:
        draws = jnp.exp(jax.random.uniform(jax.random.fold_in(own, position), (blocks,), jnp.float32, low / len(cuts), largest / len(cuts)))
        loudness = loudness * jnp.repeat(draws, shape[position] // blocks).reshape([-1 if axis == position else 1 for axis in range(len(shape))])
    return loudness


def split_up(amount, total, limit, skew):
    loads = [(1 << 20) // math.isqrt(grade ** skew) + 1 for grade in range(2, amount + 1)]
    spare, given = total - limit - (amount - 1), [1] * (amount - 1)
    while spare > 0:
        free = [i for i in range(amount - 1) if given[i] < limit]
        pool, budget = sum([loads[i] for i in free]), spare
        for i in free:
            more = min(limit - given[i], max(1, budget * loads[i] // pool), spare)
            given[i] = given[i] + more
            spare = spare - more
    return np.array([limit] + given)


def ragged(own_key, count, total, bound, lean):
    if count == 2:
        one = jax.random.randint(own_key, (), max(1, total - bound), min(bound, total - 1) + 1)
        return jnp.stack([one, total - one])
    tallies = jnp.asarray(split_up(count, total, bound, lean), jnp.int32)
    couples = (count - 1) // 2
    donor, receiver = tallies[1:1 + 2 * couples:2], tallies[2:2 + 2 * couples:2]
    slack = jnp.minimum(donor - 1, bound - receiver)
    passed = jax.random.randint(jax.random.fold_in(own_key, 1), (couples,), 0, 1 << 20) % (slack + 1)
    tallies = tallies.at[1:1 + 2 * couples:2].set(donor - passed).at[2:2 + 2 * couples:2].set(receiver + passed)
    return tallies[jax.random.permutation(jax.random.fold_in(own_key, 2), count)]


def gaussian(rng, shape, deviation, reach, shards=(), held_as=jnp.bfloat16):
    drawn = deviation * jax.random.normal(rng, shape, jnp.float32)
    if shards:
        drawn = drawn * block_levels(rng, shape, shards, -0.22, 0.18)
    return jnp.clip(drawn, -reach, reach).astype(held_as)


def setup_inputs(seed: int = 0) -> dict:
    key_list = jax.random.split(jax.random.key(seed), 19)
    tokens = gaussian(key_list[0], (SEQS, SEQ, D), 1.0, 6.0, ((0, 4), (1, 64)))
    image_ids = jax.vmap(lambda own: jnp.searchsorted(jnp.cumsum(ragged(own, 3 * N_FSDP, SEQ, TOK_DEV, 2)), jnp.arange(SEQ), side="right"))(jax.random.split(key_list[1], SEQS)).reshape((SEQS, SEQ)).astype(jnp.int32)
    patch_row = plant(jax.random.randint(key_list[2], (SEQS, SEQ), 0, 32), jax.random.fold_in(key_list[2], 1), 0, 31).astype(jnp.int32)
    patch_col = plant(jax.random.randint(key_list[3], (SEQS, SEQ), 0, 32), jax.random.fold_in(key_list[3], 1), 0, 31).astype(jnp.int32)
    cotangent = gaussian(key_list[4], (SEQS, SEQ, D), 1.0, 6.0, ((0, 4), (1, 64)))
    norm1_gain = jnp.clip(1.0 + 0.1 * jax.random.normal(key_list[5], (D,), jnp.float32), 0.5, 1.5).astype(jnp.bfloat16)
    norm1_bias = gaussian(key_list[6], (D,), 0.2, 1.0, ((0, 64),))
    qkv_weight = gaussian(key_list[7], (D, 3 * D), D ** -0.5, 0.21875, ((0, 64),))
    qkv_bias = gaussian(key_list[8], (3 * D,), 0.2, 1.0, ((0, 64),))
    frequencies = jnp.clip(jax.random.uniform(key_list[9], (2, D // 2), jnp.float32, -0.59765625, 0.59765625) * block_levels(key_list[9], (2, D // 2), ((1, 64),), -0.4, 0.0), -0.59765625, 0.59765625).astype(jnp.bfloat16)
    out_weight = gaussian(key_list[10], (D, D), (D // 16) ** -0.5, 0.875, ((0, 64),))
    out_bias = gaussian(key_list[11], (D,), 0.2, 1.0, ((0, 64),))
    norm2_gain = jnp.clip(1.0 + 0.1 * jax.random.normal(key_list[12], (D,), jnp.float32), 0.5, 1.5).astype(jnp.bfloat16)
    norm2_bias = gaussian(key_list[13], (D,), 0.2, 1.0, ((0, 64),))
    up_weight = gaussian(key_list[14], (D, FF), D ** -0.5, 0.21875, ((0, 64),))
    up_bias = gaussian(key_list[15], (FF,), 0.2, 1.0, ((0, 64),))
    down_weight = gaussian(key_list[16], (FF, D), FF ** -0.5, 0.109375, ((0, 64),))
    down_bias = gaussian(key_list[17], (D,), 0.2, 1.0, ((0, 64),))
    return dict(tokens=tokens, image_ids=image_ids, patch_row=patch_row, patch_col=patch_col, cotangent=cotangent, norm1_gain=norm1_gain, norm1_bias=norm1_bias, qkv_weight=qkv_weight, qkv_bias=qkv_bias, frequencies=frequencies, out_weight=out_weight, out_bias=out_bias, norm2_gain=norm2_gain, norm2_bias=norm2_bias, up_weight=up_weight, up_bias=up_bias, down_weight=down_weight, down_bias=down_bias)


@jax.custom_vjp
def low(v):
    return lax.optimization_barrier(v.astype(jnp.bfloat16)).astype(jnp.float32)

@jax.custom_vjp
def low_back(v):
    return v

def low_keep(v):
    return (low(v), None)

def low_pass(kept, grad):
    return (grad,)

def back_keep(v):
    return (v, None)

def back_low(kept, grad):
    return (low(grad),)
low.defvjp(low_keep, low_pass)
low_back.defvjp(back_keep, back_low)

def matmul(left, right):
    return jnp.dot(left, right, precision=lax.Precision.HIGHEST)

def norm(value, gain, bias):
    centred = value - lax.optimization_barrier(jnp.mean(value, axis=-1, keepdims=True))
    spread = lax.optimization_barrier(jnp.mean(centred * centred, axis=-1, keepdims=True))
    return centred * lax.rsqrt(spread + 1e-06) * gain + bias

def rotate(field, freqs, rows, cols):
    length = field.shape[0]
    half = HEAD_DIM // 2
    angle = rows[:, None] * freqs[0][None, :] + cols[:, None] * freqs[1][None, :]
    cosine = jnp.cos(angle).reshape(length, HEADS, half)
    sine = jnp.sin(angle).reshape(length, HEADS, half)
    parts = field.reshape(length, HEADS, 2, half)
    first = parts[:, :, 0]
    second = parts[:, :, 1]
    turned = jnp.stack([first * cosine - second * sine, first * sine + second * cosine], axis=2)
    return turned.reshape(length, HEADS * HEAD_DIM)

def attend(query_low, key_low, value_low, image_ids):
    length = query_low.shape[0]
    scale = 1.0 / math.sqrt(HEAD_DIM)
    key_pad = jnp.pad(key_low, ((TOK_DEV, TOK_DEV), (0, 0)))
    value_pad = jnp.pad(value_low, ((TOK_DEV, TOK_DEV), (0, 0)))
    ids_pad = jnp.pad(image_ids + 1, (TOK_DEV, TOK_DEV))

    def block(index):
        start = (index * TOK_DEV).astype(jnp.int32)
        queries = lax.dynamic_slice_in_dim(query_low, start, TOK_DEV, 0).reshape(TOK_DEV, HEADS, HEAD_DIM)
        keys = lax.dynamic_slice_in_dim(key_pad, start, 3 * TOK_DEV, 0).reshape(3 * TOK_DEV, HEADS, HEAD_DIM)
        values = lax.dynamic_slice_in_dim(value_pad, start, 3 * TOK_DEV, 0).reshape(3 * TOK_DEV, HEADS, HEAD_DIM)
        own_ids = lax.dynamic_slice_in_dim(ids_pad, start + TOK_DEV, TOK_DEV, 0)
        near_ids = lax.dynamic_slice_in_dim(ids_pad, start, 3 * TOK_DEV, 0)
        scores = jnp.einsum('qhd,khd->hqk', queries, keys, precision=lax.Precision.HIGHEST) * scale
        scores = low_back(scores)
        keep = own_ids[None, :, None] == near_ids[None, None, :]
        scores = jnp.where(keep, scores, -1e+30)
        top = lax.optimization_barrier(jnp.max(scores, axis=-1, keepdims=True))
        expo = jnp.exp(scores - top)
        probs = expo / lax.optimization_barrier(jnp.sum(expo, axis=-1, keepdims=True))
        mixed = jnp.einsum('hqk,khd->qhd', low(probs), values, precision=lax.Precision.HIGHEST)
        return mixed.reshape(TOK_DEV, HEADS * HEAD_DIM)
    blocks = lax.map(jax.checkpoint(block), jnp.arange(length // TOK_DEV, dtype=jnp.int32))
    return blocks.reshape(length, HEADS * HEAD_DIM)

def forward(inputs, params, image_ids, rows, cols):
    gain_one, bias_one, qkv_w, qkv_b, freqs, out_w, out_b, gain_two, bias_two, up_w, up_b, down_w, down_b = params
    width = inputs.shape[1]
    first = low(norm(inputs, gain_one, bias_one))
    mixed = low_back(matmul(first, qkv_w) + qkv_b)
    query = mixed[:, :width]
    key = mixed[:, width:2 * width]
    value = mixed[:, 2 * width:]
    query_low = low(rotate(query, freqs, rows, cols))
    key_low = low(rotate(key, freqs, rows, cols))
    value_low = low(value)
    attended = low(low_back(attend(query_low, key_low, value_low, image_ids)))
    middle = inputs + low_back(matmul(attended, out_w) + out_b)
    second = low(norm(middle, gain_two, bias_two))
    upward = low_back(matmul(second, up_w) + up_b)
    active = low(jax.nn.gelu(upward, approximate=False))
    return middle + low_back(matmul(active, down_w) + down_b)

def reference(tokens, image_ids, patch_row, patch_col, cotangent, norm1_gain, norm1_bias, qkv_weight, qkv_bias, frequencies, out_weight, out_bias, norm2_gain, norm2_bias, up_weight, up_bias, down_weight, down_bias):
    params = tuple((w.astype(jnp.float32) for w in (norm1_gain, norm1_bias, qkv_weight, qkv_bias, frequencies, out_weight, out_bias, norm2_gain, norm2_bias, up_weight, up_bias, down_weight, down_bias)))

    def one(totals, inputs):
        sequence, ids, rows, cols, grad_out = inputs
        rows_f = rows.astype(jnp.float32)
        cols_f = cols.astype(jnp.float32)
        result, back = jax.vjp(lambda v, p: forward(v, p, ids, rows_f, cols_f), sequence.astype(jnp.float32), params)
        input_grad, param_grads = back(grad_out.astype(jnp.float32))
        totals = tuple((t + g for t, g in zip(totals, param_grads)))
        return (totals, (result.astype(jnp.bfloat16), input_grad))
    zeros = tuple((jnp.zeros_like(p) for p in params))
    totals, (outputs, input_grads) = lax.scan(one, zeros, (tokens, image_ids, patch_row, patch_col, cotangent))
    return (outputs, input_grads, totals[0], totals[1], totals[2], totals[3], totals[4], totals[5], totals[6], totals[7], totals[8], totals[9], totals[10], totals[11], totals[12])
```

```python
import jax
import jax.numpy as jnp
from jax import lax
from jax.experimental import pallas as pl
from jax.experimental.pallas import tpu as pltpu
from jax.sharding import Mesh, PartitionSpec as P

NX, NY, NZ = 4, 4, 8
HEADS = 12
LOCAL_HEADS = 6
WIDTH = 768
HALF = 384
FF_HALF = 1536
TOK = 256
CHIP_TOK = 512
MASKED = -1e30
BF = jnp.bfloat16
F32 = jnp.float32
MIB = 1 << 20


def fetch(value, axis, size, step):
    return lax.ppermute(value, axis, [((i + step) % size, i) for i in range(size)])


def swap(value):
    return lax.ppermute(value, "c", [(0, 1), (1, 0)])


def in_core_order(core, own, other):
    first = jnp.where(core == 0, own, other)
    second = jnp.where(core == 0, other, own)
    return jnp.concatenate([first, second], axis=0)


def unroll_ring(parts, place):
    size = len(parts)
    twice = jnp.stack(parts + parts[:-1])
    return lax.dynamic_slice_in_dim(twice, lax.rem(size - place, size), size, 0)


def dot(a, b):
    return jnp.dot(a, b, preferred_element_type=F32)


def dot_nt(a, b):
    return lax.dot_general(a, b, (((1,), (1,)), ((), ())), preferred_element_type=F32)


def dot_tn(a, b):
    return lax.dot_general(a, b, (((0,), (0,)), ((), ())), preferred_element_type=F32)


def spread(block, axes, count):
    rows, cols = block.shape
    copies = jnp.broadcast_to(block[None], (count, rows, cols)).reshape(count * rows, cols)
    got = lax.all_to_all(copies, axes, split_axis=0, concat_axis=0, tiled=True)
    return got.reshape(count, rows, cols)


def deal(blocks, axes):
    count, rows, cols = blocks.shape
    got = lax.all_to_all(
        blocks.reshape(count * rows, cols), axes, split_axis=0, concat_axis=0, tiled=True
    )
    return jnp.sum(got.reshape(count, rows, cols).astype(F32), axis=0)


def scatter_sum(blocks, axis):
    count, rows, cols = blocks.shape
    return lax.psum_scatter(
        blocks.reshape(count * rows, cols), axis, scatter_dimension=0, tiled=True
    )


def masks(key_ids, query_ids, tile):
    keys = key_ids[TOK * tile : TOK * tile + 3 * TOK, :]
    queries = query_ids[0:1, TOK * tile : TOK * tile + TOK]
    return keys == queries


def two_heads(block):
    lane = lax.broadcasted_iota(jnp.int32, block.shape, 1)
    zero = jnp.zeros_like(block)
    return jnp.concatenate(
        [jnp.where(lane < 64, block, zero), jnp.where(lane < 64, zero, block)], axis=0
    )


def by_head(first, second):
    row = lax.broadcasted_iota(jnp.int32, first.shape, 0)
    return jnp.where(row < 64, first, second)


def window(refs, tile, which):
    return jnp.concatenate([r[which] for r in refs[tile : tile + 3]], axis=0)


def attend_kernel(
    core_ref, q_ref, prev_ref, kv0_ref, kv1_ref, next_ref, kid_ref, qid_ref, w_ref,
    o_ref, lse_ref, part_ref, acc_ref,
):
    step = pl.program_id(0)
    kv = (prev_ref, kv0_ref, kv1_ref, next_ref)
    outs = []
    for tile in range(2):
        k = window(kv, tile, 0)
        v = window(kv, tile, 1)
        q2 = two_heads(q_ref[TOK * tile : TOK * tile + TOK, :] * jnp.asarray(0.125, BF))
        keep = masks(kid_ref[...], qid_ref[...], tile)
        scores = dot_nt(k, q2)
        halves = []
        for h in range(2):
            s = jnp.where(keep, scores[:, TOK * h : TOK * h + TOK], MASKED)
            top = jnp.max(s, axis=0, keepdims=True)
            expo = jnp.exp(s - top)
            total = jnp.sum(expo, axis=0, keepdims=True)
            lse_ref[0, h : h + 1, TOK * tile : TOK * tile + TOK] = top + jnp.log(total)
            p = (expo * (1.0 / total)).astype(BF)
            halves.append(dot_tn(v, p))
        out = jnp.transpose(by_head(*halves)).astype(BF)
        o_ref[TOK * tile : TOK * tile + TOK, :] = out
        outs.append(out)
    o = jnp.concatenate(outs, axis=0)
    term = dot(o, w_ref[...])

    @pl.when(step == 0)
    def _():
        acc_ref[...] = term

    @pl.when(step > 0)
    def _():
        acc_ref[...] += term

    @pl.when(step == 2)
    def _():
        part_ref[...] = acc_ref[...].astype(BF)


def pair_spec():
    return pl.BlockSpec((CHIP_TOK, 128), lambda i, c: (0, i))


def kv_spec():
    return pl.BlockSpec((2, TOK, 128), lambda i, c: (0, 0, i))


def whole(shape):
    zeros = (0,) * len(shape)
    return pl.BlockSpec(shape, lambda i, c: zeros)


def attend(core, q, kv, key_ids, query_ids, weights):
    return pl.pallas_call(
        attend_kernel,
        grid_spec=pltpu.PrefetchScalarGridSpec(
            num_scalar_prefetch=1,
            grid=(3,),
            in_specs=[pair_spec()]
            + [kv_spec()] * 4
            + [
                whole((4 * TOK, 1)),
                whole((1, CHIP_TOK)),
                pl.BlockSpec((128, WIDTH), lambda i, c: (i, 0)),
            ],
            out_specs=[
                pair_spec(),
                pl.BlockSpec((1, 2, CHIP_TOK), lambda i, c: (i, 0, 0)),
                whole((CHIP_TOK, WIDTH)),
            ],
            scratch_shapes=[pltpu.VMEM((CHIP_TOK, WIDTH), F32)],
        ),
        out_shape=[
            jax.ShapeDtypeStruct((CHIP_TOK, HALF), BF),
            jax.ShapeDtypeStruct((3, 2, CHIP_TOK), F32),
            jax.ShapeDtypeStruct((CHIP_TOK, WIDTH), BF),
        ],
        compiler_params=pltpu.CompilerParams(vmem_limit_bytes=48 * MIB),
        cost_estimate=pl.CostEstimate(
            flops=2 * 10**9, bytes_accessed=6 * MIB, transcendentals=2400000
        ),
        name="attend",
    )(core, q, *kv, key_ids, query_ids, weights)


def attend_back_kernel(
    core_ref, q_ref, prev_ref, kv0_ref, kv1_ref, next_ref, do_ref, lse_ref, kid_ref, qid_ref,
    dq_ref, dprev_ref, d0_ref, d1_ref, dnext_ref,
):
    kv = (prev_ref, kv0_ref, kv1_ref, next_ref)
    sums = [[None, None] for _ in range(4)]
    for tile in range(2):
        k = window(kv, tile, 0)
        v = window(kv, tile, 1)
        q2 = two_heads(q_ref[TOK * tile : TOK * tile + TOK, :] * jnp.asarray(0.125, BF))
        do2 = two_heads(do_ref[TOK * tile : TOK * tile + TOK, :])
        keep = masks(kid_ref[...], qid_ref[...], tile)
        scores = dot_nt(k, q2)
        dprobs = dot_nt(v, do2)
        probs, dscores, dqs = [], [], []
        for h in range(2):
            lanes = slice(TOK * h, TOK * h + TOK)
            lse = lse_ref[0, h : h + 1, TOK * tile : TOK * tile + TOK]
            p = jnp.exp(jnp.where(keep, scores[:, lanes], MASKED) - lse)
            dp = dprobs[:, lanes]
            delta = jnp.sum(p * dp, axis=0, keepdims=True)
            ds = (p * (dp - delta)).astype(BF)
            probs.append(p.astype(BF))
            dscores.append(ds)
            dqs.append(dot_tn(k, ds))
        dq_ref[TOK * tile : TOK * tile + TOK, :] = jnp.transpose(by_head(*dqs)) * 0.125
        dk = dot(jnp.concatenate(dscores, axis=1), q2)
        dv = dot(jnp.concatenate(probs, axis=1), do2)
        for which, full in enumerate((dk, dv)):
            for j in range(3):
                part = full[TOK * j : TOK * j + TOK, :]
                before = sums[tile + j][which]
                sums[tile + j][which] = part if before is None else before + part
    for which in range(2):
        dprev_ref[which] = sums[0][which].astype(BF)
        d0_ref[which] = sums[1][which]
        d1_ref[which] = sums[2][which]
        dnext_ref[which] = sums[3][which].astype(BF)


def attend_back(core, q, kv, grad, lse, key_ids, query_ids):
    pair = jax.ShapeDtypeStruct((2, TOK, HALF), F32)
    sent = jax.ShapeDtypeStruct((2, TOK, HALF), BF)
    return pl.pallas_call(
        attend_back_kernel,
        grid_spec=pltpu.PrefetchScalarGridSpec(
            num_scalar_prefetch=1,
            grid=(3,),
            in_specs=[pair_spec()]
            + [kv_spec()] * 4
            + [
                pair_spec(),
                pl.BlockSpec((1, 2, CHIP_TOK), lambda i, c: (i, 0, 0)),
                whole((4 * TOK, 1)),
                whole((1, CHIP_TOK)),
            ],
            out_specs=[pair_spec()] + [kv_spec()] * 4,
        ),
        out_shape=[jax.ShapeDtypeStruct((CHIP_TOK, HALF), F32), sent, pair, pair, sent],
        compiler_params=pltpu.CompilerParams(vmem_limit_bytes=48 * MIB),
        cost_estimate=pl.CostEstimate(
            flops=4 * 10**9, bytes_accessed=8 * MIB, transcendentals=2400000
        ),
        name="attend_back",
    )(core, q, *kv, grad, lse, key_ids, query_ids)


def centred(value):
    shifted = value - jnp.mean(value, axis=-1, keepdims=True)
    spread = jnp.mean(shifted * shifted, axis=-1, keepdims=True)
    scale = lax.rsqrt(spread + 1e-06)
    return shifted * scale, scale


def centred_back(unit, scale, grad):
    mean = jnp.mean(grad, axis=-1, keepdims=True)
    along = jnp.mean(grad * unit, axis=-1, keepdims=True)
    return scale * (grad - mean - unit * along)


def turn(block, cosine, sine):
    shape = block.shape
    parts = block.reshape(shape[0], LOCAL_HEADS, 2, 32)
    first, second = parts[:, :, 0], parts[:, :, 1]
    cosine = cosine.reshape(shape[0], LOCAL_HEADS, 32)
    sine = sine.reshape(shape[0], LOCAL_HEADS, 32)
    turned = jnp.stack([first * cosine - second * sine, first * sine + second * cosine], axis=2)
    return turned.reshape(shape)


def angle_grad(turned, grad):
    shape = turned.shape
    t = turned.reshape(shape[0], LOCAL_HEADS, 2, 32)
    g = grad.reshape(shape[0], LOCAL_HEADS, 2, 32)
    return (g[:, :, 1] * t[:, :, 0] - g[:, :, 0] * t[:, :, 1]).reshape(shape[0], LOCAL_HEADS * 32)


def by_core(value, core):
    split = [
        jnp.concatenate([value[:, 768 * i + HALF * c : 768 * i + HALF * c + HALF] for i in range(3)], axis=1)
        for c in range(2)
    ]
    return jnp.where(core == 0, split[0], split[1]), jnp.where(core == 0, split[1], split[0])


def per_device(
    tokens, image_ids, patch_row, patch_col, cotangent,
    norm1_gain, norm1_bias, qkv_weight, qkv_bias, frequencies, out_weight, out_bias,
    norm2_gain, norm2_bias, up_weight, up_bias, down_weight, down_bias,
):
    x, y, z, core = (lax.axis_index(a) for a in ("x", "y", "z", "c"))
    place = (x, y, z)
    chip = x * NZ + z
    core_arr = core.reshape(1).astype(jnp.int32)

    groups = [norm1_gain, norm1_bias, out_bias, norm2_gain, norm2_bias, down_bias, qkv_bias, up_bias]
    groups += [frequencies[0], frequencies[1]]
    first = jnp.concatenate([v for g in groups for v in (g, jnp.zeros_like(g))] + [jnp.zeros((48,), BF)])
    second = jnp.concatenate([v for g in groups for v in (jnp.zeros_like(g), g)] + [jnp.zeros((48,), BF)])
    small = jnp.pad(jnp.where(core == 0, first, second)[None], ((0, 3), (0, 0)))
    qkv_own, qkv_other = by_core(qkv_weight, core)
    out_own = jnp.where(core == 0, out_weight[:, :HALF], out_weight[:, HALF:])
    out_other = jnp.where(core == 0, out_weight[:, HALF:], out_weight[:, :HALF])
    own = jnp.concatenate([qkv_own, out_own], axis=1)
    other = jnp.concatenate([qkv_other, out_other], axis=1)
    got = swap(jnp.concatenate([other, jnp.pad(small, ((0, 0), (0, 1152)))], axis=0))
    attn_pack = in_core_order(core, own, got[:12])
    small = small[:1] + got[12:13, :HALF]
    up_split = up_weight.reshape(12, 32, 2, 2, 24)
    up_halves = [up_split[:, :, c].transpose(0, 2, 1, 3).reshape(12, FF_HALF) for c in range(2)]
    up_own = jnp.where(core == 0, up_halves[0], up_halves[1])
    up_other = jnp.where(core == 0, up_halves[1], up_halves[0])
    up_pack = in_core_order(core, up_own, swap(up_other))
    mlp_pack = jnp.concatenate([up_pack, down_weight[:24], down_weight[24:]], axis=1)

    inputs = in_core_order(core, tokens[0], swap(tokens[0])).astype(F32)
    dy = in_core_order(core, cotangent[0], swap(cotangent[0]))
    spots = jnp.concatenate([patch_row, patch_col], axis=0).astype(BF)
    spots = in_core_order(core, spots[None], swap(spots)[None]).astype(F32)
    rows = spots[:, 0].reshape(CHIP_TOK)
    cols = spots[:, 1].reshape(CHIP_TOK)
    near = lax.dynamic_slice_in_dim(jnp.pad(image_ids[0] + 1, (TOK, TOK)), chip * CHIP_TOK, 4 * TOK, 0)
    key_ids = near[:, None]
    query_ids = near[None, TOK : 3 * TOK]

    mlp = lax.all_gather(mlp_pack, ("x", "z"), axis=0, tiled=True)
    quarter = lax.dynamic_slice_in_dim(attn_pack, y * HALF, HALF, 1)
    block = jnp.concatenate([quarter, small, jnp.zeros((7, HALF), BF)], axis=0)
    block = spread(block, "z", NZ)
    block = jnp.concatenate([block[:, :24].reshape(192, HALF), block[:, 24]], axis=0)
    weights = spread(block, ("y", "x"), 16).reshape(4, 4, 200, HALF)
    rows_of = lambda i: weights[i, :, :192].reshape(WIDTH, HALF)
    qkv_w = jnp.concatenate([rows_of(0), rows_of(1), rows_of(2)], axis=1)
    out_w = rows_of(3)
    out_keep = lax.dynamic_slice_in_dim(out_w, core * HALF, HALF, 0)
    out_got = swap(lax.dynamic_slice_in_dim(out_w, (1 - core) * HALF, HALF, 0))
    out_rows = jnp.concatenate(
        [jnp.where(core == 0, out_keep, out_got), jnp.where(core == 0, out_got, out_keep)], axis=1
    )
    up_w, down_0, down_1 = mlp[:, :FF_HALF], mlp[:, FF_HALF : FF_HALF + WIDTH], mlp[:, FF_HALF + WIDTH :]
    lines = weights[0, :, 192:].reshape(32, HALF).astype(F32)
    gain_1, bias_1, bias_out, gain_2, bias_2, bias_down = (
        lines[:, 24 * i : 24 * i + 24].reshape(WIDTH) for i in range(6)
    )
    qkv_b = by_core(lines[:, 144:216].reshape(1, 3 * WIDTH), core)[0]
    up_b = lines[:, 216:312].reshape(32, 2, 2, 24)
    up_b = jnp.where(core == 0, up_b[:, 0], up_b[:, 1]).transpose(1, 0, 2).reshape(1, FF_HALF)
    freqs = lines[:, 312:336].reshape(32, 2, 12).transpose(1, 0, 2).reshape(2, HALF)
    freqs = lax.dynamic_slice_in_dim(freqs, core * 192, 192, 1)

    unit_1, scale_1 = centred(inputs)
    a1 = (unit_1 * gain_1 + bias_1).astype(BF)
    mixed = dot(a1, qkv_w) + qkv_b
    angle = rows[:, None] * freqs[0][None] + cols[:, None] * freqs[1][None]
    cosine, sine = jnp.cos(angle), jnp.sin(angle)
    q = turn(mixed[:, :HALF], cosine, sine).astype(BF)
    k = turn(mixed[:, HALF : 2 * HALF], cosine, sine).astype(BF)
    v = mixed[:, 2 * HALF :].astype(BF)
    kv0 = jnp.stack([k[:TOK], v[:TOK]])
    kv1 = jnp.stack([k[TOK:], v[TOK:]])
    up_list = [(i, i + 1) for i in range(NX * NZ - 1)]
    down_list = [(b, a) for a, b in up_list]
    before = lax.ppermute(kv1, ("x", "z"), up_list)
    after = lax.ppermute(kv0, ("x", "z"), down_list)
    kv = (before, kv0, kv1, after)
    o, lse, branch = attend(core_arr, q, kv, key_ids, query_ids, out_rows)
    middle = inputs + (branch.astype(F32) + swap(branch).astype(F32) + bias_out)

    unit_2, scale_2 = centred(middle)
    a2 = (unit_2 * gain_2 + bias_2).astype(BF)
    u = dot(a2, up_w) + up_b
    gate = 0.5 * (1.0 + lax.erf(u * 0.7071067811865476))
    act = (u * gate).astype(BF)
    slope = gate + u * jnp.exp(-0.5 * u * u) * 0.3989422804014327
    result = dot(act[:, :WIDTH], down_0) + dot(act[:, WIDTH:], down_1)
    dact = jnp.concatenate([dot_nt(dy, down_0), dot_nt(dy, down_1)], axis=1)
    du = (slope * dact).astype(BF)
    da2 = dot_nt(du, up_w).astype(BF)
    da2 = da2.astype(F32) + swap(da2).astype(F32)
    own = core * TOK
    rest = (1 - core) * TOK
    own_rows = lambda v: lax.dynamic_slice_in_dim(v, own, TOK, 0)
    rest_rows = lambda v: lax.dynamic_slice_in_dim(v, rest, TOK, 0)
    output = (
        own_rows(middle) + own_rows(result) + swap(rest_rows(result).astype(BF)).astype(F32) + bias_down
    ).astype(BF)[None]
    dy_own = own_rows(dy).astype(F32)
    early = jnp.stack(
        [
            jnp.sum(own_rows(da2) * own_rows(unit_2), axis=0),
            jnp.sum(own_rows(da2), axis=0),
            jnp.sum(dy_own, axis=0),
            jnp.sum(du[:, :WIDTH].astype(F32), axis=0),
            jnp.sum(du[:, WIDTH:].astype(F32), axis=0),
        ]
    ).astype(BF)
    early = jnp.pad(early, ((0, 3), (0, 0)))
    mlp_grad = jnp.concatenate(
        [
            dot_tn(a2, du[:, :WIDTH]).astype(BF), early,
            dot_tn(a2, du[:, WIDTH:]).astype(BF), early,
            dot_tn(act[:, :WIDTH], dy).astype(BF), early,
            dot_tn(act[:, WIDTH:], dy).astype(BF), early,
        ]
    )
    mlp_part = scatter_sum(mlp_grad.reshape(4, 776, WIDTH), "y")
    mlp_part = jnp.concatenate(
        [v for i in range(4) for v in (mlp_part[192 * i : 192 * i + 192], mlp_part[768:])]
    )
    mlp_part = scatter_sum(mlp_part.reshape(4, 200, WIDTH), "x")

    dy_wide = dy.astype(F32)
    dmid = centred_back(unit_2, scale_2, da2 * gain_2) + dy_wide
    dbranch = dmid.astype(BF)
    do = dot_nt(dbranch, out_rows).astype(BF)
    out_part = dot_tn(o, dbranch).astype(BF)
    out_own = lax.dynamic_slice_in_dim(out_part, core * HALF, HALF, 1)
    out_send = lax.dynamic_slice_in_dim(out_part, (1 - core) * HALF, HALF, 1)
    out_grad = in_core_order(core, out_own, swap(out_send))
    dq, dprev, d0, d1, dnext = attend_back(core_arr, q, kv, do, lse, key_ids, query_ids)
    from_next = lax.ppermute(dprev, ("x", "z"), down_list)
    from_prev = lax.ppermute(dnext, ("x", "z"), up_list)
    dkv = jnp.concatenate([d0 + from_prev.astype(F32), d1 + from_next.astype(F32)], axis=1)
    dk, dv = dkv[0], dkv[1]
    dmixed = jnp.concatenate([turn(dq, cosine, -sine), turn(dk, cosine, -sine), dv], axis=1).astype(BF)
    dangle = angle_grad(q.astype(F32), dq) + angle_grad(k.astype(F32), dk)
    dfreq_0 = jnp.sum(dangle * rows[:, None], axis=0)
    dfreq_1 = jnp.sum(dangle * cols[:, None], axis=0)
    da1 = dot_nt(dmixed, qkv_w)
    late = jnp.concatenate(
        [
            jnp.sum(dmixed.astype(F32), axis=0),
            jnp.sum(da1 * unit_1, axis=0),
            jnp.sum(da1, axis=0),
            dfreq_0, dfreq_1,
            jnp.sum(own_rows(dbranch).astype(F32), axis=0),
        ]
    ).reshape(10, HALF).astype(BF)
    late = jnp.broadcast_to(jnp.pad(late, ((0, 6), (0, 0)))[None], (4, 16, HALF))
    qkv_part = dot_tn(a1, dmixed).astype(BF)
    attn_blocks = jnp.concatenate(
        [
            jnp.concatenate([g.reshape(4, 192, HALF), late], axis=1)
            for g in (qkv_part[:, :HALF], qkv_part[:, HALF : 2 * HALF], qkv_part[:, 2 * HALF :], out_grad)
        ]
    )
    attn_part = deal(attn_blocks, ("y", "x")).astype(BF)
    vector = jnp.concatenate(
        [
            attn_part[192:208].reshape(16 * HALF)[: 10 * HALF],
            mlp_part[192:197].reshape(10 * HALF),
            jnp.zeros((4 * HALF,), BF),
        ]
    ).reshape(8, 3 * HALF)
    z_blocks = jnp.concatenate([mlp_part[:192], attn_part[:192]], axis=1).reshape(8, 24, 3 * HALF)
    z_blocks = jnp.concatenate([z_blocks, jnp.broadcast_to(vector[None], (8, 8, 3 * HALF))], axis=1)
    part = deal(z_blocks, "z").astype(BF)
    da1_own = own_rows(da1) + swap(rest_rows(da1).astype(BF)).astype(F32)
    input_grad = (
        centred_back(own_rows(unit_1), own_rows(scale_1), da1_own * gain_1) + own_rows(dmid)
    )[None]

    full = spread(part, ("y", "c"), 8).reshape(4, 2, 32, 3 * HALF).astype(F32)
    sums = full[0, :, 24:].reshape(2, 24 * HALF)
    both = sums[0] + sums[1]
    mine = jnp.where(core == 0, full[:, :, :12], full[:, :, 12:24])
    qkv_grad = mine[:3, :, :, WIDTH:].transpose(2, 0, 1, 3).reshape(12, 3 * WIDTH)
    out_weight_grad = mine[3, :, :, WIDTH:].transpose(1, 0, 2).reshape(12, WIDTH)
    up_grad = mine[:2, :, :, :WIDTH].reshape(2, 2, 12, 32, 24).transpose(2, 3, 1, 0, 4).reshape(12, 4 * WIDTH)
    down_grad = full[2:, :, :24, :WIDTH]
    down_grad = jnp.where(core == 0, down_grad[:, 0], down_grad[:, 1]).reshape(48, WIDTH)
    index = chip * 2 + core
    take = lambda v, size: lax.dynamic_slice_in_dim(v, index * size, size, 0)
    qkv_bias_grad = take(sums[:, : 3 * HALF].reshape(2, 3, HALF).transpose(1, 0, 2).reshape(-1), 36)
    g1, b1 = take(both[3 * HALF : 5 * HALF], 12), take(both[5 * HALF : 7 * HALF], 12)
    freq = sums[:, 7 * HALF : 8 * HALF].reshape(2, 2, 192).transpose(1, 0, 2).reshape(2, HALF)
    freq_grad = lax.dynamic_slice_in_dim(freq, index * 6, 6, 1)
    out_b = take(both[8 * HALF : 10 * HALF], 12)
    g2, b2, down_b = (take(both[(10 + 2 * i) * HALF : (12 + 2 * i) * HALF], 12) for i in range(3))
    up_bias_sum = sums[:, 16 * HALF : 20 * HALF].reshape(2, 2, 32, 24)
    up_bias_grad = take(up_bias_sum.transpose(2, 0, 1, 3).reshape(-1), 48)
    smalls = [g1, b1, out_b, g2, b2, down_b]
    return (
        output, input_grad,
        smalls[0], smalls[1], qkv_grad, qkv_bias_grad, freq_grad, out_weight_grad, smalls[2],
        smalls[3], smalls[4], up_grad, up_bias_grad, down_grad, smalls[5],
    )


def solution(mesh):
    fine = Mesh(mesh.devices.reshape(NY, NX, NZ, 2), ("y", "x", "z", "c"))
    f = ("x", "z", "c")
    return jax.shard_map(
        per_device,
        mesh=fine,
        in_specs=(
            P("y", f, None), P("y", None), P("y", f), P("y", f), P("y", f, None),
            P(f), P(f), P(f, None), P(f), P(None, f), P(f, None), P(f),
            P(f), P(f), P(f, None), P(f), P(f, None), P(f),
        ),
        out_specs=(
            P("y", f, None), P("y", f, None),
            P(f), P(f), P(f, None), P(f), P(None, f), P(f, None), P(f),
            P(f), P(f), P(f, None), P(f), P(f, None), P(f),
        ),
        check_vma=False,
    )
```

```python
import jax
import jax.numpy as jnp
from jax import lax
from jax.experimental import pallas as pl
from jax.experimental.pallas import tpu as pltpu
from jax.sharding import Mesh, PartitionSpec as P

NX, NY, NZ = 4, 4, 8
HEADS = 12
LOCAL_HEADS = 6
WIDTH = 768
HALF = 384
FF_HALF = 1536
TOK = 256
CHIP_TOK = 512
MASKED = -1e30
BF = jnp.bfloat16
F32 = jnp.float32
MIB = 1 << 20
OWN = slice(TOK, 3 * TOK)


def fetch(value, axis, size, step):
    if step == 0:
        return value
    return lax.ppermute(value, axis, [((i + step) % size, i) for i in range(size)])


def swap(value):
    return lax.ppermute(value, "c", [(0, 1), (1, 0)])


def in_core_order(core, own, other):
    first = jnp.where(core == 0, own, other)
    second = jnp.where(core == 0, other, own)
    return jnp.concatenate([first, second], axis=0)


def dot(a, b):
    return jnp.dot(a, b, preferred_element_type=F32)


def dot_nt(a, b):
    return lax.dot_general(a, b, (((1,), (1,)), ((), ())), preferred_element_type=F32)


def dot_tn(a, b):
    return lax.dot_general(a, b, (((0,), (0,)), ((), ())), preferred_element_type=F32)


def around_axis(block, axis, size):
    return [fetch(block, axis, size, k) for k in range(size)]


def scatter_sum(blocks, axis):
    count, rows, cols = blocks.shape
    return lax.psum_scatter(
        blocks.reshape(count * rows, cols), axis, scatter_dimension=0, tiled=True
    )


def whole_call(kernel, name, outs, scalars, arrays, scratch=(), flops=0, vmem=10, far=(), away=()):
    size = sum(v.size * v.dtype.itemsize for v in arrays)
    spec = lambda remote: pl.BlockSpec(memory_space=pl.ANY if remote else pltpu.VMEM)
    shapes = [(pltpu.HBM if i in far else jax.ShapeDtypeStruct)(*o) for i, o in enumerate(outs)]
    return pl.pallas_call(
        kernel,
        out_shape=shapes,
        in_specs=[pl.BlockSpec(memory_space=pltpu.SMEM)]
        + [spec(i in away) for i in range(len(arrays))],
        out_specs=[spec(i in far) for i in range(len(outs))],
        scratch_shapes=list(scratch),
        compiler_params=pltpu.CompilerParams(vmem_limit_bytes=vmem * MIB),
        cost_estimate=pl.CostEstimate(flops=flops, bytes_accessed=size, transcendentals=0),
        name=name,
    )(
        scalars,
        *[
            pltpu.with_memory_space_constraint(v, pltpu.HBM) if i in away else v
            for i, v in enumerate(arrays)
        ],
    )


class Mover:
    def __init__(self, sems):
        self.sems, self.count, self.open = sems, 0, []

    def start(self, source, target):
        copy = pltpu.make_async_copy(source, target, self.sems.at[self.count])
        self.count += 1
        copy.start()
        return copy

    def load(self, pairs):
        return [self.start(source, target) for source, target in pairs]

    def put(self, source, target):
        self.open.append(self.start(source, target))

    def finish(self):
        for copy in self.open:
            copy.wait()


def wait_all(copies):
    for copy in copies:
        copy.wait()


def id_columns(row_ref):
    return jnp.transpose(jnp.broadcast_to(row_ref[...], (8, 4 * TOK)))[:, :1]


def two_heads(block):
    lane = lax.broadcasted_iota(jnp.int32, block.shape, 1)
    zero = jnp.zeros_like(block)
    return jnp.concatenate(
        [jnp.where(lane < 64, block, zero), jnp.where(lane < 64, zero, block)], axis=0
    )


def by_head(first, second):
    row = lax.broadcasted_iota(jnp.int32, first.shape, 0)
    return jnp.where(row < 64, first, second)


def scaled(block):
    return block * jnp.asarray(0.125, BF)


def pair_of(i):
    return pl.ds(pl.multiple_of(128 * i, 128), 128)


def attend_kernel(
    core_ref, q_ref, k_ref, v_ref, keep_ref, got_ref, id_hbm,
    part_ref, o_hbm, lse_hbm, w_hbm, o_ref, lse_ref, w_ref, id_ref, kid_ref, sems,
):
    mover = Mover(sems)
    mover.start(id_hbm, id_ref).wait()
    w_ref[:, :HALF] = pick(core_ref[0], keep_ref[...], got_ref[...])
    w_ref[:, HALF:] = pick(core_ref[0], got_ref[...], keep_ref[...])
    mover.put(w_ref, w_hbm)
    kid_ref[...] = id_columns(id_ref)

    def body(i, carry):
        pair = pair_of(i)
        for tile in range(2):
            near = slice(TOK * tile, TOK * tile + 3 * TOK)
            mine = slice(TOK * tile + TOK, TOK * tile + 2 * TOK)
            here = slice(TOK * tile, TOK * tile + TOK)
            v = v_ref[near, pair]
            keep = kid_ref[near, :] == id_ref[0:1, mine]
            scores = dot_nt(k_ref[near, pair], two_heads(scaled(q_ref[mine, pair])))
            halves = []
            for h in range(2):
                s = jnp.where(keep, scores[:, TOK * h : TOK * h + TOK], MASKED)
                top = jnp.max(s, axis=0, keepdims=True)
                expo = jnp.exp(s - top)
                total = jnp.sum(expo, axis=0, keepdims=True)
                lse_ref[i, h : h + 1, here] = top + jnp.log(total)
                p = (expo * (1.0 / total)).astype(BF)
                halves.append(dot_tn(v, p))
            o_ref[here, pair] = jnp.transpose(by_head(*halves)).astype(BF)
        return carry

    lax.fori_loop(0, 3, body, 0)
    mover.put(o_ref, o_hbm)
    mover.put(lse_ref, lse_hbm)
    part_ref[...] = dot(o_ref[...], w_ref[...]).astype(BF)
    mover.finish()


def attend(core, q, k, v, ids, keep, got):
    o, lse, weights = ((CHIP_TOK, HALF), BF), ((3, 2, CHIP_TOK), F32), ((HALF, WIDTH), BF)
    return whole_call(
        attend_kernel, "attend", [((CHIP_TOK, WIDTH), BF), o, lse, weights],
        core, [q, k, v, keep, got, ids],
        scratch=[
            pltpu.VMEM(*o), pltpu.VMEM(*lse), pltpu.VMEM(*weights),
            pltpu.VMEM((1, 4 * TOK), F32), pltpu.VMEM((4 * TOK, 1), F32), pltpu.SemaphoreType.DMA((8,)),
        ],
        flops=3 * 10**9, vmem=12, far=(1, 2, 3), away=(5,),
    )


def pair_grads(k, v, q2, do2, keep, lses, deltas):
    scores = dot_nt(k, q2)
    dprobs = dot_nt(v, do2)
    probs, dscores = [], []
    for h in range(2):
        lanes = slice(TOK * h, TOK * h + TOK)
        p = jnp.exp(jnp.where(keep, scores[:, lanes], MASKED) - lses[h])
        dscores.append((p * (dprobs[:, lanes] - deltas[h])).astype(BF))
        probs.append(p.astype(BF))
    return probs, dscores


def near_back_kernel(
    core_ref, q_hbm, k_hbm, v_hbm, lse_hbm, id_hbm, do_ref, delta_ref, dq_ref, dkv_ref,
    q_ref, k_ref, v_ref, lse_ref, id_ref, kid_ref, sems, more_sems,
):
    first_loads = Mover(more_sems).load(((id_hbm, id_ref), (lse_hbm, lse_ref)))
    sources = ((q_hbm, q_ref), (k_hbm, k_ref), (v_hbm, v_ref))

    def load(i):
        return [
            pltpu.make_async_copy(source.at[:, pair_of(i)], target.at[:, pair_of(i)], sems.at[i, j])
            for j, (source, target) in enumerate(sources)
        ]

    for i in range(3):
        for copy in load(i):
            copy.start()
    wait_all(first_loads)
    kid_ref[...] = id_columns(id_ref)

    def body(i, carry):
        pair = pair_of(i)
        wait_all(load(i))
        for tile in range(2):
            near = slice(TOK * tile, TOK * tile + 3 * TOK)
            mine = slice(TOK * tile + TOK, TOK * tile + 2 * TOK)
            here = slice(TOK * tile, TOK * tile + TOK)
            k = k_ref[near, pair]
            q2 = two_heads(scaled(q_ref[mine, pair]))
            do2 = two_heads(do_ref[here, pair])
            keep = kid_ref[near, :] == id_ref[0:1, mine]
            probs, dscores = pair_grads(
                k, v_ref[near, pair], q2, do2, keep,
                [lse_ref[i, h : h + 1, here] for h in range(2)],
                [delta_ref[i, h : h + 1, here] for h in range(2)],
            )
            dq = by_head(*[dot_tn(k, ds) for ds in dscores])
            dq_ref[here, pair] = jnp.transpose(dq) * 0.125
            first = TOK * (1 - tile)
            own = slice(first, first + 2 * TOK)
            dk = dot(jnp.concatenate([d[own] for d in dscores], axis=1), q2)
            dv = dot(jnp.concatenate([p[own] for p in probs], axis=1), do2)
            for which, full in enumerate((dk, dv)):
                if tile == 0:
                    dkv_ref[which, :, pair] = full
                else:
                    dkv_ref[which, :, pair] += full
        return carry

    lax.fori_loop(0, 3, body, 0)


def near_back(core, q, k, v, grad, lse, delta, ids):
    around = pltpu.VMEM((4 * TOK, HALF), BF)
    return whole_call(
        near_back_kernel, "near_back",
        [((CHIP_TOK, HALF), F32), ((2, CHIP_TOK, HALF), F32)],
        core, [q, k, v, lse, ids, grad, delta], away=(0, 1, 2, 3, 4),
        scratch=[
            around, around, around, pltpu.VMEM((3, 2, CHIP_TOK), F32), pltpu.VMEM((1, 4 * TOK), F32),
            pltpu.VMEM((4 * TOK, 1), F32), pltpu.SemaphoreType.DMA((3, 3)), pltpu.SemaphoreType.DMA((2,)),
        ],
        flops=4 * 10**9, vmem=14,
    )


def far_back(q_ref, k_ref, v_ref, before_ref, after_ref, id_ref, kid_ref, dkv_ref, sum_ref):
    row = lax.broadcasted_iota(jnp.int32, (8, TOK), 0)

    def body(i, carry):
        pair = pair_of(i)
        for side, ref in enumerate((before_ref, after_ref)):
            keys = slice(TOK * (side + 1), TOK * (side + 2))
            queries = slice(3 * TOK * side, 3 * TOK * side + TOK)
            tail = ref[TOK:, :TOK].astype(F32)
            deltas = tail[0:8] + tail[8:16]
            lses = tail[16:24] + tail[24:32]
            choose = lambda v, h: jnp.sum(
                jnp.where(row == 2 * i + h, v, 0.0), axis=0, keepdims=True
            )
            q2 = two_heads(scaled(q_ref[queries, pair]))
            do2 = two_heads(ref[:TOK, pair])
            keep = kid_ref[keys, :] == id_ref[0:1, queries]
            probs, dscores = pair_grads(
                k_ref[keys, pair], v_ref[keys, pair], q2, do2, keep,
                [choose(lses, h) for h in range(2)], [choose(deltas, h) for h in range(2)],
            )
            rows = slice(TOK * side, TOK * side + TOK)
            dk = dot(jnp.concatenate(dscores, axis=1), q2)
            dv = dot(jnp.concatenate(probs, axis=1), do2)
            sum_ref[0, rows, pair] = dkv_ref[0, rows, pair] + dk
            sum_ref[1, rows, pair] = dkv_ref[1, rows, pair] + dv
        return carry

    lax.fori_loop(0, 3, body, 0)


def centred(value):
    shifted = value - jnp.mean(value, axis=-1, keepdims=True)
    spread = jnp.mean(shifted * shifted, axis=-1, keepdims=True)
    scale = lax.rsqrt(spread + 1e-06)
    return shifted * scale, scale


def centred_back(unit, scale, grad):
    mean = jnp.mean(grad, axis=-1, keepdims=True)
    along = jnp.mean(grad * unit, axis=-1, keepdims=True)
    return scale * (grad - mean - unit * along)


def lanes_of(width):
    return lax.broadcasted_iota(jnp.int32, (1, width), 1).astype(F32)


def pick(core, first, second):
    return jnp.where(core == 0, first, second)


def expand(lines, shift, lane_in, owner):
    width = lane_in.shape[1]
    moved = pltpu.roll(lines, (HALF - shift) % HALF, 1)[:, :128].astype(BF)
    sub = lax.broadcasted_iota(jnp.int32, (128, width), 0).astype(F32)
    table = dot(moved, jnp.where(sub == lane_in, 1.0, 0.0).astype(BF))
    sub = lax.broadcasted_iota(jnp.int32, (64, width), 0).astype(F32)
    return jnp.sum(jnp.where(sub == owner, table, 0.0), axis=0, keepdims=True)


def split_index(index, size):
    group = jnp.floor((index + 0.5) * (1.0 / size))
    return group, index - group * size


def low_half(shape):
    return lax.bitwise_and(lax.broadcasted_iota(jnp.int32, shape, 1), 63) < 32


def swap_halves(value):
    ahead = pltpu.roll(value, HALF - 32, 1)
    behind = pltpu.roll(value, 32, 1)
    return jnp.where(low_half(value.shape), ahead, behind)


def three_parts(value):
    parts = []
    for _ in range(3):
        part = value.astype(BF)
        parts.append(part)
        value = value - part.astype(F32)
    return jnp.concatenate(parts, axis=0)


def qkv_kernel(place_ref, *refs):
    by_y, by_x, sources, refs = refs[:4], refs[4:8], refs[8:12], refs[12:]
    q_ref, k_ref, v_ref, keep_ref, send_ref = refs[:5]
    q_hbm, k_hbm, v_hbm, vec_hbm, a1_hbm, turn_hbm, w_hbm, x_hbm = refs[5:13]
    table_ref, bias_ref, line_ref, x_ref, a1_ref, turn_ref, w_ref, vec_ref, sems, x_sems = refs[13:]
    core, x, y = place_ref[0], place_ref[4], place_ref[1]
    mover = Mover(sems)

    def x_load(step, source):
        return pltpu.make_async_copy(source, x_ref.at[pl.ds(TOK * step, TOK), :], x_sems.at[step])

    own, lower, upper, far = sources

    @pl.when(core == 0)
    def _():
        for step, source in enumerate((lower, own, upper, far)):
            x_load(step, source).start()

    @pl.when(core == 1)
    def _():
        for step, source in enumerate((far, lower, own, upper)):
            x_load(step, source).start()

    core_f = core.astype(F32)
    for ky in range(4):
        for kx in range(4):
            q = lax.bitwise_and(y + ky, 3)
            chip = lax.bitwise_and(x + kx, 3)
            low = pl.ds(pl.multiple_of(192 * chip, 96), 96)
            high = pl.ds(pl.multiple_of(192 * chip + 96, 96), 96)
            w_ref[q, low, :] = by_y[ky][kx, :96, :]
            w_ref[q, high, :] = by_x[kx][ky, :96, :]
    for kx in range(4):
        chip = lax.bitwise_and(x + kx, 3)
        low = pl.ds(pl.multiple_of(16 * chip, 8), 8)
        high = pl.ds(pl.multiple_of(16 * chip + 8, 8), 8)
        line_ref[low, :] = by_y[0][kx, 96:, :].astype(F32)
        line_ref[high, :] = by_x[kx][0, 96:, :].astype(F32)
    lines = line_ref[...]
    group, inner = split_index(lanes_of(WIDTH), 12)
    rows = [expand(lines, 12 * i, inner, group) for i in range(6)]
    group, inner = split_index(lanes_of(WIDTH), 24)
    rows += [expand(lines, 108 + 24 * h, inner, 2.0 * group + core_f) for h in range(2)]
    vec_ref[...] = jnp.concatenate(rows, axis=0)
    group, inner = split_index(lanes_of(3 * WIDTH), 36)
    bias = expand(lines, 72, inner, group)
    for i in range(3):
        bias_ref[i : i + 1, :] = pick(
            core,
            bias[:, WIDTH * i : WIDTH * i + HALF],
            bias[:, WIDTH * i + HALF : WIDTH * i + WIDTH],
        )
    lane = lanes_of(HALF)
    head, _ = split_index(lane, 64)
    _, inner = split_index(lane, 32)
    group, inner = split_index(192.0 * core_f + 32.0 * head + inner, 6)
    count = lax.broadcasted_iota(jnp.int32, (32, HALF), 0).astype(F32)
    for f in range(2):
        angle = count * expand(lines, 156 + 6 * f, inner, group)
        table_ref[f] = three_parts(jnp.concatenate([jnp.cos(angle), jnp.sin(angle)], axis=1))
    keep_ref[...] = w_ref[3, pl.ds(pl.multiple_of(HALF * core, HALF), HALF), :]
    send_ref[...] = w_ref[3, pl.ds(pl.multiple_of(HALF * (1 - core), HALF), HALF), :]
    mover.put(w_ref, w_hbm)
    mover.put(vec_ref, vec_hbm)
    for step in range(4):
        rows = slice(TOK * step, TOK * step + TOK)
        x_load(step, own).wait()
        spots = x_ref[rows, WIDTH:].astype(F32)
        spot = lax.bitwise_and(lax.broadcasted_iota(jnp.int32, (TOK, 96), 1), 31).astype(F32)
        tables = [
            dot(jnp.where(spots[:, f : f + 1] == spot, 1.0, 0.0).astype(BF), table_ref[f])
            for f in range(2)
        ]
        cos_r, sin_r = tables[0][:, :HALF], tables[0][:, HALF:]
        cos_c, sin_c = tables[1][:, :HALF], tables[1][:, HALF:]
        cosine = cos_r * cos_c - sin_r * sin_c
        sine = sin_r * cos_c + cos_r * sin_c
        sine = jnp.where(low_half(sine.shape), -sine, sine)
        unit, _ = centred(x_ref[rows, :WIDTH].astype(F32))
        a1 = (unit * vec_ref[0:1, :] + vec_ref[1:2, :]).astype(BF)
        if step in (1, 2):
            here = slice(TOK * (step - 1), TOK * step)
            turn_ref[0, here, :] = cosine
            turn_ref[1, here, :] = sine
            a1_ref[here, :] = a1
            if step == 2:
                mover.put(x_ref.at[pl.ds(TOK, CHIP_TOK), :], x_hbm)
                mover.put(turn_ref, turn_hbm)
                mover.put(a1_ref, a1_hbm)
        for i, ref in enumerate((q_ref, k_ref, v_ref)):
            part = dot(a1, w_ref[i]) + bias_ref[i : i + 1, :]
            if i < 2:
                part = part * cosine + swap_halves(part) * sine
            ref[rows, :] = part.astype(BF)
            mover.put(ref.at[pl.ds(TOK * step, TOK), :], (q_hbm, k_hbm, v_hbm)[i].at[pl.ds(TOK * step, TOK), :])
    mover.finish()


def qkv_call(place, sources, by_y, by_x):
    around, square = ((4 * TOK, HALF), BF), ((HALF, HALF), BF)
    wide, turn = ((CHIP_TOK, WIDTH), BF), ((2, CHIP_TOK, HALF), F32)
    vec, full = ((8, WIDTH), F32), ((4, WIDTH, HALF), BF)
    return whole_call(
        qkv_kernel, "qkv",
        [around, around, around, square, square, around, around, around, vec, wide, turn, full]
        + [((CHIP_TOK, WIDTH + 128), BF)],
        place, [*by_y, *by_x, *sources],
        scratch=[
            pltpu.VMEM((2, 96, WIDTH), BF), pltpu.VMEM((8, HALF), F32), pltpu.VMEM((64, HALF), F32),
            pltpu.VMEM((4 * TOK, WIDTH + 128), BF), pltpu.VMEM(*wide), pltpu.VMEM(*turn),
            pltpu.VMEM(*full), pltpu.VMEM(*vec), pltpu.SemaphoreType.DMA((24,)),
            pltpu.SemaphoreType.DMA((4,)),
        ],
        flops=2 * 10**9, vmem=18, far=tuple(range(5, 13)), away=tuple(range(8, 12)),
    )


def mlp_kernel(
    place_ref, part_ref, got_ref, x_hbm, vec_hbm, w_hbm, dya_hbm, dyb_hbm,
    da2_ref, high_hbm, mid_hbm, own_hbm, send_hbm, sums_hbm, *refs,
):
    low_hbms = refs[:4]
    acc_ref, grads_ref, x_ref, w_ref, dy_ref, mid_ref, own_ref, send_ref, vec_ref, sums_ref, sems = refs[4:]
    core, x = place_ref[0], place_ref[4]
    own = pl.ds(pl.multiple_of(core * TOK, TOK), TOK)
    rest = pl.ds(pl.multiple_of((1 - core) * TOK, TOK), TOK)
    mover = Mover(sems)
    load_x = mover.load(((x_hbm.at[:, pl.ds(0, WIDTH)], x_ref), (vec_hbm, vec_ref)))
    loads = []
    for i in (0, 2, 1, 3):
        cols = pl.ds(WIDTH * i, WIDTH)
        loads.append(mover.start(w_hbm.at[:, cols], w_ref.at[:, cols]))
        if i == 0:
            load_dy = mover.load(((dya_hbm, dy_ref.at[own, :]), (dyb_hbm, dy_ref.at[rest, :])))

    def put(index, value):
        grads_ref[index] = value.astype(BF)
        for k, ref in enumerate(low_hbms):
            row = pl.multiple_of(192 * lax.bitwise_and(x + 4 - k, 3), 96)
            mover.put(grads_ref.at[index, pl.ds(row, 96), :], ref.at[index])
        for j in range(4):
            rows = pl.ds(192 * j + 96, 96)
            mover.put(grads_ref.at[index, rows, :], high_hbm.at[index, pl.ds(96 * j, 96), :])

    wait_all(load_x)
    middle = x_ref[...].astype(F32) + (
        part_ref[...].astype(F32) + got_ref[...].astype(F32) + vec_ref[2:3, :]
    )
    mid_ref[...] = middle
    mover.put(mid_ref, mid_hbm)
    unit, _ = centred(middle)
    a2 = (unit * vec_ref[3:4, :] + vec_ref[4:5, :]).astype(BF)
    da2 = None
    for h in range(2):
        lanes = slice(WIDTH * h, WIDTH * h + WIDTH)
        loads[2 * h].wait()
        loads[2 * h + 1].wait()
        if h == 0:
            wait_all(load_dy)
        dy = dy_ref[...]
        up = w_ref[:, lanes]
        down = w_ref[:, FF_HALF + WIDTH * h : FF_HALF + WIDTH * h + WIDTH]
        u = dot(a2, up) + vec_ref[6 + h : 7 + h, :]
        gate = 0.5 * (1.0 + lax.erf(u * 0.7071067811865476))
        act = (u * gate).astype(BF)
        put(2 + h, dot_tn(act, dy))
        slope = gate + u * jnp.exp(-0.5 * u * u) * 0.3989422804014327
        du = (slope * dot_nt(dy, down)).astype(BF)
        put(h, dot_tn(a2, du))
        sums_ref[h : h + 1, :] = jnp.sum(du.astype(F32), axis=0, keepdims=True)
        term = dot(act, down)
        if h == 0:
            acc_ref[...] = term
        else:
            acc_ref[...] += term
        term = dot_nt(du, up)
        da2 = term if da2 is None else da2 + term
    da2_ref[...] = da2.astype(BF)
    mover.put(sums_ref, sums_hbm)
    own_ref[...] = acc_ref[own, :] + mid_ref[own, :] + vec_ref[5:6, :]
    send_ref[...] = acc_ref[rest, :].astype(BF)
    mover.put(own_ref, own_hbm)
    mover.put(send_ref, send_hbm)
    mover.finish()


def mlp_call(place, branch, got, inputs, vec, weights, dy_own, dy_other):
    full, half = (CHIP_TOK, WIDTH), (TOK, WIDTH)
    return whole_call(
        mlp_kernel, "mlp",
        [(full, BF), ((4, HALF, WIDTH), BF), (full, F32), (half, F32), (half, BF), ((2, WIDTH), F32)]
        + [((4, 96, WIDTH), BF)] * 4,
        place, [branch, got, inputs, vec, weights, dy_own, dy_other],
        scratch=[
            pltpu.VMEM(full, F32), pltpu.VMEM((4, WIDTH, WIDTH), BF), pltpu.VMEM(full, BF),
            pltpu.VMEM((WIDTH, 4 * WIDTH), BF), pltpu.VMEM(full, BF), pltpu.VMEM(full, F32),
            pltpu.VMEM(half, F32), pltpu.VMEM(half, BF), pltpu.VMEM((8, WIDTH), F32),
            pltpu.VMEM((2, WIDTH), F32), pltpu.SemaphoreType.DMA((48,)),
        ],
        flops=8 * 10**9, vmem=34, far=tuple(range(1, 10)), away=tuple(range(2, 7)),
    )


def branch_kernel(
    core_ref, da2_ref, got_ref, mid_hbm, dya_hbm, dyb_hbm, vec_hbm, o_hbm, w_hbm, lse_hbm,
    do_ref, delta_ref, back_ref, on_ref, own_ref, send_ref, sums_ref, dmid_hbm,
    scr_ref, mid_ref, dy_ref, vec_ref, o_ref, w_ref, lse_ref, sems,
):
    core = core_ref[0]
    mover = Mover(sems)
    mine = pl.ds(pl.multiple_of(core * TOK, TOK), TOK)
    rest = pl.ds(pl.multiple_of((1 - core) * TOK, TOK), TOK)
    loads = mover.load(
        (
            (mid_hbm, mid_ref), (vec_hbm, vec_ref), (dya_hbm, dy_ref.at[mine, :]),
            (dyb_hbm, dy_ref.at[rest, :]), (w_hbm, w_ref), (o_hbm, o_ref), (lse_hbm, lse_ref),
        )
    )
    wait_all(loads)
    unit, scale = centred(mid_ref[...])
    da2 = da2_ref[...].astype(F32) + got_ref[...].astype(F32)
    dy = dy_ref[...].astype(F32)
    dmid = centred_back(unit, scale, da2 * vec_ref[3:4, :]) + dy
    low = dmid.astype(BF)
    scr_ref[...] = dmid
    mover.put(scr_ref.at[mine, :], dmid_hbm)
    do = dot_nt(low, w_ref[...]).astype(BF)
    do_ref[...] = do
    heads = lax.broadcasted_iota(jnp.int32, (8, HALF), 0)
    lane = lax.broadcasted_iota(jnp.int32, (8, HALF), 1)
    hot = jnp.where(jnp.logical_and(lane >= 64 * heads, lane < 64 * heads + 64), 1.0, 0.0)
    delta = lax.dot_general(
        hot, do.astype(F32) * o_ref[...].astype(F32), (((1,), (1,)), ((), ())),
        precision=lax.Precision.HIGHEST, preferred_element_type=F32,
    )
    for i in range(3):
        delta_ref[i] = delta[2 * i : 2 * i + 2]
    lse = jnp.concatenate([lse_ref[i] for i in range(3)] + [jnp.zeros((2, CHIP_TOK), F32)], axis=0)
    tail = []
    for value in (delta, lse):
        high = value.astype(BF)
        tail += [high, (value - high.astype(F32)).astype(BF)]
    tail = jnp.concatenate(tail, axis=0)
    for ref, rows in ((back_ref, slice(0, TOK)), (on_ref, slice(TOK, CHIP_TOK))):
        ref[:TOK, :] = do[rows]
        ref[TOK:, :] = jnp.concatenate([tail[:, rows], jnp.zeros((32, 128), BF)], axis=1)
    grad = dot_tn(o_ref[...], low).astype(BF)
    own_ref[...] = pick(core, grad[:, :HALF], grad[:, HALF:])
    send_ref[...] = pick(core, grad[:, HALF:], grad[:, :HALF])
    row = lax.broadcasted_iota(jnp.int32, (CHIP_TOK, 1), 0)
    here = jnp.logical_and(row >= core * TOK, row < core * TOK + TOK)
    total = lambda v: jnp.sum(jnp.where(here, v, 0.0), axis=0, keepdims=True)
    sums_ref[0:1, :] = total(low.astype(F32))
    sums_ref[1:2, :] = total(da2 * unit)
    sums_ref[2:3, :] = total(da2)
    sums_ref[3:4, :] = total(dy)
    mover.finish()


def qkv_grad_kernel(
    place_ref, dq_ref, near_ref, before_ref, after_ref, own_ref, got_ref, sums_ref,
    q_hbm, k_hbm, v_hbm, turn_hbm, a1_hbm, x_hbm, w_hbm, id_hbm, more_hbm, *refs,
):
    low_hbms, high_hbms, da1_own_hbm, da1_send_hbm = refs[:4], refs[4:8], refs[8], refs[9]
    da1_ref, da1_send_ref, full_ref, dkv_ref, kid_ref, id_ref, more_ref = refs[10:17]
    q_ref, k_ref, v_ref, turn_ref, a1_ref, x_ref, w_ref, sems = refs[17:25]
    low_refs, high_refs = refs[25:29], refs[29:33]
    core, x, y = place_ref[0], place_ref[4], place_ref[1]
    mover = Mover(sems)
    loads = mover.load(
        (
            (id_hbm, id_ref), (q_hbm, q_ref), (k_hbm, k_ref), (v_hbm, v_ref), (turn_hbm, turn_ref),
            (a1_hbm, a1_ref), (w_hbm.at[pl.ds(0, 3)], w_ref), (x_hbm, x_ref), (more_hbm, more_ref),
        )
    )
    wait_all(loads[:4])
    kid_ref[...] = id_columns(id_ref)
    far_back(q_ref, k_ref, v_ref, before_ref, after_ref, id_ref, kid_ref, near_ref, dkv_ref)
    wait_all(loads[4:])

    def hand_out(step, full):
        full_ref[...] = full
        for k, ref in enumerate(low_refs):
            row = pl.multiple_of(192 * lax.bitwise_and(x + 4 - k, 3), 96)
            ref[step, :96, :] = full_ref[pl.ds(row, 96), :]
        for k, ref in enumerate(high_refs):

            @pl.when(lax.bitwise_and(y + 4 - k, 3) == step)
            def _():
                for j in range(4):
                    ref[j] = full_ref[192 * j + 96 : 192 * j + 192, :]

    tail = []
    angle = 0.0
    a1 = a1_ref[...]
    for step, grad in enumerate((dq_ref[...], dkv_ref[0], dkv_ref[1])):
        if step < 2:
            other = swap_halves(grad)
            turned = (q_ref, k_ref)[step][OWN, :].astype(F32)
            angle = angle + other * turned - grad * swap_halves(turned)
            grad = grad * turn_ref[0] - other * turn_ref[1]
        low = grad.astype(BF)
        tail.append(jnp.sum(low.astype(F32), axis=0, keepdims=True))
        hand_out(step, dot_tn(a1, low).astype(BF))
        term = dot_nt(low, w_ref[step])
        if step == 0:
            da1_ref[...] = term
        else:
            da1_ref[...] += term
    first = pick(core, own_ref[...], got_ref[...])
    second = pick(core, got_ref[...], own_ref[...])
    hand_out(3, jnp.concatenate([first, second], axis=0))
    da1 = da1_ref[...]
    for source, target in zip(high_refs, high_hbms):
        mover.put(source, target)
    mover.put(da1_ref.at[pl.ds(pl.multiple_of(core * TOK, TOK), TOK), :], da1_own_hbm)
    da1_send_ref[...] = da1_ref[pl.ds(pl.multiple_of((1 - core) * TOK, TOK), TOK), :].astype(BF)
    mover.put(da1_send_ref, da1_send_hbm)
    unit, _ = centred(x_ref[:, :WIDTH].astype(F32))
    spots = x_ref[:, WIDTH:].astype(F32)
    halves = lambda v: [v[:, :HALF], v[:, HALF:]]
    tail += halves(jnp.sum(da1 * unit, axis=0, keepdims=True))
    tail += halves(jnp.sum(da1, axis=0, keepdims=True))
    tail += [jnp.sum(angle * spots[:, f : f + 1], axis=0, keepdims=True) for f in range(2)]
    for i in range(4):
        tail += halves(sums_ref[i : i + 1, :])
    for h in range(2):
        tail += halves(more_ref[h : h + 1, :])
    tail += [jnp.zeros((11, HALF), F32)]
    tail = jnp.concatenate(tail, axis=0).astype(BF)
    for ref in low_refs:
        for i in range(4):
            ref[i, 96:, :] = tail[8 * i : 8 * i + 8]
    for source, target in zip(low_refs, low_hbms):
        mover.put(source, target)
    mover.finish()


def qkv_grad_call(place, near, q, k, v, turn, a1, inputs, weights, ids, more):
    around = pltpu.VMEM((4 * TOK, HALF), BF)
    parts = [((4, 104, HALF), BF)] * 4 + [((4, 96, HALF), BF)] * 4
    return whole_call(
        qkv_grad_kernel, "qkv_grad",
        parts + [((TOK, WIDTH), F32), ((TOK, WIDTH), BF)],
        place, [*near, q, k, v, turn, a1, inputs, weights, ids, more],
        scratch=[
            pltpu.VMEM((CHIP_TOK, WIDTH), F32), pltpu.VMEM((TOK, WIDTH), BF), pltpu.VMEM((WIDTH, HALF), BF),
            pltpu.VMEM((2, CHIP_TOK, HALF), F32), pltpu.VMEM((4 * TOK, 1), F32),
            pltpu.VMEM((1, 4 * TOK), F32), pltpu.VMEM((2, WIDTH), F32),
            around, around, around, pltpu.VMEM((2, CHIP_TOK, HALF), F32),
            pltpu.VMEM((CHIP_TOK, WIDTH), BF), pltpu.VMEM((CHIP_TOK, WIDTH + 128), BF),
            pltpu.VMEM((3, WIDTH, HALF), BF), pltpu.SemaphoreType.DMA((24,)),
        ]
        + [pltpu.VMEM(*part) for part in parts],
        flops=3 * 10**9, vmem=28, far=tuple(range(10)), away=tuple(range(7, 16)),
    )


def total_of(refs):
    total = refs[0][...].astype(F32)
    for ref in refs[1:]:
        total = total + ref[...].astype(F32)
    return total.astype(BF)


def mid_kernel(place_ref, *refs):
    lows, highs, mlps, rest_ref = refs[:4], refs[4:8], refs[8:12], refs[12]
    out_low, out_high, low_ref, high_ref, mlp_ref = refs[13:17], refs[17:21], *refs[21:]
    low_ref[...] = total_of(lows)
    high_ref[...] = total_of(highs)
    mlp_ref[...] = total_of(mlps)
    x, y = place_ref[4], place_ref[1]
    for k in range(4):
        to_y, to_x = lax.bitwise_and(y + 4 - k, 3), lax.bitwise_and(x + 4 - k, 3)
        out_low[k][:96, :WIDTH] = mlp_ref[to_y]
        out_low[k][96:, :WIDTH] = jnp.zeros((24, WIDTH), BF)
        out_low[k][:96, WIDTH:] = low_ref[to_y, :96, :]
        for i in range(3):
            out_low[k][96 + 8 * i : 104 + 8 * i, WIDTH:] = low_ref[i, 96:, :]
        out_high[k][:, :WIDTH] = rest_ref[to_x]
        out_high[k][:, WIDTH:] = high_ref[to_x]


def join_kernel(core_ref, *refs):
    low, high, out_ref = total_of(refs[:4]), total_of(refs[4:8]), refs[8]
    tail = jnp.concatenate([low[96 + 8 * i : 104 + 8 * i, WIDTH:] for i in range(3)], axis=1)
    for i in range(8):
        part = (low, high)[i // 4]
        out_ref[i, :24, :] = part[24 * (i % 4) : 24 * (i % 4) + 24]
        out_ref[i, 24:, :] = tail


def total_kernel(core_ref, in_ref, out_ref):
    total = in_ref[0].astype(F32)
    for i in range(1, 8):
        total = total + in_ref[i].astype(F32)
    out_ref[...] = total.astype(BF)


def share_kernel(place_ref, own_ref, got_ref, out_ref):
    core, y = place_ref[0], place_ref[1]
    own, got = own_ref[...].astype(F32), got_ref[...].astype(F32)
    own_rows = pick(core, own[:12], own[12:24])
    got_rows = pick(core, got[:12], got[12:24])
    both = jnp.concatenate([pick(core, own_rows, got_rows), pick(core, got_rows, own_rows)], axis=0)
    out_ref[:24, WIDTH:] = both[:, WIDTH:].astype(BF)
    out_ref[:24, :WIDTH] = jnp.where(y < 2, both[:, :WIDTH], own[:24, :WIDTH]).astype(BF)
    out_ref[24:32, :] = pick(core, own[24:], got[24:]).astype(BF)
    out_ref[32:, :] = pick(core, got[24:], own[24:]).astype(BF)


def last_kernel(
    place_ref, part0_ref, part1_ref, part2_ref, part3_ref,
    qkv_ref, out_ref, up_ref, down_ref, *refs,
):
    small_refs, freq_ref, scr_ref = refs[:8], refs[8], refs[9]
    core, y, chip = place_ref[0], place_ref[1], place_ref[2]
    device = (2 * chip + core).astype(F32)
    for i, ref in enumerate((part0_ref, part1_ref, part2_ref, part3_ref)):
        scr_ref[i] = ref[...].astype(F32)
    ups = []
    for q in range(4):
        rows = scr_ref[lax.bitwise_and(q + 4 - y, 3)]
        for c in range(2):
            cols = rows[12 * c : 12 * c + 12, WIDTH:]
            if q < 3:
                qkv_ref[:, WIDTH * q + HALF * c : WIDTH * q + HALF * c + HALF] = cols
            else:
                out_ref[:, HALF * c : HALF * c + HALF] = cols
            if q < 2:
                ups.append((c, q, rows[12 * c : 12 * c + 12, :WIDTH].astype(BF)))
        if q > 1:
            down_ref[24 * (q - 2) : 24 * (q - 2) + 24, :] = rows[:24, :WIDTH]
    group, inner = split_index(lax.broadcasted_iota(jnp.int32, (HALF, 1), 0).astype(F32), 24)
    col = lax.broadcasted_iota(jnp.int32, (HALF, 4 * HALF), 1).astype(F32)
    halves = [0.0, 0.0]
    for c, q, piece in ups:
        spread_out = jnp.where(col == 96.0 * group + 48.0 * c + 24.0 * q + inner, 1.0, 0.0).astype(BF)
        for g in range(2):
            halves[g] = halves[g] + dot(piece[:, HALF * g : HALF * g + HALF], spread_out)
    for g in range(2):
        up_ref[:, 4 * HALF * g : 4 * HALF * g + 4 * HALF] = halves[g]
    rows = scr_ref[lax.bitwise_and(7 - y, 3)]
    tails = [
        jnp.concatenate(
            [rows[24 + 8 * c : 32 + 8 * c, HALF * k : HALF * k + HALF] for k in range(3)], axis=0
        ).astype(BF)
        for c in range(2)
    ]
    sub = lax.broadcasted_iota(jnp.int32, (HALF, 128), 0).astype(F32)
    lane = lax.broadcasted_iota(jnp.int32, (HALF, 128), 1).astype(F32)

    def take(tail, want, limit):
        hot = jnp.where(jnp.logical_and(sub == want, lane < limit), 1.0, 0.0).astype(BF)
        return dot(tail, hot)

    entry = 12.0 * device + lane
    low = sum(take(tail, entry, 12) for tail in tails)
    high = sum(take(tail, entry - HALF, 12) for tail in tails)
    rows = [low[3 + i : 4 + i] + high[4 + i : 5 + i] for i in (0, 2, 6, 8, 10, 12)]
    entry = 36.0 * device + lane
    bias = 0.0
    for t in range(3):
        for c in range(2):
            bias = bias + take(tails[c], entry - (WIDTH * t + HALF * c), 36)[t : t + 1]
    rows.append(bias)
    own = pick(core, tails[0], tails[1])
    entry = 24.0 * chip.astype(F32) + lane
    bias = 0.0
    for h in range(2):
        shifted = entry - 24.0 * h
        fits = jnp.logical_and(lane >= 24.0 * h, lane < 24.0 * h + 24.0)
        for k in range(2):
            want = jnp.where(fits, shifted - HALF * k, -1.0)
            bias = bias + take(own, want, 48)[17 + 2 * h + k : 18 + 2 * h + k]
    rows.append(bias)
    side = jnp.where(chip < 16, 0.0, 1.0)
    source = jnp.where(chip < 16, tails[0], tails[1])
    head, inner = split_index(6.0 * device + lane - 192.0 * side, 32)
    freq = take(source, 64.0 * head + inner, 6)
    freq_ref[...] = freq[7:9, :6]
    for ref, row in zip(small_refs, rows):
        ref[...] = row[0, : ref.shape[0]]


def per_device(
    tokens, image_ids, patch_row, patch_col, cotangent,
    norm1_gain, norm1_bias, qkv_weight, qkv_bias, frequencies, out_weight, out_bias,
    norm2_gain, norm2_bias, up_weight, up_bias, down_weight, down_bias,
):
    x, y, z, core = (lax.axis_index(a) for a in ("x", "y", "z", "c"))
    place = jnp.stack([core, y, x * NZ + z, z, x]).astype(jnp.int32)
    chip = x * NZ + z
    core_arr = core.reshape(1).astype(jnp.int32)

    groups = [norm1_gain, norm1_bias, out_bias, norm2_gain, norm2_bias, down_bias, qkv_bias, up_bias]
    small = jnp.concatenate(groups + [frequencies[0], frequencies[1], jnp.zeros((216,), BF)])[None]
    pieces = []
    for c in range(2):
        cols = [qkv_weight[:, WIDTH * i + HALF * c : WIDTH * i + HALF * c + HALF] for i in range(3)]
        cols.append(out_weight[:, HALF * c : HALF * c + HALF])
        piece = cols[3]
        for i in range(3):
            piece = jnp.where(y == i, cols[i], piece)
        pieces.append(jnp.concatenate([piece, small, jnp.zeros((3, HALF), BF)], axis=0))
    block = jnp.broadcast_to(jnp.stack(pieces)[None], (NZ, 2, 16, HALF)).reshape(256, HALF)
    up_split = up_weight.reshape(12, 32, 2, 2, 24)
    up_halves = [up_split[:, :, c].transpose(0, 2, 1, 3).reshape(12, FF_HALF) for c in range(2)]
    up_own = jnp.where(core == 0, up_halves[0], up_halves[1])
    up_other = jnp.where(core == 0, up_halves[1], up_halves[0])
    up_pack = in_core_order(core, up_own, swap(up_other))
    mlp_pack = jnp.concatenate([up_pack, down_weight[:24], down_weight[24:]], axis=1)

    f = ("x", "z", "c")
    onward = [(i, i + 1) for i in range(2 * NX * NZ - 1)]
    backward = [(b, a) for a, b in onward]
    spots = jnp.stack([patch_row[0], patch_col[0]], axis=1).astype(BF)
    own = jnp.concatenate([tokens[0], jnp.pad(spots, ((0, 0), (0, 126)))], axis=1)
    lower, upper = lax.ppermute(own, f, onward), lax.ppermute(own, f, backward)
    near = lax.dynamic_slice_in_dim(jnp.pad(image_ids[0] + 1, (TOK, TOK)), chip * CHIP_TOK, 4 * TOK, 0)
    ids = near[None].astype(F32)

    mlp = lax.all_gather(mlp_pack, ("x", "z"), axis=0, tiled=True)
    block = lax.all_to_all(block, ("z", "c"), split_axis=0, concat_axis=0, tiled=True)
    block = block.reshape(16, 16, HALF)
    rows, lines = block[:, :12].reshape(192, HALF), block[:, 12]
    low = jnp.concatenate([rows[:96], lines[:8]], axis=0)
    high = jnp.concatenate([rows[96:], lines[8:]], axis=0)
    low = jnp.stack(around_axis(low, "x", NX))
    high = jnp.stack(around_axis(high, "y", NY))
    low, high, lower, upper, dy_own = lax.optimization_barrier((low, high, lower, upper, cotangent[0]))
    edge = jnp.where(core == 0, lower, upper)
    far = swap(edge)
    sources = [own, lower, upper, far]
    dy_other = swap(dy_own)
    by_y = around_axis(low, "y", NY)
    by_x = around_axis(high, "x", NX)

    wide, half, square = ((CHIP_TOK, WIDTH), BF), ((CHIP_TOK, HALF), BF), ((HALF, HALF), BF)
    ids, *parts = lax.optimization_barrier((ids, *by_y, *by_x))
    q, k, v, keep, send, *kept = qkv_call(place, sources, parts[:4], parts[4:])
    q_kept, k_kept, v_kept, vec, a1, turn, weights, inputs = kept
    got = swap(send)
    branch, o, lse, out_rows = attend(core_arr, q, k, v, ids, keep, got)

    branch, mlp = lax.optimization_barrier((branch, mlp))
    da2, high, middle, result, result_send, du_sums, *lows = mlp_call(
        place, branch, swap(branch), inputs, vec, mlp, dy_own, dy_other
    )
    output = (result + swap(result_send).astype(F32)).astype(BF)[None]
    mlp_high = scatter_sum(high, "y").reshape(4, 96, WIDTH)
    mlp_lows = [fetch(part, "x", NX, k) for k, part in enumerate(lows)]

    do, delta, to_prev, to_next, out_own, out_send, sums, dmid = whole_call(
        branch_kernel, "branch",
        [((CHIP_TOK, HALF), BF), ((3, 2, CHIP_TOK), F32), ((288, HALF), BF), ((288, HALF), BF),
         ((HALF, HALF), BF), ((HALF, HALF), BF), ((4, WIDTH), F32), ((TOK, WIDTH), F32)],
        core_arr, [da2, swap(da2), middle, dy_own, dy_other, vec, o, out_rows, lse],
        scratch=[
            pltpu.VMEM((CHIP_TOK, WIDTH), F32), pltpu.VMEM((CHIP_TOK, WIDTH), F32),
            pltpu.VMEM((CHIP_TOK, WIDTH), BF), pltpu.VMEM((8, WIDTH), F32), pltpu.VMEM((CHIP_TOK, HALF), BF),
            pltpu.VMEM((HALF, WIDTH), BF), pltpu.VMEM((3, 2, CHIP_TOK), F32), pltpu.SemaphoreType.DMA((8,)),
        ],
        flops=10**9, vmem=16, far=(7,), away=tuple(range(2, 9)),
    )
    up_list = [(i, i + 1) for i in range(NX * NZ - 1)]
    down_list = [(b, a) for a, b in up_list]
    from_prev = lax.ppermute(to_next, ("x", "z"), up_list)
    from_next = lax.ppermute(to_prev, ("x", "z"), down_list)
    dq, dkv = near_back(core_arr, q_kept, k_kept, v_kept, do, lse, delta, ids)
    *parts, da1_own, da1_send = qkv_grad_call(
        place, [dq, dkv, from_prev, from_next, out_own, swap(out_send), sums],
        q_kept, k_kept, v_kept, turn, a1, inputs, weights, ids, du_sums,
    )
    lows = [fetch(part, "x", NX, k) for k, part in enumerate(parts[:4])]
    highs = [fetch(part, "y", NY, k) for k, part in enumerate(parts[4:])]
    da1 = da1_own + swap(da1_send).astype(F32)
    unit, scale = centred(tokens[0].astype(F32))
    input_grad = (centred_back(unit, scale, da1 * vec[0]) + dmid)[None]

    seconds = whole_call(
        mid_kernel, "mid", [((120, 3 * HALF), BF)] * 4 + [((96, 3 * HALF), BF)] * 4, place,
        [*lows, *highs, *mlp_lows, mlp_high],
        scratch=[
            pltpu.VMEM((4, 104, HALF), BF), pltpu.VMEM((4, 96, HALF), BF), pltpu.VMEM((4, 96, WIDTH), BF),
        ],
        vmem=14,
    )
    lows = [fetch(part, "y", NY, k) for k, part in enumerate(seconds[:4])]
    highs = [fetch(part, "x", NX, k) for k, part in enumerate(seconds[4:])]
    (joined,) = whole_call(
        join_kernel, "join", [((8, 32, 3 * HALF), BF)], core_arr, lows + highs
    )
    joined = lax.all_to_all(
        joined.reshape(256, 3 * HALF), "z", split_axis=0, concat_axis=0, tiled=True
    )
    (mine,) = whole_call(
        total_kernel, "total", [((32, 3 * HALF), BF)],
        core_arr, [joined.reshape(8, 32, 3 * HALF)],
    )
    (part,) = whole_call(
        share_kernel, "share", [((40, 3 * HALF), BF)], place, [mine, swap(mine)]
    )
    parts = [fetch(part, "y", NY, k) for k in range(NY)]
    qkv_grad, out_weight_grad, up_grad, down_grad, *smalls, freq_grad = whole_call(
        last_kernel, "last",
        [((12, 3 * WIDTH), F32), ((12, WIDTH), F32), ((12, 4 * WIDTH), F32), ((48, WIDTH), F32)]
        + [((size,), F32) for size in (12, 12, 12, 12, 12, 12, 36, 48)]
        + [((2, 6), F32)],
        place, parts, scratch=[pltpu.VMEM((4, 40, 3 * HALF), F32)],
    )
    qkv_bias_grad, up_bias_grad = smalls[6:]
    return (
        output, input_grad,
        smalls[0], smalls[1], qkv_grad, qkv_bias_grad, freq_grad, out_weight_grad, smalls[2],
        smalls[3], smalls[4], up_grad, up_bias_grad, down_grad, smalls[5],
    )


def solution(mesh):
    fine = Mesh(mesh.devices.reshape(NY, NX, NZ, 2), ("y", "x", "z", "c"))
    f = ("x", "z", "c")
    return jax.shard_map(
        per_device,
        mesh=fine,
        in_specs=(
            P("y", f, None), P("y", None), P("y", f), P("y", f), P("y", f, None),
            P(f), P(f), P(f, None), P(f), P(None, f), P(f, None), P(f),
            P(f), P(f), P(f, None), P(f), P(f, None), P(f),
        ),
        out_specs=(
            P("y", f, None), P("y", f, None),
            P(f), P(f), P(f, None), P(f), P(None, f), P(f, None), P(f),
            P(f), P(f), P(f, None), P(f), P(f, None), P(f),
        ),
        check_vma=False,
    )
```

```python
import jax
import jax.numpy as jnp
from jax import lax
from jax.experimental import pallas as pl
from jax.experimental.pallas import tpu as pltpu
from jax.sharding import Mesh, PartitionSpec as P

NX, NY, NZ = 4, 4, 8
HEADS = 12
LOCAL_HEADS = 6
WIDTH = 768
HALF = 384
FF_HALF = 1536
TOK = 256
CHIP_TOK = 512
MASKED = -1e30
BF = jnp.bfloat16
F32 = jnp.float32
MIB = 1 << 20
OWN = slice(TOK, 3 * TOK)


def fetch(value, axis, size, step):
    if step == 0:
        return value
    return lax.ppermute(value, axis, [((i + step) % size, i) for i in range(size)])


def swap(value):
    return lax.ppermute(value, "c", [(0, 1), (1, 0)])


def in_core_order(core, own, other):
    first = jnp.where(core == 0, own, other)
    second = jnp.where(core == 0, other, own)
    return jnp.concatenate([first, second], axis=0)


def dot(a, b):
    return jnp.dot(a, b, preferred_element_type=F32)


def dot_nt(a, b):
    return lax.dot_general(a, b, (((1,), (1,)), ((), ())), preferred_element_type=F32)


def dot_tn(a, b):
    return lax.dot_general(a, b, (((0,), (0,)), ((), ())), preferred_element_type=F32)


def around_axis(block, axis, size):
    return [fetch(block, axis, size, k) for k in range(size)]


def scatter_sum(blocks, axis):
    count, rows, cols = blocks.shape
    return lax.psum_scatter(
        blocks.reshape(count * rows, cols), axis, scatter_dimension=0, tiled=True
    )


def whole_call(kernel, name, outs, scalars, arrays, scratch=(), flops=0, vmem=10, far=(), away=()):
    size = sum(v.size * v.dtype.itemsize for v in arrays)
    spec = lambda remote: pl.BlockSpec(memory_space=pl.ANY if remote else pltpu.VMEM)
    shapes = [(pltpu.HBM if i in far else jax.ShapeDtypeStruct)(*o) for i, o in enumerate(outs)]
    return pl.pallas_call(
        kernel,
        out_shape=shapes,
        in_specs=[pl.BlockSpec(memory_space=pltpu.SMEM)]
        + [spec(i in away) for i in range(len(arrays))],
        out_specs=[spec(i in far) for i in range(len(outs))],
        scratch_shapes=list(scratch),
        compiler_params=pltpu.CompilerParams(vmem_limit_bytes=vmem * MIB),
        cost_estimate=pl.CostEstimate(flops=flops, bytes_accessed=size, transcendentals=0),
        name=name,
    )(
        scalars,
        *[
            pltpu.with_memory_space_constraint(v, pltpu.HBM) if i in away else v
            for i, v in enumerate(arrays)
        ],
    )


class Mover:
    def __init__(self, sems):
        self.sems, self.count, self.open = sems, 0, []

    def start(self, source, target):
        copy = pltpu.make_async_copy(source, target, self.sems.at[self.count])
        self.count += 1
        copy.start()
        return copy

    def load(self, pairs):
        return [self.start(source, target) for source, target in pairs]

    def put(self, source, target):
        self.open.append(self.start(source, target))

    def finish(self):
        for copy in self.open:
            copy.wait()


def wait_all(copies):
    for copy in copies:
        copy.wait()


def id_columns(row_ref):
    return jnp.transpose(jnp.broadcast_to(row_ref[...], (8, 4 * TOK)))[:, :1]


def two_heads(block):
    lane = lax.broadcasted_iota(jnp.int32, block.shape, 1)
    zero = jnp.zeros_like(block)
    return jnp.concatenate(
        [jnp.where(lane < 64, block, zero), jnp.where(lane < 64, zero, block)], axis=0
    )


def by_head(first, second):
    row = lax.broadcasted_iota(jnp.int32, first.shape, 0)
    return jnp.where(row < 64, first, second)


def scaled(block):
    return block * jnp.asarray(0.125, BF)


def pair_of(i):
    return pl.ds(pl.multiple_of(128 * i, 128), 128)


def attend_kernel(
    core_ref, q_ref, k_ref, v_ref, keep_ref, got_ref, id_hbm,
    part_ref, o_hbm, lse_hbm, w_hbm, o_ref, lse_ref, w_ref, id_ref, kid_ref, sems,
):
    mover = Mover(sems)
    mover.start(id_hbm, id_ref).wait()
    w_ref[:, :HALF] = pick(core_ref[0], keep_ref[...], got_ref[...])
    w_ref[:, HALF:] = pick(core_ref[0], got_ref[...], keep_ref[...])
    mover.put(w_ref, w_hbm)
    kid_ref[...] = id_columns(id_ref)

    def body(i, carry):
        pair = pair_of(i)
        v_turned = jnp.transpose(v_ref[:, pair])
        for tile in range(2):
            near = slice(TOK * tile, TOK * tile + 3 * TOK)
            mine = slice(TOK * tile + TOK, TOK * tile + 2 * TOK)
            here = slice(TOK * tile, TOK * tile + TOK)
            keep = kid_ref[near, :] == id_ref[0:1, mine]
            scores = dot_nt(k_ref[near, pair], two_heads(scaled(q_ref[mine, pair])))
            halves = []
            for h in range(2):
                s = jnp.where(keep, scores[:, TOK * h : TOK * h + TOK], MASKED)
                top = jnp.max(s, axis=0, keepdims=True)
                expo = jnp.exp(s - top)
                total = jnp.sum(expo, axis=0, keepdims=True)
                lse_ref[i, h : h + 1, here] = top + jnp.log(total)
                p = (expo * (1.0 / total)).astype(BF)
                halves.append(dot(v_turned[:, near], p))
            o_ref[here, pair] = jnp.transpose(by_head(*halves)).astype(BF)
        return carry

    lax.fori_loop(0, 3, body, 0)
    mover.put(o_ref, o_hbm)
    mover.put(lse_ref, lse_hbm)
    part_ref[...] = dot(o_ref[...], w_ref[...]).astype(BF)
    mover.finish()


def attend(core, q, k, v, ids, keep, got):
    o, lse, weights = ((CHIP_TOK, HALF), BF), ((3, 2, CHIP_TOK), F32), ((HALF, WIDTH), BF)
    return whole_call(
        attend_kernel, "attend", [((CHIP_TOK, WIDTH), BF), o, lse, weights],
        core, [q, k, v, keep, got, ids],
        scratch=[
            pltpu.VMEM(*o), pltpu.VMEM(*lse), pltpu.VMEM(*weights),
            pltpu.VMEM((1, 4 * TOK), F32), pltpu.VMEM((4 * TOK, 1), F32), pltpu.SemaphoreType.DMA((8,)),
        ],
        flops=3 * 10**9, vmem=12, far=(1, 2, 3), away=(5,),
    )


def pair_grads(k, v, q2, do2, keep, lses, deltas):
    scores = dot_nt(k, q2)
    dprobs = dot_nt(v, do2)
    probs, dscores = [], []
    for h in range(2):
        lanes = slice(TOK * h, TOK * h + TOK)
        p = jnp.exp(jnp.where(keep, scores[:, lanes], MASKED) - lses[h])
        dscores.append((p * (dprobs[:, lanes] - deltas[h])).astype(BF))
        probs.append(p.astype(BF))
    return probs, dscores


def near_back_kernel(
    core_ref, q_hbm, k_hbm, v_hbm, turn_hbm, a1_hbm, x_hbm, w_hbm, lse_hbm, id_hbm, do_ref, delta_ref,
    dq_ref, dkv_ref, q_ref, k_ref, v_ref, turn_ref, a1_ref, x_ref, w_ref,
    lse_ref, id_ref, kid_ref, sems, more_sems,
):
    mover = Mover(more_sems)
    first_loads = mover.load(((id_hbm, id_ref), (lse_hbm, lse_ref)))
    sources = ((q_hbm, q_ref), (k_hbm, k_ref), (v_hbm, v_ref))

    def load(i):
        return [
            pltpu.make_async_copy(source.at[:, pair_of(i)], target.at[:, pair_of(i)], sems.at[i, j])
            for j, (source, target) in enumerate(sources)
        ]

    for i in range(3):
        for copy in load(i):
            copy.start()
    later = mover.load(
        ((turn_hbm, turn_ref), (a1_hbm, a1_ref), (w_hbm.at[pl.ds(0, 3)], w_ref), (x_hbm, x_ref))
    )
    wait_all(first_loads)
    kid_ref[...] = id_columns(id_ref)

    def body(i, carry):
        pair = pair_of(i)
        wait_all(load(i))
        k_turned = jnp.transpose(k_ref[:, pair])
        for tile in range(2):
            near = slice(TOK * tile, TOK * tile + 3 * TOK)
            mine = slice(TOK * tile + TOK, TOK * tile + 2 * TOK)
            here = slice(TOK * tile, TOK * tile + TOK)
            k = k_ref[near, pair]
            q2 = two_heads(scaled(q_ref[mine, pair]))
            do2 = two_heads(do_ref[here, pair])
            keep = kid_ref[near, :] == id_ref[0:1, mine]
            probs, dscores = pair_grads(
                k, v_ref[near, pair], q2, do2, keep,
                [lse_ref[i, h : h + 1, here] for h in range(2)],
                [delta_ref[i, h : h + 1, here] for h in range(2)],
            )
            dq = by_head(*[dot(k_turned[:, near], ds) for ds in dscores])
            dq_ref[here, pair] = jnp.transpose(dq) * 0.125
            first = TOK * (1 - tile)
            own = slice(first, first + 2 * TOK)
            dk = dot(jnp.concatenate([d[own] for d in dscores], axis=1), q2)
            dv = dot(jnp.concatenate([p[own] for p in probs], axis=1), do2)
            for which, full in enumerate((dk, dv)):
                if tile == 0:
                    dkv_ref[which, :, pair] = full
                else:
                    dkv_ref[which, :, pair] += full
        return carry

    lax.fori_loop(0, 3, body, 0)
    wait_all(later)


def near_back(core, kept, grad, lse, delta, ids):
    around = ((4 * TOK, HALF), BF)
    return whole_call(
        near_back_kernel, "near_back",
        [
            ((CHIP_TOK, HALF), F32), ((2, CHIP_TOK, HALF), F32), around, around, around,
            ((2, CHIP_TOK, HALF), F32), ((CHIP_TOK, WIDTH), BF), ((CHIP_TOK, WIDTH + 128), BF),
            ((3, WIDTH, HALF), BF),
        ],
        core, [*kept, lse, ids, grad, delta], away=tuple(range(9)),
        scratch=[
            pltpu.VMEM((3, 2, CHIP_TOK), F32), pltpu.VMEM((1, 4 * TOK), F32),
            pltpu.VMEM((4 * TOK, 1), F32), pltpu.SemaphoreType.DMA((3, 3)), pltpu.SemaphoreType.DMA((8,)),
        ],
        flops=4 * 10**9, vmem=12,
    )


def far_back(q_ref, k_ref, v_ref, before_ref, after_ref, id_ref, kid_ref, dkv_ref, sum_ref):
    row = lax.broadcasted_iota(jnp.int32, (8, TOK), 0)

    def body(i, carry):
        pair = pair_of(i)
        for side, ref in enumerate((before_ref, after_ref)):
            keys = slice(TOK * (side + 1), TOK * (side + 2))
            queries = slice(3 * TOK * side, 3 * TOK * side + TOK)
            tail = ref[TOK:, :TOK].astype(F32)
            deltas = tail[0:8] + tail[8:16]
            lses = tail[16:24] + tail[24:32]
            choose = lambda v, h: jnp.sum(
                jnp.where(row == 2 * i + h, v, 0.0), axis=0, keepdims=True
            )
            q2 = two_heads(scaled(q_ref[queries, pair]))
            do2 = two_heads(ref[:TOK, pair])
            keep = kid_ref[keys, :] == id_ref[0:1, queries]
            probs, dscores = pair_grads(
                k_ref[keys, pair], v_ref[keys, pair], q2, do2, keep,
                [choose(lses, h) for h in range(2)], [choose(deltas, h) for h in range(2)],
            )
            rows = slice(TOK * side, TOK * side + TOK)
            dk = dot(jnp.concatenate(dscores, axis=1), q2)
            dv = dot(jnp.concatenate(probs, axis=1), do2)
            sum_ref[0, rows, pair] = dkv_ref[0, rows, pair] + dk
            sum_ref[1, rows, pair] = dkv_ref[1, rows, pair] + dv
        return carry

    lax.fori_loop(0, 3, body, 0)


def centred(value):
    shifted = value - jnp.mean(value, axis=-1, keepdims=True)
    spread = jnp.mean(shifted * shifted, axis=-1, keepdims=True)
    scale = lax.rsqrt(spread + 1e-06)
    return shifted * scale, scale


def centred_back(unit, scale, grad):
    mean = jnp.mean(grad, axis=-1, keepdims=True)
    along = jnp.mean(grad * unit, axis=-1, keepdims=True)
    return scale * (grad - mean - unit * along)


def lanes_of(width):
    return lax.broadcasted_iota(jnp.int32, (1, width), 1).astype(F32)


def pick(core, first, second):
    return jnp.where(core == 0, first, second)


def expand(lines, shift, lane_in, owner):
    width = lane_in.shape[1]
    moved = pltpu.roll(lines, (HALF - shift) % HALF, 1)[:, :128].astype(BF)
    sub = lax.broadcasted_iota(jnp.int32, (128, width), 0).astype(F32)
    table = dot(moved, jnp.where(sub == lane_in, 1.0, 0.0).astype(BF))
    sub = lax.broadcasted_iota(jnp.int32, (64, width), 0).astype(F32)
    return jnp.sum(jnp.where(sub == owner, table, 0.0), axis=0, keepdims=True)


def split_index(index, size):
    group = jnp.floor((index + 0.5) * (1.0 / size))
    return group, index - group * size


def low_half(shape):
    return lax.bitwise_and(lax.broadcasted_iota(jnp.int32, shape, 1), 63) < 32


def swap_halves(value):
    ahead = pltpu.roll(value, HALF - 32, 1)
    behind = pltpu.roll(value, 32, 1)
    return jnp.where(low_half(value.shape), ahead, behind)


def three_parts(value):
    parts = []
    for _ in range(3):
        part = value.astype(BF)
        parts.append(part)
        value = value - part.astype(F32)
    return jnp.concatenate(parts, axis=0)


def qkv_kernel(place_ref, *refs):
    by_y, by_x, sources, refs = refs[:4], refs[4:8], refs[8:12], refs[12:]
    q_ref, k_ref, v_ref, keep_ref, send_ref = refs[:5]
    q_hbm, k_hbm, v_hbm, vec_hbm, a1_hbm, turn_hbm, w_hbm, x_hbm = refs[5:13]
    table_ref, bias_ref, line_ref, x_ref, a1_ref, turn_ref, w_ref, vec_ref, sems, x_sems = refs[13:]
    core, x, y = place_ref[0], place_ref[4], place_ref[1]
    mover = Mover(sems)

    def x_load(step, source):
        return pltpu.make_async_copy(source, x_ref.at[pl.ds(TOK * step, TOK), :], x_sems.at[step])

    own, lower, upper, far = sources

    @pl.when(core == 0)
    def _():
        for step, source in enumerate((lower, own, upper, far)):
            x_load(step, source).start()

    @pl.when(core == 1)
    def _():
        for step, source in enumerate((far, lower, own, upper)):
            x_load(step, source).start()

    core_f = core.astype(F32)
    for ky in range(4):
        for kx in range(4):
            q = lax.bitwise_and(y + ky, 3)
            chip = lax.bitwise_and(x + kx, 3)
            low = pl.ds(pl.multiple_of(192 * chip, 96), 96)
            high = pl.ds(pl.multiple_of(192 * chip + 96, 96), 96)
            w_ref[q, low, :] = by_y[ky][kx, :96, :]
            w_ref[q, high, :] = by_x[kx][ky, :96, :]
    for kx in range(4):
        chip = lax.bitwise_and(x + kx, 3)
        low = pl.ds(pl.multiple_of(16 * chip, 8), 8)
        high = pl.ds(pl.multiple_of(16 * chip + 8, 8), 8)
        line_ref[low, :] = by_y[0][kx, 96:, :].astype(F32)
        line_ref[high, :] = by_x[kx][0, 96:, :].astype(F32)
    lines = line_ref[...]
    group, inner = split_index(lanes_of(WIDTH), 12)
    rows = [expand(lines, 12 * i, inner, group) for i in range(6)]
    group, inner = split_index(lanes_of(WIDTH), 24)
    rows += [expand(lines, 108 + 24 * h, inner, 2.0 * group + core_f) for h in range(2)]
    vec_ref[...] = jnp.concatenate(rows, axis=0)
    group, inner = split_index(lanes_of(3 * WIDTH), 36)
    bias = expand(lines, 72, inner, group)
    for i in range(3):
        bias_ref[i : i + 1, :] = pick(
            core,
            bias[:, WIDTH * i : WIDTH * i + HALF],
            bias[:, WIDTH * i + HALF : WIDTH * i + WIDTH],
        )
    lane = lanes_of(HALF)
    head, _ = split_index(lane, 64)
    _, inner = split_index(lane, 32)
    group, inner = split_index(192.0 * core_f + 32.0 * head + inner, 6)
    count = lax.broadcasted_iota(jnp.int32, (32, HALF), 0).astype(F32)
    for f in range(2):
        angle = count * expand(lines, 156 + 6 * f, inner, group)
        table_ref[f] = three_parts(jnp.concatenate([jnp.cos(angle), jnp.sin(angle)], axis=1))
    keep_ref[...] = w_ref[3, pl.ds(pl.multiple_of(HALF * core, HALF), HALF), :]
    send_ref[...] = w_ref[3, pl.ds(pl.multiple_of(HALF * (1 - core), HALF), HALF), :]
    mover.put(w_ref, w_hbm)
    mover.put(vec_ref, vec_hbm)
    for step in range(4):
        rows = slice(TOK * step, TOK * step + TOK)
        x_load(step, own).wait()
        spots = x_ref[rows, WIDTH:].astype(F32)
        spot = lax.bitwise_and(lax.broadcasted_iota(jnp.int32, (TOK, 96), 1), 31).astype(F32)
        tables = [
            dot(jnp.where(spots[:, f : f + 1] == spot, 1.0, 0.0).astype(BF), table_ref[f])
            for f in range(2)
        ]
        cos_r, sin_r = tables[0][:, :HALF], tables[0][:, HALF:]
        cos_c, sin_c = tables[1][:, :HALF], tables[1][:, HALF:]
        cosine = cos_r * cos_c - sin_r * sin_c
        sine = sin_r * cos_c + cos_r * sin_c
        sine = jnp.where(low_half(sine.shape), -sine, sine)
        unit, _ = centred(x_ref[rows, :WIDTH].astype(F32))
        a1 = (unit * vec_ref[0:1, :] + vec_ref[1:2, :]).astype(BF)
        if step in (1, 2):
            here = slice(TOK * (step - 1), TOK * step)
            turn_ref[0, here, :] = cosine
            turn_ref[1, here, :] = sine
            a1_ref[here, :] = a1
            if step == 2:
                mover.put(x_ref.at[pl.ds(TOK, CHIP_TOK), :], x_hbm)
                mover.put(turn_ref, turn_hbm)
                mover.put(a1_ref, a1_hbm)
        for i, ref in enumerate((q_ref, k_ref, v_ref)):
            part = dot(a1, w_ref[i]) + bias_ref[i : i + 1, :]
            if i < 2:
                part = part * cosine + swap_halves(part) * sine
            ref[rows, :] = part.astype(BF)
            mover.put(ref.at[pl.ds(TOK * step, TOK), :], (q_hbm, k_hbm, v_hbm)[i].at[pl.ds(TOK * step, TOK), :])
    mover.finish()


def qkv_call(place, sources, by_y, by_x):
    around, square = ((4 * TOK, HALF), BF), ((HALF, HALF), BF)
    wide, turn = ((CHIP_TOK, WIDTH), BF), ((2, CHIP_TOK, HALF), F32)
    vec, full = ((8, WIDTH), F32), ((4, WIDTH, HALF), BF)
    return whole_call(
        qkv_kernel, "qkv",
        [around, around, around, square, square, around, around, around, vec, wide, turn, full]
        + [((CHIP_TOK, WIDTH + 128), BF)],
        place, [*by_y, *by_x, *sources],
        scratch=[
            pltpu.VMEM((2, 96, WIDTH), BF), pltpu.VMEM((8, HALF), F32), pltpu.VMEM((64, HALF), F32),
            pltpu.VMEM((4 * TOK, WIDTH + 128), BF), pltpu.VMEM(*wide), pltpu.VMEM(*turn),
            pltpu.VMEM(*full), pltpu.VMEM(*vec), pltpu.SemaphoreType.DMA((24,)),
            pltpu.SemaphoreType.DMA((4,)),
        ],
        flops=2 * 10**9, vmem=18, far=tuple(range(5, 13)), away=tuple(range(8, 12)),
    )


def mlp_kernel(
    place_ref, part_ref, got_ref, x_hbm, vec_hbm, w_hbm, dya_hbm, dyb_hbm,
    da2_ref, high_hbm, mid_hbm, own_hbm, send_hbm, sums_hbm, *refs,
):
    low_hbms = refs[:4]
    acc_ref, grads_ref, x_ref, w_ref, dy_ref, mid_ref, own_ref, send_ref, vec_ref, sums_ref = refs[4:14]
    act_ref, du_ref, sems = refs[14:]
    core, x = place_ref[0], place_ref[4]
    own = pl.ds(pl.multiple_of(core * TOK, TOK), TOK)
    rest = pl.ds(pl.multiple_of((1 - core) * TOK, TOK), TOK)
    mover = Mover(sems)
    load_x = mover.load(((x_hbm.at[:, pl.ds(0, WIDTH)], x_ref), (vec_hbm, vec_ref)))
    loads = []
    for i in (0, 2, 1, 3):
        cols = pl.ds(WIDTH * i, WIDTH)
        loads.append(mover.start(w_hbm.at[:, cols], w_ref.at[:, cols]))
        if i == 0:
            load_dy = mover.load(((dya_hbm, dy_ref.at[own, :]), (dyb_hbm, dy_ref.at[rest, :])))

    def put(index, value):
        grads_ref[index] = value.astype(BF)
        for k, ref in enumerate(low_hbms):
            row = pl.multiple_of(192 * lax.bitwise_and(x + 4 - k, 3), 96)
            mover.put(grads_ref.at[index, pl.ds(row, 96), :], ref.at[index])
        for j in range(4):
            rows = pl.ds(192 * j + 96, 96)
            mover.put(grads_ref.at[index, rows, :], high_hbm.at[index, pl.ds(96 * j, 96), :])

    wait_all(load_x)
    middle = x_ref[...].astype(F32) + (
        part_ref[...].astype(F32) + got_ref[...].astype(F32) + vec_ref[2:3, :]
    )
    mid_ref[...] = middle
    mover.put(mid_ref, mid_hbm)
    unit, _ = centred(middle)
    a2 = (unit * vec_ref[3:4, :] + vec_ref[4:5, :]).astype(BF)
    a2_turned = jnp.transpose(a2)
    da2 = None
    for h in range(2):
        lanes = slice(WIDTH * h, WIDTH * h + WIDTH)
        loads[2 * h].wait()
        loads[2 * h + 1].wait()
        if h == 0:
            wait_all(load_dy)
        dy = dy_ref[...]
        up = w_ref[:, lanes]
        down = w_ref[:, FF_HALF + WIDTH * h : FF_HALF + WIDTH * h + WIDTH]
        for j in range(3):
            cols = slice(TOK * j, TOK * j + TOK)
            u = dot(a2, up[:, cols]) + vec_ref[6 + h : 7 + h, cols]
            gate = 0.5 * (1.0 + lax.erf(u * 0.7071067811865476))
            act_ref[:, cols] = (u * gate).astype(BF)
            slope = gate + u * jnp.exp(-0.5 * u * u) * 0.3989422804014327
            low = (slope * dot_nt(dy, down[cols, :])).astype(BF)
            du_ref[:, cols] = low
            sums_ref[h : h + 1, cols] = jnp.sum(low.astype(F32), axis=0, keepdims=True)
        act, du = act_ref[...], du_ref[...]
        put(2 + h, dot_tn(act, dy))
        put(h, dot(a2_turned, du))
        term = dot(act, down)
        if h == 0:
            acc_ref[...] = term
        else:
            acc_ref[...] += term
        term = dot_nt(du, up)
        da2 = term if da2 is None else da2 + term
    da2_ref[...] = da2.astype(BF)
    mover.put(sums_ref, sums_hbm)
    own_ref[...] = acc_ref[own, :] + mid_ref[own, :] + vec_ref[5:6, :]
    send_ref[...] = acc_ref[rest, :].astype(BF)
    mover.put(own_ref, own_hbm)
    mover.put(send_ref, send_hbm)
    mover.finish()


def mlp_call(place, branch, got, inputs, vec, weights, dy_own, dy_other):
    full, half = (CHIP_TOK, WIDTH), (TOK, WIDTH)
    return whole_call(
        mlp_kernel, "mlp",
        [(full, BF), ((4, HALF, WIDTH), BF), (full, F32), (half, F32), (half, BF), ((2, WIDTH), F32)]
        + [((4, 96, WIDTH), BF)] * 4,
        place, [branch, got, inputs, vec, weights, dy_own, dy_other],
        scratch=[
            pltpu.VMEM(full, F32), pltpu.VMEM((4, WIDTH, WIDTH), BF), pltpu.VMEM(full, BF),
            pltpu.VMEM((WIDTH, 4 * WIDTH), BF), pltpu.VMEM(full, BF), pltpu.VMEM(full, F32),
            pltpu.VMEM(half, F32), pltpu.VMEM(half, BF), pltpu.VMEM((8, WIDTH), F32),
            pltpu.VMEM((2, WIDTH), F32), pltpu.VMEM(full, BF), pltpu.VMEM(full, BF),
            pltpu.SemaphoreType.DMA((48,)),
        ],
        flops=8 * 10**9, vmem=34, far=tuple(range(1, 10)), away=tuple(range(2, 7)),
    )


def branch_kernel(
    core_ref, da2_ref, got_ref, mid_hbm, dya_hbm, dyb_hbm, vec_hbm, o_hbm, w_hbm, lse_hbm,
    do_ref, delta_ref, back_ref, on_ref, own_ref, send_ref, sums_ref, dmid_hbm,
    scr_ref, mid_ref, dy_ref, vec_ref, o_ref, w_ref, lse_ref, sems,
):
    core = core_ref[0]
    mover = Mover(sems)
    mine = pl.ds(pl.multiple_of(core * TOK, TOK), TOK)
    rest = pl.ds(pl.multiple_of((1 - core) * TOK, TOK), TOK)
    loads = mover.load(
        (
            (mid_hbm, mid_ref), (vec_hbm, vec_ref), (dya_hbm, dy_ref.at[mine, :]),
            (dyb_hbm, dy_ref.at[rest, :]), (w_hbm, w_ref), (o_hbm, o_ref), (lse_hbm, lse_ref),
        )
    )
    wait_all(loads)
    unit, scale = centred(mid_ref[...])
    da2 = da2_ref[...].astype(F32) + got_ref[...].astype(F32)
    dy = dy_ref[...].astype(F32)
    dmid = centred_back(unit, scale, da2 * vec_ref[3:4, :]) + dy
    low = dmid.astype(BF)
    scr_ref[...] = dmid
    mover.put(scr_ref.at[mine, :], dmid_hbm)
    do = dot_nt(low, w_ref[...]).astype(BF)
    do_ref[...] = do
    heads = lax.broadcasted_iota(jnp.int32, (8, HALF), 0)
    lane = lax.broadcasted_iota(jnp.int32, (8, HALF), 1)
    hot = jnp.where(jnp.logical_and(lane >= 64 * heads, lane < 64 * heads + 64), 1.0, 0.0)
    delta = lax.dot_general(
        hot, do.astype(F32) * o_ref[...].astype(F32), (((1,), (1,)), ((), ())),
        precision=lax.Precision.HIGHEST, preferred_element_type=F32,
    )
    for i in range(3):
        delta_ref[i] = delta[2 * i : 2 * i + 2]
    lse = jnp.concatenate([lse_ref[i] for i in range(3)] + [jnp.zeros((2, CHIP_TOK), F32)], axis=0)
    tail = []
    for value in (delta, lse):
        high = value.astype(BF)
        tail += [high, (value - high.astype(F32)).astype(BF)]
    tail = jnp.concatenate(tail, axis=0)
    for ref, rows in ((back_ref, slice(0, TOK)), (on_ref, slice(TOK, CHIP_TOK))):
        ref[:TOK, :] = do[rows]
        ref[TOK:, :] = jnp.concatenate([tail[:, rows], jnp.zeros((32, 128), BF)], axis=1)
    grad = dot_tn(o_ref[...], low).astype(BF)
    own_ref[...] = pick(core, grad[:, :HALF], grad[:, HALF:])
    send_ref[...] = pick(core, grad[:, HALF:], grad[:, :HALF])
    row = lax.broadcasted_iota(jnp.int32, (CHIP_TOK, 1), 0)
    here = jnp.logical_and(row >= core * TOK, row < core * TOK + TOK)
    total = lambda v: jnp.sum(jnp.where(here, v, 0.0), axis=0, keepdims=True)
    sums_ref[0:1, :] = total(low.astype(F32))
    sums_ref[1:2, :] = total(da2 * unit)
    sums_ref[2:3, :] = total(da2)
    sums_ref[3:4, :] = total(dy)
    mover.finish()


def qkv_grad_kernel(
    place_ref, dq_ref, near_ref, before_ref, after_ref, own_ref, got_ref, sums_ref,
    q_ref, k_ref, v_ref, turn_ref, a1_ref, x_ref, w_ref, id_hbm, more_hbm,
    *refs,
):
    low_hbms, high_hbms, da1_own_hbm, da1_send_hbm = refs[:4], refs[4:8], refs[8], refs[9]
    da1_ref, da1_send_ref, full_ref, tail_ref, dkv_ref, kid_ref, id_ref, more_ref, sems, high_sems = refs[10:]
    core, x, y = place_ref[0], place_ref[4], place_ref[1]
    mover = Mover(sems)
    wait_all(mover.load(((id_hbm, id_ref), (more_hbm, more_ref))))
    kid_ref[...] = id_columns(id_ref)
    far_back(q_ref, k_ref, v_ref, before_ref, after_ref, id_ref, kid_ref, near_ref, dkv_ref)

    def high_copies(step, k):
        return [
            pltpu.make_async_copy(
                full_ref.at[step, pl.ds(192 * j + 96, 96), :], high_hbms[k].at[j], high_sems.at[k, j]
            )
            for j in range(4)
        ]

    def hand_out(step, full):
        full_ref[step] = full
        for k, ref in enumerate(low_hbms):
            row = pl.multiple_of(192 * lax.bitwise_and(x + 4 - k, 3), 96)
            mover.put(full_ref.at[step, pl.ds(row, 96), :], ref.at[step, pl.ds(0, 96), :])
        for k in range(4):

            @pl.when(lax.bitwise_and(y + 4 - k, 3) == step)
            def _():
                for copy in high_copies(step, k):
                    copy.start()

    tail = []
    angle = 0.0
    a1_turned = jnp.transpose(a1_ref[...])
    for step, grad in enumerate((dq_ref[...], dkv_ref[0], dkv_ref[1])):
        if step < 2:
            other = swap_halves(grad)
            turned = (q_ref, k_ref)[step][OWN, :].astype(F32)
            angle = angle + other * turned - grad * swap_halves(turned)
            grad = grad * turn_ref[0] - other * turn_ref[1]
        low = grad.astype(BF)
        tail.append(jnp.sum(low.astype(F32), axis=0, keepdims=True))
        hand_out(step, dot(a1_turned, low).astype(BF))
        term = dot_nt(low, w_ref[step])
        if step == 0:
            da1_ref[...] = term
        else:
            da1_ref[...] += term
    first = pick(core, own_ref[...], got_ref[...])
    second = pick(core, got_ref[...], own_ref[...])
    hand_out(3, jnp.concatenate([first, second], axis=0))
    da1 = da1_ref[...]
    mover.put(da1_ref.at[pl.ds(pl.multiple_of(core * TOK, TOK), TOK), :], da1_own_hbm)
    da1_send_ref[...] = da1_ref[pl.ds(pl.multiple_of((1 - core) * TOK, TOK), TOK), :].astype(BF)
    mover.put(da1_send_ref, da1_send_hbm)
    unit, _ = centred(x_ref[:, :WIDTH].astype(F32))
    spots = x_ref[:, WIDTH:].astype(F32)
    halves = lambda v: [v[:, :HALF], v[:, HALF:]]
    tail += halves(jnp.sum(da1 * unit, axis=0, keepdims=True))
    tail += halves(jnp.sum(da1, axis=0, keepdims=True))
    tail += [jnp.sum(angle * spots[:, f : f + 1], axis=0, keepdims=True) for f in range(2)]
    for i in range(4):
        tail += halves(sums_ref[i : i + 1, :])
    for h in range(2):
        tail += halves(more_ref[h : h + 1, :])
    tail += [jnp.zeros((11, HALF), F32)]
    tail_ref[...] = jnp.concatenate(tail, axis=0).astype(BF)
    for ref in low_hbms:
        for i in range(4):
            mover.put(tail_ref.at[pl.ds(16 * (i % 2), 16), :], ref.at[i, pl.ds(96, 16), :])
    mover.finish()
    for k in range(4):
        wait_all(high_copies(0, k))


def qkv_grad_call(place, near, kept, ids, more):
    return whole_call(
        qkv_grad_kernel, "qkv_grad",
        [((4, 112, HALF), BF)] * 4 + [((4, 96, HALF), BF)] * 4 + [((TOK, WIDTH), F32), ((TOK, WIDTH), BF)],
        place, [*near, *kept, ids, more],
        scratch=[
            pltpu.VMEM((CHIP_TOK, WIDTH), F32), pltpu.VMEM((TOK, WIDTH), BF),
            pltpu.VMEM((4, WIDTH, HALF), BF), pltpu.VMEM((32, HALF), BF),
            pltpu.VMEM((2, CHIP_TOK, HALF), F32), pltpu.VMEM((4 * TOK, 1), F32),
            pltpu.VMEM((1, 4 * TOK), F32), pltpu.VMEM((2, WIDTH), F32), pltpu.SemaphoreType.DMA((48,)),
            pltpu.SemaphoreType.DMA((4, 4)),
        ],
        flops=3 * 10**9, vmem=20, far=tuple(range(10)), away=(14, 15),
    )


def total_of(refs):
    total = refs[0][...].astype(F32)
    for ref in refs[1:]:
        total = total + ref[...].astype(F32)
    return total.astype(BF)


def mid_kernel(place_ref, *refs):
    sources, out_low, out_high = refs[:13], refs[13:17], refs[17:21]
    low_ref, high_ref, mlp_ref, rest_ref, sems = refs[21:]
    targets = [r.at[i] for r in (low_ref, high_ref, mlp_ref) for i in range(4)] + [rest_ref]
    copies = Mover(sems).load(tuple(zip(sources, targets)))
    x, y = place_ref[4], place_ref[1]

    def total(ref):
        value = ref[0].astype(F32)
        for i in range(1, 4):
            value = value + ref[i].astype(F32)
        ref[0] = value.astype(BF)

    for i, ref in enumerate((low_ref, high_ref, mlp_ref)):
        wait_all(copies[4 * i : 4 * i + 4])
        total(ref)
    copies[12].wait()
    for k in range(4):
        to_y, to_x = lax.bitwise_and(y + 4 - k, 3), lax.bitwise_and(x + 4 - k, 3)
        out_low[k][:96, :WIDTH] = mlp_ref[0, to_y]
        out_low[k][:96, WIDTH:] = low_ref[0, to_y, :96, :]
        for i in range(3):
            first = 96 + 8 * (i % 2)
            out_low[k][96:, HALF * i : HALF * i + HALF] = low_ref[0, i // 2, first : first + 8, :]
        out_high[k][:, :WIDTH] = rest_ref[to_x]
        out_high[k][:, WIDTH:] = high_ref[0, to_x]


def join_kernel(core_ref, *refs):
    low, high, out_ref = total_of(refs[:4]), total_of(refs[4:8]), refs[8]
    for i in range(8):
        part = (low, high)[i // 4]
        out_ref[i, :24, :] = part[24 * (i % 4) : 24 * (i % 4) + 24]
        out_ref[i, 24:, :] = low[96:]


def total_kernel(core_ref, in_ref, out_ref):
    total = in_ref[0].astype(F32)
    for i in range(1, 8):
        total = total + in_ref[i].astype(F32)
    out_ref[...] = total.astype(BF)


def share_kernel(place_ref, own_ref, got_ref, out_ref):
    core, y = place_ref[0], place_ref[1]
    own, got = own_ref[...].astype(F32), got_ref[...].astype(F32)
    own_rows = pick(core, own[:12], own[12:24])
    got_rows = pick(core, got[:12], got[12:24])
    both = jnp.concatenate([pick(core, own_rows, got_rows), pick(core, got_rows, own_rows)], axis=0)
    out_ref[:24, WIDTH:] = both[:, WIDTH:].astype(BF)
    out_ref[:24, :WIDTH] = jnp.where(y < 2, both[:, :WIDTH], own[:24, :WIDTH]).astype(BF)
    out_ref[24:32, :] = pick(core, own[24:], got[24:]).astype(BF)
    out_ref[32:, :] = pick(core, got[24:], own[24:]).astype(BF)


def last_kernel(
    place_ref, part0_ref, part1_ref, part2_ref, part3_ref,
    qkv_ref, out_ref, up_ref, down_ref, *refs,
):
    small_refs, freq_ref, scr_ref = refs[:8], refs[8], refs[9]
    core, y, chip = place_ref[0], place_ref[1], place_ref[2]
    device = (2 * chip + core).astype(F32)
    for i, ref in enumerate((part0_ref, part1_ref, part2_ref, part3_ref)):
        scr_ref[i] = ref[...].astype(F32)
    ups = []
    for q in range(4):
        rows = scr_ref[lax.bitwise_and(q + 4 - y, 3)]
        for c in range(2):
            cols = rows[12 * c : 12 * c + 12, WIDTH:]
            if q < 3:
                qkv_ref[:, WIDTH * q + HALF * c : WIDTH * q + HALF * c + HALF] = cols
            else:
                out_ref[:, HALF * c : HALF * c + HALF] = cols
            if q < 2:
                ups.append((c, q, rows[12 * c : 12 * c + 12, :WIDTH]))
        if q > 1:
            down_ref[24 * (q - 2) : 24 * (q - 2) + 24, :] = rows[:24, :WIDTH]
    group, inner = split_index(lax.broadcasted_iota(jnp.int32, (HALF, 1), 0).astype(F32), 24)
    col = lax.broadcasted_iota(jnp.int32, (HALF, 4 * HALF), 1).astype(F32)
    spread_out = jnp.where(col == 96.0 * group + inner, 1.0, 0.0).astype(BF)
    stack = jnp.concatenate(
        [jnp.concatenate([piece, jnp.zeros((4, WIDTH), F32)], axis=0) for _, _, piece in ups], axis=0
    ).astype(BF)
    for g in range(2):
        parts = dot(stack[:, HALF * g : HALF * g + HALF], spread_out)
        total = parts[:12]
        for i, (c, q, _) in enumerate(ups):
            if i:
                total = total + pltpu.roll(parts[16 * i : 16 * i + 16], 48 * c + 24 * q, 1)[:12]
        up_ref[:, 4 * HALF * g : 4 * HALF * g + 4 * HALF] = total
    rows = scr_ref[lax.bitwise_and(7 - y, 3)]
    tails = [
        jnp.concatenate(
            [rows[24 + 8 * c : 32 + 8 * c, HALF * k : HALF * k + HALF] for k in range(3)], axis=0
        ).astype(BF)
        for c in range(2)
    ]
    sub = lax.broadcasted_iota(jnp.int32, (HALF, 128), 0).astype(F32)
    lane = lax.broadcasted_iota(jnp.int32, (HALF, 128), 1).astype(F32)

    def take(tail, want, limit):
        hot = jnp.where(jnp.logical_and(sub == want, lane < limit), 1.0, 0.0).astype(BF)
        return dot(tail, hot)

    entry = 12.0 * device + lane
    low = sum(take(tail, entry, 12) for tail in tails)
    high = sum(take(tail, entry - HALF, 12) for tail in tails)
    rows = [low[3 + i : 4 + i] + high[4 + i : 5 + i] for i in (0, 2, 6, 8, 10, 12)]
    entry = 36.0 * device + lane
    bias = 0.0
    for t in range(3):
        for c in range(2):
            bias = bias + take(tails[c], entry - (WIDTH * t + HALF * c), 36)[t : t + 1]
    rows.append(bias)
    own = pick(core, tails[0], tails[1])
    entry = 24.0 * chip.astype(F32) + lane
    bias = 0.0
    for h in range(2):
        shifted = entry - 24.0 * h
        fits = jnp.logical_and(lane >= 24.0 * h, lane < 24.0 * h + 24.0)
        for k in range(2):
            want = jnp.where(fits, shifted - HALF * k, -1.0)
            bias = bias + take(own, want, 48)[17 + 2 * h + k : 18 + 2 * h + k]
    rows.append(bias)
    side = jnp.where(chip < 16, 0.0, 1.0)
    source = jnp.where(chip < 16, tails[0], tails[1])
    head, inner = split_index(6.0 * device + lane - 192.0 * side, 32)
    freq = take(source, 64.0 * head + inner, 6)
    freq_ref[...] = freq[7:9, :6]
    for ref, row in zip(small_refs, rows):
        ref[...] = row[0, : ref.shape[0]]


def per_device(
    tokens, image_ids, patch_row, patch_col, cotangent,
    norm1_gain, norm1_bias, qkv_weight, qkv_bias, frequencies, out_weight, out_bias,
    norm2_gain, norm2_bias, up_weight, up_bias, down_weight, down_bias,
):
    x, y, z, core = (lax.axis_index(a) for a in ("x", "y", "z", "c"))
    place = jnp.stack([core, y, x * NZ + z, z, x]).astype(jnp.int32)
    chip = x * NZ + z
    core_arr = core.reshape(1).astype(jnp.int32)

    groups = [norm1_gain, norm1_bias, out_bias, norm2_gain, norm2_bias, down_bias, qkv_bias, up_bias]
    small = jnp.concatenate(groups + [frequencies[0], frequencies[1], jnp.zeros((216,), BF)])[None]
    pieces = []
    for c in range(2):
        cols = [qkv_weight[:, WIDTH * i + HALF * c : WIDTH * i + HALF * c + HALF] for i in range(3)]
        cols.append(out_weight[:, HALF * c : HALF * c + HALF])
        piece = cols[3]
        for i in range(3):
            piece = jnp.where(y == i, cols[i], piece)
        pieces.append(jnp.concatenate([piece, small, jnp.zeros((3, HALF), BF)], axis=0))
    block = jnp.broadcast_to(jnp.stack(pieces)[None], (NZ, 2, 16, HALF)).reshape(256, HALF)
    up_split = up_weight.reshape(12, 32, 2, 2, 24)
    up_halves = [up_split[:, :, c].transpose(0, 2, 1, 3).reshape(12, FF_HALF) for c in range(2)]
    up_own = jnp.where(core == 0, up_halves[0], up_halves[1])
    up_other = jnp.where(core == 0, up_halves[1], up_halves[0])
    up_pack = in_core_order(core, up_own, swap(up_other))
    mlp_pack = jnp.concatenate([up_pack, down_weight[:24], down_weight[24:]], axis=1)

    f = ("x", "z", "c")
    onward = [(i, i + 1) for i in range(2 * NX * NZ - 1)]
    backward = [(b, a) for a, b in onward]
    spots = jnp.stack([patch_row[0], patch_col[0]], axis=1).astype(BF)
    own = jnp.concatenate([tokens[0], jnp.pad(spots, ((0, 0), (0, 126)))], axis=1)
    lower, upper = lax.ppermute(own, f, onward), lax.ppermute(own, f, backward)
    near = lax.dynamic_slice_in_dim(jnp.pad(image_ids[0] + 1, (TOK, TOK)), chip * CHIP_TOK, 4 * TOK, 0)
    ids = near[None].astype(F32)

    mlp = lax.all_gather(mlp_pack, ("x", "z"), axis=0, tiled=True)
    block = lax.all_to_all(block, ("z", "c"), split_axis=0, concat_axis=0, tiled=True)
    block = block.reshape(16, 16, HALF)
    rows, lines = block[:, :12].reshape(192, HALF), block[:, 12]
    low = jnp.concatenate([rows[:96], lines[:8]], axis=0)
    high = jnp.concatenate([rows[96:], lines[8:]], axis=0)
    low = jnp.stack(around_axis(low, "x", NX))
    high = jnp.stack(around_axis(high, "y", NY))
    low, high, lower, upper, dy_own = lax.optimization_barrier((low, high, lower, upper, cotangent[0]))
    edge = jnp.where(core == 0, lower, upper)
    far = swap(edge)
    sources = [own, lower, upper, far]
    dy_other = swap(dy_own)
    by_y = around_axis(low, "y", NY)
    by_x = around_axis(high, "x", NX)

    wide, half, square = ((CHIP_TOK, WIDTH), BF), ((CHIP_TOK, HALF), BF), ((HALF, HALF), BF)
    ids, *parts = lax.optimization_barrier((ids, *by_y, *by_x))
    q, k, v, keep, send, *kept = qkv_call(place, sources, parts[:4], parts[4:])
    q_kept, k_kept, v_kept, vec, a1, turn, weights, inputs = kept
    got = swap(send)
    branch, o, lse, out_rows = attend(core_arr, q, k, v, ids, keep, got)

    da2, high, middle, result, result_send, du_sums, *lows = mlp_call(
        place, branch, swap(branch), inputs, vec, mlp, dy_own, dy_other
    )
    output = (result + swap(result_send).astype(F32)).astype(BF)[None]
    mlp_high = scatter_sum(high, "y").reshape(4, 96, WIDTH)
    mlp_lows = [fetch(part, "x", NX, k) for k, part in enumerate(lows)]

    do, delta, to_prev, to_next, out_own, out_send, sums, dmid = whole_call(
        branch_kernel, "branch",
        [((CHIP_TOK, HALF), BF), ((3, 2, CHIP_TOK), F32), ((288, HALF), BF), ((288, HALF), BF),
         ((HALF, HALF), BF), ((HALF, HALF), BF), ((4, WIDTH), F32), ((TOK, WIDTH), F32)],
        core_arr, [da2, swap(da2), middle, dy_own, dy_other, vec, o, out_rows, lse],
        scratch=[
            pltpu.VMEM((CHIP_TOK, WIDTH), F32), pltpu.VMEM((CHIP_TOK, WIDTH), F32),
            pltpu.VMEM((CHIP_TOK, WIDTH), BF), pltpu.VMEM((8, WIDTH), F32), pltpu.VMEM((CHIP_TOK, HALF), BF),
            pltpu.VMEM((HALF, WIDTH), BF), pltpu.VMEM((3, 2, CHIP_TOK), F32), pltpu.SemaphoreType.DMA((8,)),
        ],
        flops=10**9, vmem=16, far=(7,), away=tuple(range(2, 9)),
    )
    up_list = [(i, i + 1) for i in range(NX * NZ - 1)]
    down_list = [(b, a) for a, b in up_list]
    from_prev = lax.ppermute(to_next, ("x", "z"), up_list)
    from_next = lax.ppermute(to_prev, ("x", "z"), down_list)
    dq, dkv, *kept = near_back(
        core_arr, [q_kept, k_kept, v_kept, turn, a1, inputs, weights], do, lse, delta, ids
    )
    *parts, da1_own, da1_send = qkv_grad_call(
        place, [dq, dkv, from_prev, from_next, out_own, swap(out_send), sums], kept, ids, du_sums
    )
    lows = [fetch(part, "x", NX, k) for k, part in enumerate(parts[:4])]
    highs = [fetch(part, "y", NY, k) for k, part in enumerate(parts[4:])]
    da1 = da1_own + swap(da1_send).astype(F32)
    unit, scale = centred(tokens[0].astype(F32))
    input_grad = (centred_back(unit, scale, da1 * vec[0]) + dmid)[None]

    seconds = whole_call(
        mid_kernel, "mid", [((104, 3 * HALF), BF)] * 4 + [((96, 3 * HALF), BF)] * 4, place,
        [*lows, *highs, *mlp_lows, mlp_high],
        scratch=[
            pltpu.VMEM((4, 4, 112, HALF), BF), pltpu.VMEM((4, 4, 96, HALF), BF),
            pltpu.VMEM((4, 4, 96, WIDTH), BF), pltpu.VMEM((4, 96, WIDTH), BF),
            pltpu.SemaphoreType.DMA((16,)),
        ],
        vmem=16, away=tuple(range(13)),
    )
    lows = [fetch(part, "y", NY, k) for k, part in enumerate(seconds[:4])]
    highs = [fetch(part, "x", NX, k) for k, part in enumerate(seconds[4:])]
    (joined,) = whole_call(
        join_kernel, "join", [((8, 32, 3 * HALF), BF)], core_arr, lows + highs
    )
    joined = lax.all_to_all(
        joined.reshape(256, 3 * HALF), "z", split_axis=0, concat_axis=0, tiled=True
    )
    (mine,) = whole_call(
        total_kernel, "total", [((32, 3 * HALF), BF)],
        core_arr, [joined.reshape(8, 32, 3 * HALF)],
    )
    (part,) = whole_call(
        share_kernel, "share", [((40, 3 * HALF), BF)], place, [mine, swap(mine)]
    )
    parts = [fetch(part, "y", NY, k) for k in range(NY)]
    qkv_grad, out_weight_grad, up_grad, down_grad, *smalls, freq_grad = whole_call(
        last_kernel, "last",
        [((12, 3 * WIDTH), F32), ((12, WIDTH), F32), ((12, 4 * WIDTH), F32), ((48, WIDTH), F32)]
        + [((size,), F32) for size in (12, 12, 12, 12, 12, 12, 36, 48)]
        + [((2, 6), F32)],
        place, parts, scratch=[pltpu.VMEM((4, 40, 3 * HALF), F32)],
    )
    qkv_bias_grad, up_bias_grad = smalls[6:]
    return (
        output, input_grad,
        smalls[0], smalls[1], qkv_grad, qkv_bias_grad, freq_grad, out_weight_grad, smalls[2],
        smalls[3], smalls[4], up_grad, up_bias_grad, down_grad, smalls[5],
    )


def solution(mesh):
    fine = Mesh(mesh.devices.reshape(NY, NX, NZ, 2), ("y", "x", "z", "c"))
    f = ("x", "z", "c")
    return jax.shard_map(
        per_device,
        mesh=fine,
        in_specs=(
            P("y", f, None), P("y", None), P("y", f), P("y", f), P("y", f, None),
            P(f), P(f), P(f, None), P(f), P(None, f), P(f, None), P(f),
            P(f), P(f), P(f, None), P(f), P(f, None), P(f),
        ),
        out_specs=(
            P("y", f, None), P("y", f, None),
            P(f), P(f), P(f, None), P(f), P(None, f), P(f, None), P(f),
            P(f), P(f), P(f, None), P(f), P(f, None), P(f),
        ),
        check_vma=False,
    )
```

```python
import jax
import jax.numpy as jnp
from jax import lax
from jax.experimental import pallas as pl
from jax.experimental.pallas import tpu as pltpu
from jax.sharding import Mesh, PartitionSpec as P

NX, NY, NZ = 4, 4, 8
HEADS = 12
LOCAL_HEADS = 6
WIDTH = 768
HALF = 384
FF_HALF = 1536
TOK = 256
CHIP_TOK = 512
MASKED = -1e30
BF = jnp.bfloat16
F32 = jnp.float32
MIB = 1 << 20
OWN = slice(TOK, 3 * TOK)


def fetch(value, axis, size, step):
    if step == 0:
        return value
    return lax.ppermute(value, axis, [((i + step) % size, i) for i in range(size)])


def swap(value):
    return lax.ppermute(value, "c", [(0, 1), (1, 0)])


def in_core_order(core, own, other):
    first = jnp.where(core == 0, own, other)
    second = jnp.where(core == 0, other, own)
    return jnp.concatenate([first, second], axis=0)


def dot(a, b):
    return jnp.dot(a, b, preferred_element_type=F32)


def dot_nt(a, b):
    return lax.dot_general(a, b, (((1,), (1,)), ((), ())), preferred_element_type=F32)


def dot_tn(a, b):
    return lax.dot_general(a, b, (((0,), (0,)), ((), ())), preferred_element_type=F32)


def around_axis(block, axis, size):
    return [fetch(block, axis, size, k) for k in range(size)]


def scatter_sum(blocks, axis):
    count, rows, cols = blocks.shape
    return lax.psum_scatter(
        blocks.reshape(count * rows, cols), axis, scatter_dimension=0, tiled=True
    )


def whole_call(kernel, name, outs, scalars, arrays, scratch=(), flops=0, vmem=10, far=(), away=()):
    size = sum(v.size * v.dtype.itemsize for v in arrays)
    spec = lambda remote: pl.BlockSpec(memory_space=pl.ANY if remote else pltpu.VMEM)
    shapes = [(pltpu.HBM if i in far else jax.ShapeDtypeStruct)(*o) for i, o in enumerate(outs)]
    return pl.pallas_call(
        kernel,
        out_shape=shapes,
        in_specs=[pl.BlockSpec(memory_space=pltpu.SMEM)]
        + [spec(i in away) for i in range(len(arrays))],
        out_specs=[spec(i in far) for i in range(len(outs))],
        scratch_shapes=list(scratch),
        compiler_params=pltpu.CompilerParams(vmem_limit_bytes=vmem * MIB),
        cost_estimate=pl.CostEstimate(flops=flops, bytes_accessed=size, transcendentals=0),
        name=name,
    )(
        scalars,
        *[
            pltpu.with_memory_space_constraint(v, pltpu.HBM) if i in away else v
            for i, v in enumerate(arrays)
        ],
    )


class Mover:
    def __init__(self, sems):
        self.sems, self.count, self.open = sems, 0, []

    def start(self, source, target):
        copy = pltpu.make_async_copy(source, target, self.sems.at[self.count])
        self.count += 1
        copy.start()
        return copy

    def load(self, pairs):
        return [self.start(source, target) for source, target in pairs]

    def put(self, source, target):
        self.open.append(self.start(source, target))

    def finish(self):
        for copy in self.open:
            copy.wait()


def wait_all(copies):
    for copy in copies:
        copy.wait()


def id_columns(row_ref):
    return jnp.transpose(jnp.broadcast_to(row_ref[...], (8, 4 * TOK)))[:, :1]


def two_heads(block):
    lane = lax.broadcasted_iota(jnp.int32, block.shape, 1)
    zero = jnp.zeros_like(block)
    return jnp.concatenate(
        [jnp.where(lane < 64, block, zero), jnp.where(lane < 64, zero, block)], axis=0
    )


def by_head(first, second):
    row = lax.broadcasted_iota(jnp.int32, first.shape, 0)
    return jnp.where(row < 64, first, second)


def scaled(block):
    return block * jnp.asarray(0.125, BF)


def pair_of(i):
    return pl.ds(pl.multiple_of(128 * i, 128), 128)


def attend_kernel(
    core_ref, q_ref, k_ref, v_ref, keep_ref, got_ref, id_hbm,
    part_ref, o_hbm, lse_hbm, w_hbm, o_ref, lse_ref, w_ref, id_ref, kid_ref, sems,
):
    mover = Mover(sems)
    mover.start(id_hbm, id_ref).wait()
    w_ref[:, :HALF] = pick(core_ref[0], keep_ref[...], got_ref[...])
    w_ref[:, HALF:] = pick(core_ref[0], got_ref[...], keep_ref[...])
    mover.put(w_ref, w_hbm)
    kid_ref[...] = id_columns(id_ref)

    def body(i, carry):
        pair = pair_of(i)
        v_turned = jnp.transpose(v_ref[:, pair])
        for tile in range(2):
            near = slice(TOK * tile, TOK * tile + 3 * TOK)
            mine = slice(TOK * tile + TOK, TOK * tile + 2 * TOK)
            here = slice(TOK * tile, TOK * tile + TOK)
            keep = kid_ref[near, :] == id_ref[0:1, mine]
            scores = dot_nt(k_ref[near, pair], two_heads(scaled(q_ref[mine, pair])))
            halves = []
            for h in range(2):
                s = jnp.where(keep, scores[:, TOK * h : TOK * h + TOK], MASKED)
                top = jnp.max(s, axis=0, keepdims=True)
                expo = jnp.exp(s - top)
                total = jnp.sum(expo, axis=0, keepdims=True)
                lse_ref[i, h : h + 1, here] = top + jnp.log(total)
                p = (expo * (1.0 / total)).astype(BF)
                halves.append(dot(v_turned[:, near], p))
            o_ref[here, pair] = jnp.transpose(by_head(*halves)).astype(BF)
        return carry

    lax.fori_loop(0, 3, body, 0)
    mover.put(o_ref, o_hbm)
    mover.put(lse_ref, lse_hbm)
    part_ref[...] = dot(o_ref[...], w_ref[...]).astype(BF)
    mover.finish()


def attend(core, q, k, v, ids, keep, got):
    o, lse, weights = ((CHIP_TOK, HALF), BF), ((3, 2, CHIP_TOK), F32), ((HALF, WIDTH), BF)
    return whole_call(
        attend_kernel, "attend", [((CHIP_TOK, WIDTH), BF), o, lse, weights],
        core, [q, k, v, keep, got, ids],
        scratch=[
            pltpu.VMEM(*o), pltpu.VMEM(*lse), pltpu.VMEM(*weights),
            pltpu.VMEM((1, 4 * TOK), F32), pltpu.VMEM((4 * TOK, 1), F32), pltpu.SemaphoreType.DMA((8,)),
        ],
        flops=3 * 10**9, vmem=12, far=(1, 2, 3), away=(5,),
    )


def pair_grads(k, v, q2, do2, keep, lses, deltas):
    scores = dot_nt(k, q2)
    dprobs = dot_nt(v, do2)
    probs, dscores = [], []
    for h in range(2):
        lanes = slice(TOK * h, TOK * h + TOK)
        p = jnp.exp(jnp.where(keep, scores[:, lanes], MASKED) - lses[h])
        dscores.append((p * (dprobs[:, lanes] - deltas[h])).astype(BF))
        probs.append(p.astype(BF))
    return probs, dscores


def near_back_kernel(
    core_ref, q_hbm, k_hbm, v_hbm, turn_hbm, a1_hbm, x_hbm, w_hbm, lse_hbm, id_hbm, do_ref, delta_ref,
    dq_ref, dkv_ref, q_ref, k_ref, v_ref, turn_ref, a1_ref, x_ref, w_ref,
    lse_ref, id_ref, kid_ref, sems, more_sems,
):
    mover = Mover(more_sems)
    first_loads = mover.load(((id_hbm, id_ref), (lse_hbm, lse_ref)))
    sources = ((q_hbm, q_ref), (k_hbm, k_ref), (v_hbm, v_ref))

    def load(i):
        return [
            pltpu.make_async_copy(source.at[:, pair_of(i)], target.at[:, pair_of(i)], sems.at[i, j])
            for j, (source, target) in enumerate(sources)
        ]

    for i in range(3):
        for copy in load(i):
            copy.start()
    later = mover.load(
        ((turn_hbm, turn_ref), (a1_hbm, a1_ref), (w_hbm.at[pl.ds(0, 3)], w_ref), (x_hbm, x_ref))
    )
    wait_all(first_loads)
    kid_ref[...] = id_columns(id_ref)

    def body(i, carry):
        pair = pair_of(i)
        wait_all(load(i))
        k_turned = jnp.transpose(k_ref[:, pair])
        for tile in range(2):
            near = slice(TOK * tile, TOK * tile + 3 * TOK)
            mine = slice(TOK * tile + TOK, TOK * tile + 2 * TOK)
            here = slice(TOK * tile, TOK * tile + TOK)
            k = k_ref[near, pair]
            q2 = two_heads(scaled(q_ref[mine, pair]))
            do2 = two_heads(do_ref[here, pair])
            keep = kid_ref[near, :] == id_ref[0:1, mine]
            probs, dscores = pair_grads(
                k, v_ref[near, pair], q2, do2, keep,
                [lse_ref[i, h : h + 1, here] for h in range(2)],
                [delta_ref[i, h : h + 1, here] for h in range(2)],
            )
            dq = by_head(*[dot(k_turned[:, near], ds) for ds in dscores])
            dq_ref[here, pair] = jnp.transpose(dq) * 0.125
            first = TOK * (1 - tile)
            own = slice(first, first + 2 * TOK)
            dk = dot(jnp.concatenate([d[own] for d in dscores], axis=1), q2)
            dv = dot(jnp.concatenate([p[own] for p in probs], axis=1), do2)
            for which, full in enumerate((dk, dv)):
                if tile == 0:
                    dkv_ref[which, :, pair] = full
                else:
                    dkv_ref[which, :, pair] += full
        return carry

    lax.fori_loop(0, 3, body, 0)
    wait_all(later)


def near_back(core, kept, grad, lse, delta, ids):
    around = ((4 * TOK, HALF), BF)
    return whole_call(
        near_back_kernel, "near_back",
        [
            ((CHIP_TOK, HALF), F32), ((2, CHIP_TOK, HALF), F32), around, around, around,
            ((2, CHIP_TOK, HALF), F32), ((CHIP_TOK, WIDTH), BF), ((CHIP_TOK, WIDTH + 128), BF),
            ((3, WIDTH, HALF), BF),
        ],
        core, [*kept, lse, ids, grad, delta], away=tuple(range(9)),
        scratch=[
            pltpu.VMEM((3, 2, CHIP_TOK), F32), pltpu.VMEM((1, 4 * TOK), F32),
            pltpu.VMEM((4 * TOK, 1), F32), pltpu.SemaphoreType.DMA((3, 3)), pltpu.SemaphoreType.DMA((8,)),
        ],
        flops=4 * 10**9, vmem=12,
    )


def far_back(q_ref, k_ref, v_ref, before_ref, after_ref, id_ref, kid_ref, dkv_ref, sum_ref):
    row = lax.broadcasted_iota(jnp.int32, (8, TOK), 0)

    def body(i, carry):
        pair = pair_of(i)
        for side, ref in enumerate((before_ref, after_ref)):
            keys = slice(TOK * (side + 1), TOK * (side + 2))
            queries = slice(3 * TOK * side, 3 * TOK * side + TOK)
            tail = ref[TOK:, :TOK].astype(F32)
            deltas = tail[0:8] + tail[8:16]
            lses = tail[16:24] + tail[24:32]
            choose = lambda v, h: jnp.sum(
                jnp.where(row == 2 * i + h, v, 0.0), axis=0, keepdims=True
            )
            q2 = two_heads(scaled(q_ref[queries, pair]))
            do2 = two_heads(ref[:TOK, pair])
            keep = kid_ref[keys, :] == id_ref[0:1, queries]
            probs, dscores = pair_grads(
                k_ref[keys, pair], v_ref[keys, pair], q2, do2, keep,
                [choose(lses, h) for h in range(2)], [choose(deltas, h) for h in range(2)],
            )
            rows = slice(TOK * side, TOK * side + TOK)
            dk = dot(jnp.concatenate(dscores, axis=1), q2)
            dv = dot(jnp.concatenate(probs, axis=1), do2)
            sum_ref[0, rows, pair] = dkv_ref[0, rows, pair] + dk
            sum_ref[1, rows, pair] = dkv_ref[1, rows, pair] + dv
        return carry

    lax.fori_loop(0, 3, body, 0)


def centred(value):
    shifted = value - jnp.mean(value, axis=-1, keepdims=True)
    spread = jnp.mean(shifted * shifted, axis=-1, keepdims=True)
    scale = lax.rsqrt(spread + 1e-06)
    return shifted * scale, scale


def centred_back(unit, scale, grad):
    mean = jnp.mean(grad, axis=-1, keepdims=True)
    along = jnp.mean(grad * unit, axis=-1, keepdims=True)
    return scale * (grad - mean - unit * along)


def lanes_of(width):
    return lax.broadcasted_iota(jnp.int32, (1, width), 1).astype(F32)


def pick(core, first, second):
    return jnp.where(core == 0, first, second)


def expand(lines, shift, lane_in, owner):
    width = lane_in.shape[1]
    moved = pltpu.roll(lines, (HALF - shift) % HALF, 1)[:, :128].astype(BF)
    sub = lax.broadcasted_iota(jnp.int32, (128, width), 0).astype(F32)
    table = dot(moved, jnp.where(sub == lane_in, 1.0, 0.0).astype(BF))
    sub = lax.broadcasted_iota(jnp.int32, (64, width), 0).astype(F32)
    return jnp.sum(jnp.where(sub == owner, table, 0.0), axis=0, keepdims=True)


def split_index(index, size):
    group = jnp.floor((index + 0.5) * (1.0 / size))
    return group, index - group * size


def low_half(shape):
    return lax.bitwise_and(lax.broadcasted_iota(jnp.int32, shape, 1), 63) < 32


def swap_halves(value):
    ahead = pltpu.roll(value, HALF - 32, 1)
    behind = pltpu.roll(value, 32, 1)
    return jnp.where(low_half(value.shape), ahead, behind)


def three_parts(value):
    parts = []
    for _ in range(3):
        part = value.astype(BF)
        parts.append(part)
        value = value - part.astype(F32)
    return jnp.concatenate(parts, axis=0)


def qkv_kernel(place_ref, *refs):
    by_y, by_x, sources, refs = refs[:4], refs[4:8], refs[8:12], refs[12:]
    q_ref, k_ref, v_ref, keep_ref, send_ref = refs[:5]
    q_hbm, k_hbm, v_hbm, vec_hbm, a1_hbm, turn_hbm, w_hbm, x_hbm = refs[5:13]
    table_ref, bias_ref, line_ref, x_ref, a1_ref, turn_ref, w_ref, vec_ref, sems, x_sems = refs[13:]
    core, x, y = place_ref[0], place_ref[4], place_ref[1]
    mover = Mover(sems)

    def x_load(step, source):
        return pltpu.make_async_copy(source, x_ref.at[pl.ds(TOK * step, TOK), :], x_sems.at[step])

    own, lower, upper, far = sources

    @pl.when(core == 0)
    def _():
        for step, source in enumerate((lower, own, upper, far)):
            x_load(step, source).start()

    @pl.when(core == 1)
    def _():
        for step, source in enumerate((far, lower, own, upper)):
            x_load(step, source).start()

    core_f = core.astype(F32)
    for ky in range(4):
        for kx in range(4):
            q = lax.bitwise_and(y + ky, 3)
            chip = lax.bitwise_and(x + kx, 3)
            low = pl.ds(pl.multiple_of(192 * chip, 96), 96)
            high = pl.ds(pl.multiple_of(192 * chip + 96, 96), 96)
            w_ref[q, low, :] = by_y[ky][kx, :96, :]
            w_ref[q, high, :] = by_x[kx][ky, :96, :]
    for kx in range(4):
        chip = lax.bitwise_and(x + kx, 3)
        low = pl.ds(pl.multiple_of(16 * chip, 8), 8)
        high = pl.ds(pl.multiple_of(16 * chip + 8, 8), 8)
        line_ref[low, :] = by_y[0][kx, 96:, :].astype(F32)
        line_ref[high, :] = by_x[kx][0, 96:, :].astype(F32)
    lines = line_ref[...]
    group, inner = split_index(lanes_of(WIDTH), 12)
    rows = [expand(lines, 12 * i, inner, group) for i in range(6)]
    group, inner = split_index(lanes_of(WIDTH), 24)
    rows += [expand(lines, 108 + 24 * h, inner, 2.0 * group + core_f) for h in range(2)]
    vec_ref[...] = jnp.concatenate(rows, axis=0)
    group, inner = split_index(lanes_of(3 * WIDTH), 36)
    bias = expand(lines, 72, inner, group)
    for i in range(3):
        bias_ref[i : i + 1, :] = pick(
            core,
            bias[:, WIDTH * i : WIDTH * i + HALF],
            bias[:, WIDTH * i + HALF : WIDTH * i + WIDTH],
        )
    lane = lanes_of(HALF)
    head, _ = split_index(lane, 64)
    _, inner = split_index(lane, 32)
    group, inner = split_index(192.0 * core_f + 32.0 * head + inner, 6)
    count = lax.broadcasted_iota(jnp.int32, (32, HALF), 0).astype(F32)
    for f in range(2):
        angle = count * expand(lines, 156 + 6 * f, inner, group)
        table_ref[f] = three_parts(jnp.concatenate([jnp.cos(angle), jnp.sin(angle)], axis=1))
    keep_ref[...] = w_ref[3, pl.ds(pl.multiple_of(HALF * core, HALF), HALF), :]
    send_ref[...] = w_ref[3, pl.ds(pl.multiple_of(HALF * (1 - core), HALF), HALF), :]
    mover.put(w_ref, w_hbm)
    mover.put(vec_ref, vec_hbm)
    for step in range(4):
        rows = slice(TOK * step, TOK * step + TOK)
        x_load(step, own).wait()
        spots = x_ref[rows, WIDTH:].astype(F32)
        spot = lax.bitwise_and(lax.broadcasted_iota(jnp.int32, (TOK, 96), 1), 31).astype(F32)
        tables = [
            dot(jnp.where(spots[:, f : f + 1] == spot, 1.0, 0.0).astype(BF), table_ref[f])
            for f in range(2)
        ]
        cos_r, sin_r = tables[0][:, :HALF], tables[0][:, HALF:]
        cos_c, sin_c = tables[1][:, :HALF], tables[1][:, HALF:]
        cosine = cos_r * cos_c - sin_r * sin_c
        sine = sin_r * cos_c + cos_r * sin_c
        sine = jnp.where(low_half(sine.shape), -sine, sine)
        unit, _ = centred(x_ref[rows, :WIDTH].astype(F32))
        a1 = (unit * vec_ref[0:1, :] + vec_ref[1:2, :]).astype(BF)
        if step in (1, 2):
            here = slice(TOK * (step - 1), TOK * step)
            turn_ref[0, here, :] = cosine
            turn_ref[1, here, :] = sine
            a1_ref[here, :] = a1
            if step == 2:
                mover.put(x_ref.at[pl.ds(TOK, CHIP_TOK), :], x_hbm)
                mover.put(turn_ref, turn_hbm)
                mover.put(a1_ref, a1_hbm)
        for i, ref in enumerate((q_ref, k_ref, v_ref)):
            part = dot(a1, w_ref[i]) + bias_ref[i : i + 1, :]
            if i < 2:
                part = part * cosine + swap_halves(part) * sine
            ref[rows, :] = part.astype(BF)
            mover.put(ref.at[pl.ds(TOK * step, TOK), :], (q_hbm, k_hbm, v_hbm)[i].at[pl.ds(TOK * step, TOK), :])
    mover.finish()


def qkv_call(place, sources, by_y, by_x):
    around, square = ((4 * TOK, HALF), BF), ((HALF, HALF), BF)
    wide, turn = ((CHIP_TOK, WIDTH), BF), ((2, CHIP_TOK, HALF), F32)
    vec, full = ((8, WIDTH), F32), ((4, WIDTH, HALF), BF)
    return whole_call(
        qkv_kernel, "qkv",
        [around, around, around, square, square, around, around, around, vec, wide, turn, full]
        + [((CHIP_TOK, WIDTH + 128), BF)],
        place, [*by_y, *by_x, *sources],
        scratch=[
            pltpu.VMEM((2, 96, WIDTH), BF), pltpu.VMEM((8, HALF), F32), pltpu.VMEM((64, HALF), F32),
            pltpu.VMEM((4 * TOK, WIDTH + 128), BF), pltpu.VMEM(*wide), pltpu.VMEM(*turn),
            pltpu.VMEM(*full), pltpu.VMEM(*vec), pltpu.SemaphoreType.DMA((24,)),
            pltpu.SemaphoreType.DMA((4,)),
        ],
        flops=2 * 10**9, vmem=18, far=tuple(range(5, 13)), away=tuple(range(8, 12)),
    )


def norm_kernel(core_ref, part_ref, got_ref, x_hbm, vec_hbm, a2_ref, mid_hbm, x_ref, vec_ref, mid_ref, sems):
    mover = Mover(sems)
    wait_all(mover.load(((x_hbm.at[:, pl.ds(0, WIDTH)], x_ref), (vec_hbm, vec_ref))))
    middle = x_ref[...].astype(F32) + (
        part_ref[...].astype(F32) + got_ref[...].astype(F32) + vec_ref[2:3, :]
    )
    mid_ref[...] = middle
    mover.put(mid_ref, mid_hbm)
    unit, _ = centred(middle)
    a2_ref[...] = (unit * vec_ref[3:4, :] + vec_ref[4:5, :]).astype(BF)
    mover.finish()


def mlp_kernel(
    place_ref, a2_ref, vec_hbm, w_hbm, dya_hbm, dyb_hbm, mid_hbm, o_hbm, wo_hbm, lse_hbm,
    da2_ref, mid_ref, dy_ref, vec_ref, o_ref, wo_ref, lse_ref, high_hbm, own_hbm, send_hbm, sums_hbm, *refs,
):
    low_hbms = refs[:4]
    acc_ref, grads_ref, w_ref, own_ref, send_ref, sums_ref, act_ref, du_ref, sems = refs[4:]
    core, x = place_ref[0], place_ref[4]
    own = pl.ds(pl.multiple_of(core * TOK, TOK), TOK)
    rest = pl.ds(pl.multiple_of((1 - core) * TOK, TOK), TOK)
    mover = Mover(sems)
    load_vec = mover.start(vec_hbm, vec_ref)
    loads = []
    for i in (0, 2, 1, 3):
        cols = pl.ds(WIDTH * i, WIDTH)
        loads.append(mover.start(w_hbm.at[:, cols], w_ref.at[:, cols]))
        if i == 0:
            load_dy = mover.load(((dya_hbm, dy_ref.at[own, :]), (dyb_hbm, dy_ref.at[rest, :])))

    def put(index, value):
        grads_ref[index] = value.astype(BF)
        for k, ref in enumerate(low_hbms):
            row = pl.multiple_of(192 * lax.bitwise_and(x + 4 - k, 3), 96)
            mover.put(grads_ref.at[index, pl.ds(row, 96), :], ref.at[index])
        for j in range(4):
            rows = pl.ds(192 * j + 96, 96)
            mover.put(grads_ref.at[index, rows, :], high_hbm.at[index, pl.ds(96 * j, 96), :])

    load_vec.wait()
    a2 = a2_ref[...]
    a2_turned = jnp.transpose(a2)
    da2 = None
    for h in range(2):
        lanes = slice(WIDTH * h, WIDTH * h + WIDTH)
        loads[2 * h].wait()
        loads[2 * h + 1].wait()
        if h == 0:
            wait_all(load_dy)
            later = mover.load(((mid_hbm, mid_ref), (o_hbm, o_ref), (wo_hbm, wo_ref), (lse_hbm, lse_ref)))
        dy = dy_ref[...]
        up = w_ref[:, lanes]
        down = w_ref[:, FF_HALF + WIDTH * h : FF_HALF + WIDTH * h + WIDTH]
        for j in range(3):
            cols = slice(TOK * j, TOK * j + TOK)
            u = dot(a2, up[:, cols]) + vec_ref[6 + h : 7 + h, cols]
            gate = 0.5 * (1.0 + lax.erf(u * 0.7071067811865476))
            act_ref[:, cols] = (u * gate).astype(BF)
            slope = gate + u * jnp.exp(-0.5 * u * u) * 0.3989422804014327
            low = (slope * dot_nt(dy, down[cols, :])).astype(BF)
            du_ref[:, cols] = low
            sums_ref[h : h + 1, cols] = jnp.sum(low.astype(F32), axis=0, keepdims=True)
        act, du = act_ref[...], du_ref[...]
        put(2 + h, dot_tn(act, dy))
        put(h, dot(a2_turned, du))
        term = dot(act, down)
        if h == 0:
            acc_ref[...] = term
        else:
            acc_ref[...] += term
        term = dot_nt(du, up)
        da2 = term if da2 is None else da2 + term
    da2_ref[...] = da2.astype(BF)
    mover.put(sums_ref, sums_hbm)
    wait_all(later)
    own_ref[...] = acc_ref[own, :] + mid_ref[own, :] + vec_ref[5:6, :]
    send_ref[...] = acc_ref[rest, :].astype(BF)
    mover.put(own_ref, own_hbm)
    mover.put(send_ref, send_hbm)
    mover.finish()


def norm_call(core, branch, got, inputs, vec):
    full = (CHIP_TOK, WIDTH)
    return whole_call(
        norm_kernel, "norm", [(full, BF), (full, F32)], core, [branch, got, inputs, vec],
        scratch=[
            pltpu.VMEM(full, BF), pltpu.VMEM((8, WIDTH), F32), pltpu.VMEM(full, F32),
            pltpu.SemaphoreType.DMA((4,)),
        ],
        vmem=12, far=(1,), away=(2, 3),
    )


def mlp_call(place, a2, vec, weights, dy_own, dy_other, middle, o, out_rows, lse):
    full, half = (CHIP_TOK, WIDTH), (TOK, WIDTH)
    return whole_call(
        mlp_kernel, "mlp",
        [
            (full, BF), (full, F32), (full, BF), ((8, WIDTH), F32), ((CHIP_TOK, HALF), BF),
            ((HALF, WIDTH), BF), ((3, 2, CHIP_TOK), F32), ((4, HALF, WIDTH), BF), (half, F32), (half, BF),
            ((2, WIDTH), F32),
        ]
        + [((4, 96, WIDTH), BF)] * 4,
        place, [a2, vec, weights, dy_own, dy_other, middle, o, out_rows, lse],
        scratch=[
            pltpu.VMEM(full, F32), pltpu.VMEM((4, WIDTH, WIDTH), BF), pltpu.VMEM((WIDTH, 4 * WIDTH), BF),
            pltpu.VMEM(half, F32), pltpu.VMEM(half, BF), pltpu.VMEM((2, WIDTH), F32),
            pltpu.VMEM(full, BF), pltpu.VMEM(full, BF), pltpu.SemaphoreType.DMA((56,)),
        ],
        flops=8 * 10**9, vmem=30, far=tuple(range(7, 15)), away=tuple(range(1, 9)),
    )


def branch_kernel(
    core_ref, da2_ref, got_ref, mid_ref, dy_ref, vec_ref, o_ref, w_ref, lse_ref,
    do_ref, delta_ref, back_ref, on_ref, own_ref, send_ref, sums_ref, dmid_hbm, scr_ref, sems,
):
    core = core_ref[0]
    mover = Mover(sems)
    mine = pl.ds(pl.multiple_of(core * TOK, TOK), TOK)
    unit, scale = centred(mid_ref[...])
    da2 = da2_ref[...].astype(F32) + got_ref[...].astype(F32)
    dy = dy_ref[...].astype(F32)
    dmid = centred_back(unit, scale, da2 * vec_ref[3:4, :]) + dy
    low = dmid.astype(BF)
    scr_ref[...] = dmid
    mover.put(scr_ref.at[mine, :], dmid_hbm)
    do = dot_nt(low, w_ref[...]).astype(BF)
    do_ref[...] = do
    heads = lax.broadcasted_iota(jnp.int32, (8, HALF), 0)
    lane = lax.broadcasted_iota(jnp.int32, (8, HALF), 1)
    hot = jnp.where(jnp.logical_and(lane >= 64 * heads, lane < 64 * heads + 64), 1.0, 0.0)
    delta = lax.dot_general(
        hot, do.astype(F32) * o_ref[...].astype(F32), (((1,), (1,)), ((), ())),
        precision=lax.Precision.HIGHEST, preferred_element_type=F32,
    )
    for i in range(3):
        delta_ref[i] = delta[2 * i : 2 * i + 2]
    lse = jnp.concatenate([lse_ref[i] for i in range(3)] + [jnp.zeros((2, CHIP_TOK), F32)], axis=0)
    tail = []
    for value in (delta, lse):
        high = value.astype(BF)
        tail += [high, (value - high.astype(F32)).astype(BF)]
    tail = jnp.concatenate(tail, axis=0)
    for ref, rows in ((back_ref, slice(0, TOK)), (on_ref, slice(TOK, CHIP_TOK))):
        ref[:TOK, :] = do[rows]
        ref[TOK:, :] = jnp.concatenate([tail[:, rows], jnp.zeros((32, 128), BF)], axis=1)
    grad = dot_tn(o_ref[...], low).astype(BF)
    own_ref[...] = pick(core, grad[:, :HALF], grad[:, HALF:])
    send_ref[...] = pick(core, grad[:, HALF:], grad[:, :HALF])
    row = lax.broadcasted_iota(jnp.int32, (CHIP_TOK, 1), 0)
    here = jnp.logical_and(row >= core * TOK, row < core * TOK + TOK)
    total = lambda v: jnp.sum(jnp.where(here, v, 0.0), axis=0, keepdims=True)
    sums_ref[0:1, :] = total(low.astype(F32))
    sums_ref[1:2, :] = total(da2 * unit)
    sums_ref[2:3, :] = total(da2)
    sums_ref[3:4, :] = total(dy)
    mover.finish()


def qkv_grad_kernel(
    place_ref, dq_ref, near_ref, before_ref, after_ref, own_ref, got_ref, sums_ref,
    q_ref, k_ref, v_ref, turn_ref, a1_ref, x_ref, w_ref, id_hbm, more_hbm,
    *refs,
):
    low_hbms, high_hbms, da1_own_hbm, da1_send_hbm = refs[:4], refs[4:8], refs[8], refs[9]
    da1_ref, da1_send_ref, full_ref, tail_ref, dkv_ref, kid_ref, id_ref, more_ref, sems, high_sems = refs[10:]
    core, x, y = place_ref[0], place_ref[4], place_ref[1]
    mover = Mover(sems)
    wait_all(mover.load(((id_hbm, id_ref), (more_hbm, more_ref))))
    kid_ref[...] = id_columns(id_ref)
    far_back(q_ref, k_ref, v_ref, before_ref, after_ref, id_ref, kid_ref, near_ref, dkv_ref)

    def high_copies(step, k):
        return [
            pltpu.make_async_copy(
                full_ref.at[step, pl.ds(192 * j + 96, 96), :], high_hbms[k].at[j], high_sems.at[k, j]
            )
            for j in range(4)
        ]

    def hand_out(step, full):
        full_ref[step] = full
        for k, ref in enumerate(low_hbms):
            row = pl.multiple_of(192 * lax.bitwise_and(x + 4 - k, 3), 96)
            mover.put(full_ref.at[step, pl.ds(row, 96), :], ref.at[step, pl.ds(0, 96), :])
        for k in range(4):

            @pl.when(lax.bitwise_and(y + 4 - k, 3) == step)
            def _():
                for copy in high_copies(step, k):
                    copy.start()

    tail = []
    angle = 0.0
    a1_turned = jnp.transpose(a1_ref[...])
    for step, grad in enumerate((dq_ref[...], dkv_ref[0], dkv_ref[1])):
        if step < 2:
            other = swap_halves(grad)
            turned = (q_ref, k_ref)[step][OWN, :].astype(F32)
            angle = angle + other * turned - grad * swap_halves(turned)
            grad = grad * turn_ref[0] - other * turn_ref[1]
        low = grad.astype(BF)
        tail.append(jnp.sum(low.astype(F32), axis=0, keepdims=True))
        hand_out(step, dot(a1_turned, low).astype(BF))
        term = dot_nt(low, w_ref[step])
        if step == 0:
            da1_ref[...] = term
        else:
            da1_ref[...] += term
    first = pick(core, own_ref[...], got_ref[...])
    second = pick(core, got_ref[...], own_ref[...])
    hand_out(3, jnp.concatenate([first, second], axis=0))
    da1 = da1_ref[...]
    mover.put(da1_ref.at[pl.ds(pl.multiple_of(core * TOK, TOK), TOK), :], da1_own_hbm)
    da1_send_ref[...] = da1_ref[pl.ds(pl.multiple_of((1 - core) * TOK, TOK), TOK), :].astype(BF)
    mover.put(da1_send_ref, da1_send_hbm)
    unit, _ = centred(x_ref[:, :WIDTH].astype(F32))
    spots = x_ref[:, WIDTH:].astype(F32)
    halves = lambda v: [v[:, :HALF], v[:, HALF:]]
    tail += halves(jnp.sum(da1 * unit, axis=0, keepdims=True))
    tail += halves(jnp.sum(da1, axis=0, keepdims=True))
    tail += [jnp.sum(angle * spots[:, f : f + 1], axis=0, keepdims=True) for f in range(2)]
    for i in range(4):
        tail += halves(sums_ref[i : i + 1, :])
    for h in range(2):
        tail += halves(more_ref[h : h + 1, :])
    tail += [jnp.zeros((11, HALF), F32)]
    tail_ref[...] = jnp.concatenate(tail, axis=0).astype(BF)
    for ref in low_hbms:
        for i in range(4):
            mover.put(tail_ref.at[pl.ds(16 * (i % 2), 16), :], ref.at[i, pl.ds(96, 16), :])
    mover.finish()
    for k in range(4):
        wait_all(high_copies(0, k))


def qkv_grad_call(place, near, kept, ids, more):
    return whole_call(
        qkv_grad_kernel, "qkv_grad",
        [((4, 112, HALF), BF)] * 4 + [((4, 96, HALF), BF)] * 4 + [((TOK, WIDTH), F32), ((TOK, WIDTH), BF)],
        place, [*near, *kept, ids, more],
        scratch=[
            pltpu.VMEM((CHIP_TOK, WIDTH), F32), pltpu.VMEM((TOK, WIDTH), BF),
            pltpu.VMEM((4, WIDTH, HALF), BF), pltpu.VMEM((32, HALF), BF),
            pltpu.VMEM((2, CHIP_TOK, HALF), F32), pltpu.VMEM((4 * TOK, 1), F32),
            pltpu.VMEM((1, 4 * TOK), F32), pltpu.VMEM((2, WIDTH), F32), pltpu.SemaphoreType.DMA((48,)),
            pltpu.SemaphoreType.DMA((4, 4)),
        ],
        flops=3 * 10**9, vmem=20, far=tuple(range(10)), away=(14, 15),
    )


def total_of(refs):
    total = refs[0][...].astype(F32)
    for ref in refs[1:]:
        total = total + ref[...].astype(F32)
    return total.astype(BF)


def mid_kernel(place_ref, *refs):
    sources, out_low, out_high = refs[:13], refs[13:17], refs[17:21]
    low_ref, high_ref, mlp_ref, rest_ref, sems = refs[21:]
    targets = [r.at[i] for r in (high_ref, low_ref, mlp_ref) for i in range(4)] + [rest_ref]
    copies = Mover(sems).load(tuple(zip(sources, targets)))
    x, y = place_ref[4], place_ref[1]

    def total(ref):
        value = ref[0].astype(F32)
        for i in range(1, 4):
            value = value + ref[i].astype(F32)
        ref[0] = value.astype(BF)

    for i, ref in enumerate((high_ref, low_ref, mlp_ref)):
        wait_all(copies[4 * i : 4 * i + 4])
        total(ref)
    copies[12].wait()
    for k in range(4):
        to_y, to_x = lax.bitwise_and(y + 4 - k, 3), lax.bitwise_and(x + 4 - k, 3)
        out_low[k][:96, :WIDTH] = mlp_ref[0, to_y]
        out_low[k][:96, WIDTH:] = low_ref[0, to_y, :96, :]
        for i in range(3):
            first = 96 + 8 * (i % 2)
            out_low[k][96:, HALF * i : HALF * i + HALF] = low_ref[0, i // 2, first : first + 8, :]
        out_high[k][:, :WIDTH] = rest_ref[to_x]
        out_high[k][:, WIDTH:] = high_ref[0, to_x]


def join_kernel(core_ref, *refs):
    low, high, out_ref = total_of(refs[:4]), total_of(refs[4:8]), refs[8]
    for i in range(8):
        part = (low, high)[i // 4]
        out_ref[i, :24, :] = part[24 * (i % 4) : 24 * (i % 4) + 24]
        out_ref[i, 24:, :] = low[96:]


def total_kernel(core_ref, in_ref, out_ref):
    total = in_ref[0].astype(F32)
    for i in range(1, 8):
        total = total + in_ref[i].astype(F32)
    out_ref[...] = total.astype(BF)


def share_kernel(place_ref, own_ref, got_ref, out_ref):
    core, y = place_ref[0], place_ref[1]
    own, got = own_ref[...].astype(F32), got_ref[...].astype(F32)
    own_rows = pick(core, own[:12], own[12:24])
    got_rows = pick(core, got[:12], got[12:24])
    both = jnp.concatenate([pick(core, own_rows, got_rows), pick(core, got_rows, own_rows)], axis=0)
    out_ref[:24, WIDTH:] = both[:, WIDTH:].astype(BF)
    out_ref[:24, :WIDTH] = jnp.where(y < 2, both[:, :WIDTH], own[:24, :WIDTH]).astype(BF)
    out_ref[24:32, :] = pick(core, own[24:], got[24:]).astype(BF)
    out_ref[32:, :] = pick(core, got[24:], own[24:]).astype(BF)


def last_kernel(
    place_ref, part0_ref, part1_ref, part2_ref, part3_ref,
    qkv_ref, out_ref, up_ref, down_ref, *refs,
):
    small_refs, freq_ref, scr_ref = refs[:8], refs[8], refs[9]
    core, y, chip = place_ref[0], place_ref[1], place_ref[2]
    device = (2 * chip + core).astype(F32)
    for i, ref in enumerate((part0_ref, part1_ref, part2_ref, part3_ref)):
        scr_ref[i] = ref[...].astype(F32)
    ups = []
    for q in range(4):
        rows = scr_ref[lax.bitwise_and(q + 4 - y, 3)]
        for c in range(2):
            cols = rows[12 * c : 12 * c + 12, WIDTH:]
            if q < 3:
                qkv_ref[:, WIDTH * q + HALF * c : WIDTH * q + HALF * c + HALF] = cols
            else:
                out_ref[:, HALF * c : HALF * c + HALF] = cols
            if q < 2:
                ups.append((c, q, rows[12 * c : 12 * c + 12, :WIDTH]))
        if q > 1:
            down_ref[24 * (q - 2) : 24 * (q - 2) + 24, :] = rows[:24, :WIDTH]
    group, inner = split_index(lax.broadcasted_iota(jnp.int32, (HALF, 1), 0).astype(F32), 24)
    col = lax.broadcasted_iota(jnp.int32, (HALF, 4 * HALF), 1).astype(F32)
    spread_out = jnp.where(col == 96.0 * group + inner, 1.0, 0.0).astype(BF)
    stack = jnp.concatenate(
        [jnp.concatenate([piece, jnp.zeros((4, WIDTH), F32)], axis=0) for _, _, piece in ups], axis=0
    ).astype(BF)
    for g in range(2):
        parts = dot(stack[:, HALF * g : HALF * g + HALF], spread_out)
        total = parts[:12]
        for i, (c, q, _) in enumerate(ups):
            if i:
                total = total + pltpu.roll(parts[16 * i : 16 * i + 16], 48 * c + 24 * q, 1)[:12]
        up_ref[:, 4 * HALF * g : 4 * HALF * g + 4 * HALF] = total
    rows = scr_ref[lax.bitwise_and(7 - y, 3)]
    tails = [
        jnp.concatenate(
            [rows[24 + 8 * c : 32 + 8 * c, HALF * k : HALF * k + HALF] for k in range(3)], axis=0
        ).astype(BF)
        for c in range(2)
    ]
    sub = lax.broadcasted_iota(jnp.int32, (HALF, 128), 0).astype(F32)
    lane = lax.broadcasted_iota(jnp.int32, (HALF, 128), 1).astype(F32)

    def take(tail, want, limit):
        hot = jnp.where(jnp.logical_and(sub == want, lane < limit), 1.0, 0.0).astype(BF)
        return dot(tail, hot)

    entry = 12.0 * device + lane
    low = sum(take(tail, entry, 12) for tail in tails)
    high = sum(take(tail, entry - HALF, 12) for tail in tails)
    rows = [low[3 + i : 4 + i] + high[4 + i : 5 + i] for i in (0, 2, 6, 8, 10, 12)]
    entry = 36.0 * device + lane
    bias = 0.0
    for t in range(3):
        for c in range(2):
            bias = bias + take(tails[c], entry - (WIDTH * t + HALF * c), 36)[t : t + 1]
    rows.append(bias)
    own = pick(core, tails[0], tails[1])
    entry = 24.0 * chip.astype(F32) + lane
    bias = 0.0
    for h in range(2):
        shifted = entry - 24.0 * h
        fits = jnp.logical_and(lane >= 24.0 * h, lane < 24.0 * h + 24.0)
        for k in range(2):
            want = jnp.where(fits, shifted - HALF * k, -1.0)
            bias = bias + take(own, want, 48)[17 + 2 * h + k : 18 + 2 * h + k]
    rows.append(bias)
    side = jnp.where(chip < 16, 0.0, 1.0)
    source = jnp.where(chip < 16, tails[0], tails[1])
    head, inner = split_index(6.0 * device + lane - 192.0 * side, 32)
    freq = take(source, 64.0 * head + inner, 6)
    freq_ref[...] = freq[7:9, :6]
    for ref, row in zip(small_refs, rows):
        ref[...] = row[0, : ref.shape[0]]


def per_device(
    tokens, image_ids, patch_row, patch_col, cotangent,
    norm1_gain, norm1_bias, qkv_weight, qkv_bias, frequencies, out_weight, out_bias,
    norm2_gain, norm2_bias, up_weight, up_bias, down_weight, down_bias,
):
    x, y, z, core = (lax.axis_index(a) for a in ("x", "y", "z", "c"))
    place = jnp.stack([core, y, x * NZ + z, z, x]).astype(jnp.int32)
    chip = x * NZ + z
    core_arr = core.reshape(1).astype(jnp.int32)

    groups = [norm1_gain, norm1_bias, out_bias, norm2_gain, norm2_bias, down_bias, qkv_bias, up_bias]
    small = jnp.concatenate(groups + [frequencies[0], frequencies[1], jnp.zeros((216,), BF)])[None]
    pieces = []
    for c in range(2):
        cols = [qkv_weight[:, WIDTH * i + HALF * c : WIDTH * i + HALF * c + HALF] for i in range(3)]
        cols.append(out_weight[:, HALF * c : HALF * c + HALF])
        piece = cols[3]
        for i in range(3):
            piece = jnp.where(y == i, cols[i], piece)
        pieces.append(jnp.concatenate([piece, small, jnp.zeros((3, HALF), BF)], axis=0))
    block = jnp.broadcast_to(jnp.stack(pieces)[None], (NZ, 2, 16, HALF)).reshape(256, HALF)
    up_split = up_weight.reshape(12, 32, 2, 2, 24)
    up_halves = [up_split[:, :, c].transpose(0, 2, 1, 3).reshape(12, FF_HALF) for c in range(2)]
    up_own = jnp.where(core == 0, up_halves[0], up_halves[1])
    up_other = jnp.where(core == 0, up_halves[1], up_halves[0])
    up_pack = in_core_order(core, up_own, swap(up_other))
    mlp_pack = jnp.concatenate([up_pack, down_weight[:24], down_weight[24:]], axis=1)

    f = ("x", "z", "c")
    onward = [(i, i + 1) for i in range(2 * NX * NZ - 1)]
    backward = [(b, a) for a, b in onward]
    spots = jnp.stack([patch_row[0], patch_col[0]], axis=1).astype(BF)
    own = jnp.concatenate([tokens[0], jnp.pad(spots, ((0, 0), (0, 126)))], axis=1)
    lower, upper = lax.ppermute(own, f, onward), lax.ppermute(own, f, backward)
    near = lax.dynamic_slice_in_dim(jnp.pad(image_ids[0] + 1, (TOK, TOK)), chip * CHIP_TOK, 4 * TOK, 0)
    ids = near[None].astype(F32)

    mlp = lax.all_gather(mlp_pack, ("x", "z"), axis=0, tiled=True)
    block = lax.all_to_all(block, ("z", "c"), split_axis=0, concat_axis=0, tiled=True)
    block = block.reshape(16, 16, HALF)
    rows, lines = block[:, :12].reshape(192, HALF), block[:, 12]
    low = jnp.concatenate([rows[:96], lines[:8]], axis=0)
    high = jnp.concatenate([rows[96:], lines[8:]], axis=0)
    low = jnp.stack(around_axis(low, "x", NX))
    high = jnp.stack(around_axis(high, "y", NY))
    low, high, lower, upper, dy_own = lax.optimization_barrier((low, high, lower, upper, cotangent[0]))
    edge = jnp.where(core == 0, lower, upper)
    far = swap(edge)
    sources = [own, lower, upper, far]
    dy_other = swap(dy_own)
    by_y = around_axis(low, "y", NY)
    by_x = around_axis(high, "x", NX)

    wide, half, square = ((CHIP_TOK, WIDTH), BF), ((CHIP_TOK, HALF), BF), ((HALF, HALF), BF)
    ids, *parts = lax.optimization_barrier((ids, *by_y, *by_x))
    q, k, v, keep, send, *kept = qkv_call(place, sources, parts[:4], parts[4:])
    q_kept, k_kept, v_kept, vec, a1, turn, weights, inputs = kept
    got = swap(send)
    branch, o, lse, out_rows = attend(core_arr, q, k, v, ids, keep, got)

    a2, middle = norm_call(core_arr, branch, swap(branch), inputs, vec)
    da2, *held, high, result, result_send, du_sums, l0, l1, l2, l3 = mlp_call(
        place, a2, vec, mlp, dy_own, dy_other, middle, o, out_rows, lse
    )
    output = (result + swap(result_send).astype(F32)).astype(BF)[None]
    mlp_lows = [fetch(part, "x", NX, k) for k, part in enumerate((l0, l1, l2, l3))]

    do, delta, to_prev, to_next, out_own, out_send, sums, dmid = whole_call(
        branch_kernel, "branch",
        [((CHIP_TOK, HALF), BF), ((3, 2, CHIP_TOK), F32), ((288, HALF), BF), ((288, HALF), BF),
         ((HALF, HALF), BF), ((HALF, HALF), BF), ((4, WIDTH), F32), ((TOK, WIDTH), F32)],
        core_arr, [da2, swap(da2), *held],
        scratch=[pltpu.VMEM((CHIP_TOK, WIDTH), F32), pltpu.SemaphoreType.DMA((2,))],
        flops=10**9, vmem=14, far=(7,),
    )
    high, do = lax.optimization_barrier((high, do))
    mlp_high = scatter_sum(high, "y").reshape(4, 96, WIDTH)
    up_list = [(i, i + 1) for i in range(NX * NZ - 1)]
    down_list = [(b, a) for a, b in up_list]
    from_prev = lax.ppermute(to_next, ("x", "z"), up_list)
    from_next = lax.ppermute(to_prev, ("x", "z"), down_list)
    dq, dkv, *kept = near_back(
        core_arr, [q_kept, k_kept, v_kept, turn, a1, inputs, weights], do, lse, delta, ids
    )
    *parts, da1_own, da1_send = qkv_grad_call(
        place, [dq, dkv, from_prev, from_next, out_own, swap(out_send), sums], kept, ids, du_sums
    )
    highs = [fetch(part, "y", NY, k) for k, part in enumerate(parts[4:])]
    lows = [fetch(part, "x", NX, k) for k, part in enumerate(parts[:4])]
    da1 = da1_own + swap(da1_send).astype(F32)
    unit, scale = centred(tokens[0].astype(F32))
    input_grad = (centred_back(unit, scale, da1 * vec[0]) + dmid)[None]

    seconds = whole_call(
        mid_kernel, "mid", [((104, 3 * HALF), BF)] * 4 + [((96, 3 * HALF), BF)] * 4, place,
        [*highs, *lows, *mlp_lows, mlp_high],
        scratch=[
            pltpu.VMEM((4, 4, 112, HALF), BF), pltpu.VMEM((4, 4, 96, HALF), BF),
            pltpu.VMEM((4, 4, 96, WIDTH), BF), pltpu.VMEM((4, 96, WIDTH), BF),
            pltpu.SemaphoreType.DMA((16,)),
        ],
        vmem=16, away=tuple(range(13)),
    )
    lows = [fetch(part, "y", NY, k) for k, part in enumerate(seconds[:4])]
    highs = [fetch(part, "x", NX, k) for k, part in enumerate(seconds[4:])]
    (joined,) = whole_call(
        join_kernel, "join", [((8, 32, 3 * HALF), BF)], core_arr, lows + highs
    )
    joined = lax.all_to_all(
        joined.reshape(256, 3 * HALF), "z", split_axis=0, concat_axis=0, tiled=True
    )
    (mine,) = whole_call(
        total_kernel, "total", [((32, 3 * HALF), BF)],
        core_arr, [joined.reshape(8, 32, 3 * HALF)],
    )
    (part,) = whole_call(
        share_kernel, "share", [((40, 3 * HALF), BF)], place, [mine, swap(mine)]
    )
    parts = [fetch(part, "y", NY, k) for k in range(NY)]
    qkv_grad, out_weight_grad, up_grad, down_grad, *smalls, freq_grad = whole_call(
        last_kernel, "last",
        [((12, 3 * WIDTH), F32), ((12, WIDTH), F32), ((12, 4 * WIDTH), F32), ((48, WIDTH), F32)]
        + [((size,), F32) for size in (12, 12, 12, 12, 12, 12, 36, 48)]
        + [((2, 6), F32)],
        place, parts, scratch=[pltpu.VMEM((4, 40, 3 * HALF), F32)],
    )
    qkv_bias_grad, up_bias_grad = smalls[6:]
    return (
        output, input_grad,
        smalls[0], smalls[1], qkv_grad, qkv_bias_grad, freq_grad, out_weight_grad, smalls[2],
        smalls[3], smalls[4], up_grad, up_bias_grad, down_grad, smalls[5],
    )


def solution(mesh):
    fine = Mesh(mesh.devices.reshape(NY, NX, NZ, 2), ("y", "x", "z", "c"))
    f = ("x", "z", "c")
    return jax.shard_map(
        per_device,
        mesh=fine,
        in_specs=(
            P("y", f, None), P("y", None), P("y", f), P("y", f), P("y", f, None),
            P(f), P(f), P(f, None), P(f), P(None, f), P(f, None), P(f),
            P(f), P(f), P(f, None), P(f), P(f, None), P(f),
        ),
        out_specs=(
            P("y", f, None), P("y", f, None),
            P(f), P(f), P(f, None), P(f), P(None, f), P(f, None), P(f),
            P(f), P(f), P(f, None), P(f), P(f, None), P(f),
        ),
        check_vma=False,
    )
```

```python
import jax
import jax.numpy as jnp
from jax import lax
from jax.experimental import pallas as pl
from jax.experimental.pallas import tpu as pltpu
from jax.sharding import Mesh, PartitionSpec as P

NX, NY, NZ = 4, 4, 8
HEADS = 12
LOCAL_HEADS = 6
WIDTH = 768
HALF = 384
FF_HALF = 1536
TOK = 256
CHIP_TOK = 512
MASKED = -1e30
BF = jnp.bfloat16
F32 = jnp.float32
MIB = 1 << 20
OWN = slice(TOK, 3 * TOK)


def fetch(value, axis, size, step):
    if step == 0:
        return value
    return lax.ppermute(value, axis, [((i + step) % size, i) for i in range(size)])


def swap(value):
    return lax.ppermute(value, "c", [(0, 1), (1, 0)])


def in_core_order(core, own, other):
    first = jnp.where(core == 0, own, other)
    second = jnp.where(core == 0, other, own)
    return jnp.concatenate([first, second], axis=0)


def dot(a, b):
    return jnp.dot(a, b, preferred_element_type=F32)


def dot_nt(a, b):
    return lax.dot_general(a, b, (((1,), (1,)), ((), ())), preferred_element_type=F32)


def dot_tn(a, b):
    return lax.dot_general(a, b, (((0,), (0,)), ((), ())), preferred_element_type=F32)


def around_axis(block, axis, size):
    return [fetch(block, axis, size, k) for k in range(size)]


def scatter_sum(blocks, axis):
    count, rows, cols = blocks.shape
    return lax.psum_scatter(
        blocks.reshape(count * rows, cols), axis, scatter_dimension=0, tiled=True
    )


def whole_call(kernel, name, outs, scalars, arrays, scratch=(), flops=0, vmem=10, far=(), away=()):
    size = sum(v.size * v.dtype.itemsize for v in arrays)
    spec = lambda remote: pl.BlockSpec(memory_space=pl.ANY if remote else pltpu.VMEM)
    shapes = [(pltpu.HBM if i in far else jax.ShapeDtypeStruct)(*o) for i, o in enumerate(outs)]
    return pl.pallas_call(
        kernel,
        out_shape=shapes,
        in_specs=[pl.BlockSpec(memory_space=pltpu.SMEM)]
        + [spec(i in away) for i in range(len(arrays))],
        out_specs=[spec(i in far) for i in range(len(outs))],
        scratch_shapes=list(scratch),
        compiler_params=pltpu.CompilerParams(vmem_limit_bytes=vmem * MIB),
        cost_estimate=pl.CostEstimate(flops=flops, bytes_accessed=size, transcendentals=0),
        name=name,
    )(
        scalars,
        *[
            pltpu.with_memory_space_constraint(v, pltpu.HBM) if i in away else v
            for i, v in enumerate(arrays)
        ],
    )


class Mover:
    def __init__(self, sems):
        self.sems, self.count, self.open = sems, 0, []

    def start(self, source, target):
        copy = pltpu.make_async_copy(source, target, self.sems.at[self.count])
        self.count += 1
        copy.start()
        return copy

    def load(self, pairs):
        return [self.start(source, target) for source, target in pairs]

    def put(self, source, target):
        self.open.append(self.start(source, target))

    def finish(self):
        for copy in self.open:
            copy.wait()


def wait_all(copies):
    for copy in copies:
        copy.wait()


def id_columns(row_ref):
    return jnp.transpose(jnp.broadcast_to(row_ref[...], (8, 4 * TOK)))[:, :1]


def two_heads(block):
    lane = lax.broadcasted_iota(jnp.int32, block.shape, 1)
    zero = jnp.zeros_like(block)
    return jnp.concatenate(
        [jnp.where(lane < 64, block, zero), jnp.where(lane < 64, zero, block)], axis=0
    )


def by_head(first, second):
    row = lax.broadcasted_iota(jnp.int32, first.shape, 0)
    return jnp.where(row < 64, first, second)


def scaled(block):
    return block * jnp.asarray(0.125, BF)


def pair_of(i):
    return pl.ds(pl.multiple_of(128 * i, 128), 128)


def attend_kernel(
    core_ref, q_ref, k_ref, v_ref, keep_ref, got_ref, id_hbm,
    part_ref, o_hbm, lse_hbm, w_hbm, o_ref, lse_ref, w_ref, id_ref, kid_ref, sems,
):
    mover = Mover(sems)
    mover.start(id_hbm, id_ref).wait()
    w_ref[:, :HALF] = pick(core_ref[0], keep_ref[...], got_ref[...])
    w_ref[:, HALF:] = pick(core_ref[0], got_ref[...], keep_ref[...])
    mover.put(w_ref, w_hbm)
    kid_ref[...] = id_columns(id_ref)

    def body(i, carry):
        pair = pair_of(i)
        v_turned = jnp.transpose(v_ref[:, pair])
        for tile in range(2):
            near = slice(TOK * tile, TOK * tile + 3 * TOK)
            mine = slice(TOK * tile + TOK, TOK * tile + 2 * TOK)
            here = slice(TOK * tile, TOK * tile + TOK)
            keep = kid_ref[near, :] == id_ref[0:1, mine]
            scores = dot_nt(k_ref[near, pair], two_heads(scaled(q_ref[mine, pair])))
            halves = []
            for h in range(2):
                s = jnp.where(keep, scores[:, TOK * h : TOK * h + TOK], MASKED)
                top = jnp.max(s, axis=0, keepdims=True)
                expo = jnp.exp(s - top)
                total = jnp.sum(expo, axis=0, keepdims=True)
                lse_ref[i, h : h + 1, here] = top + jnp.log(total)
                p = (expo * (1.0 / total)).astype(BF)
                halves.append(dot(v_turned[:, near], p))
            o_ref[here, pair] = jnp.transpose(by_head(*halves)).astype(BF)
        return carry

    lax.fori_loop(0, 3, body, 0)
    mover.put(o_ref, o_hbm)
    mover.put(lse_ref, lse_hbm)
    part_ref[...] = dot(o_ref[...], w_ref[...]).astype(BF)
    mover.finish()


def attend(core, q, k, v, ids, keep, got):
    o, lse, weights = ((CHIP_TOK, HALF), BF), ((3, 2, CHIP_TOK), F32), ((HALF, WIDTH), BF)
    return whole_call(
        attend_kernel, "attend", [((CHIP_TOK, WIDTH), BF), o, lse, weights],
        core, [q, k, v, keep, got, ids],
        scratch=[
            pltpu.VMEM(*o), pltpu.VMEM(*lse), pltpu.VMEM(*weights),
            pltpu.VMEM((1, 4 * TOK), F32), pltpu.VMEM((4 * TOK, 1), F32), pltpu.SemaphoreType.DMA((8,)),
        ],
        flops=3 * 10**9, vmem=12, far=(1, 2, 3), away=(5,),
    )


def pair_grads(k, v, q2, do2, keep, lses, deltas):
    scores = dot_nt(k, q2)
    dprobs = dot_nt(v, do2)
    probs, dscores = [], []
    for h in range(2):
        lanes = slice(TOK * h, TOK * h + TOK)
        p = jnp.exp(jnp.where(keep, scores[:, lanes], MASKED) - lses[h])
        dscores.append((p * (dprobs[:, lanes] - deltas[h])).astype(BF))
        probs.append(p.astype(BF))
    return probs, dscores


def near_back_kernel(
    core_ref, q_hbm, k_hbm, v_hbm, turn_hbm, a1_hbm, x_hbm, w_hbm, lse_hbm, id_hbm, do_ref, delta_ref,
    dq_ref, dkv_ref, q_ref, k_ref, v_ref, turn_ref, a1_ref, x_ref, w_ref,
    lse_ref, id_ref, kid_ref, sems, more_sems,
):
    mover = Mover(more_sems)
    first_loads = mover.load(((id_hbm, id_ref), (lse_hbm, lse_ref)))
    sources = ((q_hbm, q_ref), (k_hbm, k_ref), (v_hbm, v_ref))

    def load(i):
        return [
            pltpu.make_async_copy(source.at[:, pair_of(i)], target.at[:, pair_of(i)], sems.at[i, j])
            for j, (source, target) in enumerate(sources)
        ]

    for i in range(3):
        for copy in load(i):
            copy.start()
    later = mover.load(
        ((turn_hbm, turn_ref), (a1_hbm, a1_ref), (w_hbm.at[pl.ds(0, 3)], w_ref), (x_hbm, x_ref))
    )
    wait_all(first_loads)
    kid_ref[...] = id_columns(id_ref)

    def body(i, carry):
        pair = pair_of(i)
        wait_all(load(i))
        k_turned = jnp.transpose(k_ref[:, pair])
        for tile in range(2):
            near = slice(TOK * tile, TOK * tile + 3 * TOK)
            mine = slice(TOK * tile + TOK, TOK * tile + 2 * TOK)
            here = slice(TOK * tile, TOK * tile + TOK)
            k = k_ref[near, pair]
            q2 = two_heads(scaled(q_ref[mine, pair]))
            do2 = two_heads(do_ref[here, pair])
            keep = kid_ref[near, :] == id_ref[0:1, mine]
            probs, dscores = pair_grads(
                k, v_ref[near, pair], q2, do2, keep,
                [lse_ref[i, h : h + 1, here] for h in range(2)],
                [delta_ref[i, h : h + 1, here] for h in range(2)],
            )
            dq = by_head(*[dot(k_turned[:, near], ds) for ds in dscores])
            dq_ref[here, pair] = jnp.transpose(dq) * 0.125
            first = TOK * (1 - tile)
            own = slice(first, first + 2 * TOK)
            dk = dot(jnp.concatenate([d[own] for d in dscores], axis=1), q2)
            dv = dot(jnp.concatenate([p[own] for p in probs], axis=1), do2)
            for which, full in enumerate((dk, dv)):
                if tile == 0:
                    dkv_ref[which, :, pair] = full
                else:
                    dkv_ref[which, :, pair] += full
        return carry

    lax.fori_loop(0, 3, body, 0)
    wait_all(later)


def near_back(core, kept, grad, lse, delta, ids):
    around = ((4 * TOK, HALF), BF)
    return whole_call(
        near_back_kernel, "near_back",
        [
            ((CHIP_TOK, HALF), F32), ((2, CHIP_TOK, HALF), F32), around, around, around,
            ((2, CHIP_TOK, HALF), F32), ((CHIP_TOK, WIDTH), BF), ((CHIP_TOK, WIDTH + 128), BF),
            ((3, WIDTH, HALF), BF),
        ],
        core, [*kept, lse, ids, grad, delta], away=tuple(range(9)),
        scratch=[
            pltpu.VMEM((3, 2, CHIP_TOK), F32), pltpu.VMEM((1, 4 * TOK), F32),
            pltpu.VMEM((4 * TOK, 1), F32), pltpu.SemaphoreType.DMA((3, 3)), pltpu.SemaphoreType.DMA((8,)),
        ],
        flops=4 * 10**9, vmem=12,
    )


def far_back(q_ref, k_ref, v_ref, before_ref, after_ref, id_ref, kid_ref, dkv_ref, sum_ref):
    row = lax.broadcasted_iota(jnp.int32, (8, TOK), 0)

    def body(i, carry):
        pair = pair_of(i)
        for side, ref in enumerate((before_ref, after_ref)):
            keys = slice(TOK * (side + 1), TOK * (side + 2))
            queries = slice(3 * TOK * side, 3 * TOK * side + TOK)
            tail = ref[TOK:, :TOK].astype(F32)
            deltas = tail[0:8] + tail[8:16]
            lses = tail[16:24] + tail[24:32]
            choose = lambda v, h: jnp.sum(
                jnp.where(row == 2 * i + h, v, 0.0), axis=0, keepdims=True
            )
            q2 = two_heads(scaled(q_ref[queries, pair]))
            do2 = two_heads(ref[:TOK, pair])
            keep = kid_ref[keys, :] == id_ref[0:1, queries]
            probs, dscores = pair_grads(
                k_ref[keys, pair], v_ref[keys, pair], q2, do2, keep,
                [choose(lses, h) for h in range(2)], [choose(deltas, h) for h in range(2)],
            )
            rows = slice(TOK * side, TOK * side + TOK)
            dk = dot(jnp.concatenate(dscores, axis=1), q2)
            dv = dot(jnp.concatenate(probs, axis=1), do2)
            sum_ref[0, rows, pair] = dkv_ref[0, rows, pair] + dk
            sum_ref[1, rows, pair] = dkv_ref[1, rows, pair] + dv
        return carry

    lax.fori_loop(0, 3, body, 0)


def centred(value):
    shifted = value - jnp.mean(value, axis=-1, keepdims=True)
    spread = jnp.mean(shifted * shifted, axis=-1, keepdims=True)
    scale = lax.rsqrt(spread + 1e-06)
    return shifted * scale, scale


def centred_back(unit, scale, grad):
    mean = jnp.mean(grad, axis=-1, keepdims=True)
    along = jnp.mean(grad * unit, axis=-1, keepdims=True)
    return scale * (grad - mean - unit * along)


def lanes_of(width):
    return lax.broadcasted_iota(jnp.int32, (1, width), 1).astype(F32)


def pick(core, first, second):
    return jnp.where(core == 0, first, second)


def expand(lines, shift, lane_in, owner):
    width = lane_in.shape[1]
    moved = pltpu.roll(lines, (HALF - shift) % HALF, 1)[:, :128].astype(BF)
    sub = lax.broadcasted_iota(jnp.int32, (128, width), 0).astype(F32)
    table = dot(moved, jnp.where(sub == lane_in, 1.0, 0.0).astype(BF))
    sub = lax.broadcasted_iota(jnp.int32, (64, width), 0).astype(F32)
    return jnp.sum(jnp.where(sub == owner, table, 0.0), axis=0, keepdims=True)


def split_index(index, size):
    group = jnp.floor((index + 0.5) * (1.0 / size))
    return group, index - group * size


def low_half(shape):
    return lax.bitwise_and(lax.broadcasted_iota(jnp.int32, shape, 1), 63) < 32


def swap_halves(value):
    ahead = pltpu.roll(value, HALF - 32, 1)
    behind = pltpu.roll(value, 32, 1)
    return jnp.where(low_half(value.shape), ahead, behind)


def three_parts(value):
    parts = []
    for _ in range(3):
        part = value.astype(BF)
        parts.append(part)
        value = value - part.astype(F32)
    return jnp.concatenate(parts, axis=0)


def qkv_kernel(place_ref, *refs):
    by_y, by_x, sources, refs = refs[:4], refs[4:8], refs[8:12], refs[12:]
    q_ref, k_ref, v_ref, keep_ref, send_ref = refs[:5]
    q_hbm, k_hbm, v_hbm, vec_hbm, a1_hbm, turn_hbm, w_hbm, x_hbm = refs[5:13]
    table_ref, bias_ref, line_ref, x_ref, a1_ref, turn_ref, w_ref, vec_ref, sems, x_sems = refs[13:]
    core, x, y = place_ref[0], place_ref[4], place_ref[1]
    mover = Mover(sems)

    def x_load(step, source):
        return pltpu.make_async_copy(source, x_ref.at[pl.ds(TOK * step, TOK), :], x_sems.at[step])

    own, lower, upper, far = sources

    @pl.when(core == 0)
    def _():
        for step, source in enumerate((lower, own, upper, far)):
            x_load(step, source).start()

    @pl.when(core == 1)
    def _():
        for step, source in enumerate((far, lower, own, upper)):
            x_load(step, source).start()

    core_f = core.astype(F32)
    for ky in range(4):
        for kx in range(4):
            q = lax.bitwise_and(y + ky, 3)
            chip = lax.bitwise_and(x + kx, 3)
            low = pl.ds(pl.multiple_of(192 * chip, 96), 96)
            high = pl.ds(pl.multiple_of(192 * chip + 96, 96), 96)
            w_ref[q, low, :] = by_y[ky][kx, :96, :]
            w_ref[q, high, :] = by_x[kx][ky, :96, :]
    for kx in range(4):
        chip = lax.bitwise_and(x + kx, 3)
        low = pl.ds(pl.multiple_of(16 * chip, 8), 8)
        high = pl.ds(pl.multiple_of(16 * chip + 8, 8), 8)
        line_ref[low, :] = by_y[0][kx, 96:, :].astype(F32)
        line_ref[high, :] = by_x[kx][0, 96:, :].astype(F32)
    lines = line_ref[...]
    group, inner = split_index(lanes_of(WIDTH), 12)
    rows = [expand(lines, 12 * i, inner, group) for i in range(6)]
    group, inner = split_index(lanes_of(WIDTH), 24)
    rows += [expand(lines, 108 + 24 * h, inner, 2.0 * group + core_f) for h in range(2)]
    vec_ref[...] = jnp.concatenate(rows, axis=0)
    group, inner = split_index(lanes_of(3 * WIDTH), 36)
    bias = expand(lines, 72, inner, group)
    for i in range(3):
        bias_ref[i : i + 1, :] = pick(
            core,
            bias[:, WIDTH * i : WIDTH * i + HALF],
            bias[:, WIDTH * i + HALF : WIDTH * i + WIDTH],
        )
    lane = lanes_of(HALF)
    head, _ = split_index(lane, 64)
    _, inner = split_index(lane, 32)
    group, inner = split_index(192.0 * core_f + 32.0 * head + inner, 6)
    count = lax.broadcasted_iota(jnp.int32, (32, HALF), 0).astype(F32)
    for f in range(2):
        angle = count * expand(lines, 156 + 6 * f, inner, group)
        table_ref[f] = three_parts(jnp.concatenate([jnp.cos(angle), jnp.sin(angle)], axis=1))
    keep_ref[...] = w_ref[3, pl.ds(pl.multiple_of(HALF * core, HALF), HALF), :]
    send_ref[...] = w_ref[3, pl.ds(pl.multiple_of(HALF * (1 - core), HALF), HALF), :]
    mover.put(w_ref, w_hbm)
    mover.put(vec_ref, vec_hbm)
    for step in range(4):
        rows = slice(TOK * step, TOK * step + TOK)
        x_load(step, own).wait()
        spots = x_ref[rows, WIDTH:].astype(F32)
        spot = lax.bitwise_and(lax.broadcasted_iota(jnp.int32, (TOK, 96), 1), 31).astype(F32)
        tables = [
            dot(jnp.where(spots[:, f : f + 1] == spot, 1.0, 0.0).astype(BF), table_ref[f])
            for f in range(2)
        ]
        cos_r, sin_r = tables[0][:, :HALF], tables[0][:, HALF:]
        cos_c, sin_c = tables[1][:, :HALF], tables[1][:, HALF:]
        cosine = cos_r * cos_c - sin_r * sin_c
        sine = sin_r * cos_c + cos_r * sin_c
        sine = jnp.where(low_half(sine.shape), -sine, sine)
        unit, _ = centred(x_ref[rows, :WIDTH].astype(F32))
        a1 = (unit * vec_ref[0:1, :] + vec_ref[1:2, :]).astype(BF)
        if step in (1, 2):
            here = slice(TOK * (step - 1), TOK * step)
            turn_ref[0, here, :] = cosine
            turn_ref[1, here, :] = sine
            a1_ref[here, :] = a1
            if step == 2:
                mover.put(x_ref.at[pl.ds(TOK, CHIP_TOK), :], x_hbm)
                mover.put(turn_ref, turn_hbm)
                mover.put(a1_ref, a1_hbm)
        for i, ref in enumerate((q_ref, k_ref, v_ref)):
            part = dot(a1, w_ref[i]) + bias_ref[i : i + 1, :]
            if i < 2:
                part = part * cosine + swap_halves(part) * sine
            ref[rows, :] = part.astype(BF)
            mover.put(ref.at[pl.ds(TOK * step, TOK), :], (q_hbm, k_hbm, v_hbm)[i].at[pl.ds(TOK * step, TOK), :])
    mover.finish()


def qkv_call(place, sources, by_y, by_x):
    around, square = ((4 * TOK, HALF), BF), ((HALF, HALF), BF)
    wide, turn = ((CHIP_TOK, WIDTH), BF), ((2, CHIP_TOK, HALF), F32)
    vec, full = ((8, WIDTH), F32), ((4, WIDTH, HALF), BF)
    return whole_call(
        qkv_kernel, "qkv",
        [around, around, around, square, square, around, around, around, vec, wide, turn, full]
        + [((CHIP_TOK, WIDTH + 128), BF)],
        place, [*by_y, *by_x, *sources],
        scratch=[
            pltpu.VMEM((2, 96, WIDTH), BF), pltpu.VMEM((8, HALF), F32), pltpu.VMEM((64, HALF), F32),
            pltpu.VMEM((4 * TOK, WIDTH + 128), BF), pltpu.VMEM(*wide), pltpu.VMEM(*turn),
            pltpu.VMEM(*full), pltpu.VMEM(*vec), pltpu.SemaphoreType.DMA((24,)),
            pltpu.SemaphoreType.DMA((4,)),
        ],
        flops=2 * 10**9, vmem=18, far=tuple(range(5, 13)), away=tuple(range(8, 12)),
    )


def norm_kernel(core_ref, part_ref, got_ref, x_hbm, vec_hbm, a2_ref, mid_hbm, x_ref, vec_ref, mid_ref, sems):
    mover = Mover(sems)
    wait_all(mover.load(((x_hbm.at[:, pl.ds(0, WIDTH)], x_ref), (vec_hbm, vec_ref))))
    middle = x_ref[...].astype(F32) + (
        part_ref[...].astype(F32) + got_ref[...].astype(F32) + vec_ref[2:3, :]
    )
    mid_ref[...] = middle
    mover.put(mid_ref, mid_hbm)
    unit, _ = centred(middle)
    a2_ref[...] = (unit * vec_ref[3:4, :] + vec_ref[4:5, :]).astype(BF)
    mover.finish()


def mlp_kernel(
    place_ref, a2_ref, vec_hbm, w_hbm, dya_hbm, dyb_hbm, mid_hbm, o_hbm, wo_hbm, lse_hbm,
    da2_ref, mid_ref, dy_ref, vec_ref, o_ref, wo_ref, lse_ref, high_hbm, own_hbm, send_hbm, sums_hbm, *refs,
):
    low_hbms = refs[:4]
    acc_ref, grads_ref, w_ref, own_ref, send_ref, sums_ref, act_ref, du_ref, sems = refs[4:]
    core, x = place_ref[0], place_ref[4]
    own = pl.ds(pl.multiple_of(core * TOK, TOK), TOK)
    rest = pl.ds(pl.multiple_of((1 - core) * TOK, TOK), TOK)
    mover = Mover(sems)
    load_vec = mover.start(vec_hbm, vec_ref)
    loads = []
    for i in (0, 2, 1, 3):
        cols = pl.ds(WIDTH * i, WIDTH)
        loads.append(mover.start(w_hbm.at[:, cols], w_ref.at[:, cols]))
        if i == 0:
            load_dy = mover.load(((dya_hbm, dy_ref.at[own, :]), (dyb_hbm, dy_ref.at[rest, :])))

    def put(index, value):
        grads_ref[index] = value.astype(BF)
        for k, ref in enumerate(low_hbms):
            row = pl.multiple_of(192 * lax.bitwise_and(x + 4 - k, 3), 96)
            mover.put(grads_ref.at[index, pl.ds(row, 96), :], ref.at[index])
        for j in range(4):
            rows = pl.ds(192 * j + 96, 96)
            mover.put(grads_ref.at[index, rows, :], high_hbm.at[index, pl.ds(96 * j, 96), :])

    load_vec.wait()
    a2 = a2_ref[...]
    a2_turned = jnp.transpose(a2)
    da2 = None
    for h in range(2):
        lanes = slice(WIDTH * h, WIDTH * h + WIDTH)
        loads[2 * h].wait()
        loads[2 * h + 1].wait()
        if h == 0:
            wait_all(load_dy)
            later = mover.load(((mid_hbm, mid_ref), (o_hbm, o_ref), (wo_hbm, wo_ref), (lse_hbm, lse_ref)))
        dy = dy_ref[...]
        up = w_ref[:, lanes]
        down = w_ref[:, FF_HALF + WIDTH * h : FF_HALF + WIDTH * h + WIDTH]
        for j in range(3):
            cols = slice(TOK * j, TOK * j + TOK)
            u = dot(a2, up[:, cols]) + vec_ref[6 + h : 7 + h, cols]
            gate = 0.5 * (1.0 + lax.erf(u * 0.7071067811865476))
            act_ref[:, cols] = (u * gate).astype(BF)
            slope = gate + u * jnp.exp(-0.5 * u * u) * 0.3989422804014327
            low = (slope * dot_nt(dy, down[cols, :])).astype(BF)
            du_ref[:, cols] = low
            sums_ref[h : h + 1, cols] = jnp.sum(low.astype(F32), axis=0, keepdims=True)
        act, du = act_ref[...], du_ref[...]
        put(2 + h, dot_tn(act, dy))
        put(h, dot(a2_turned, du))
        term = dot(act, down)
        if h == 0:
            acc_ref[...] = term
        else:
            acc_ref[...] += term
        term = dot_nt(du, up)
        da2 = term if da2 is None else da2 + term
    da2_ref[...] = da2.astype(BF)
    mover.put(sums_ref, sums_hbm)
    wait_all(later)
    own_ref[...] = acc_ref[own, :] + mid_ref[own, :] + vec_ref[5:6, :]
    send_ref[...] = acc_ref[rest, :].astype(BF)
    mover.put(own_ref, own_hbm)
    mover.put(send_ref, send_hbm)
    mover.finish()


def norm_call(core, branch, got, inputs, vec):
    full = (CHIP_TOK, WIDTH)
    return whole_call(
        norm_kernel, "norm", [(full, BF), (full, F32)], core, [branch, got, inputs, vec],
        scratch=[
            pltpu.VMEM(full, BF), pltpu.VMEM((8, WIDTH), F32), pltpu.VMEM(full, F32),
            pltpu.SemaphoreType.DMA((4,)),
        ],
        vmem=12, far=(1,), away=(2, 3),
    )


def mlp_call(place, a2, vec, weights, dy_own, dy_other, middle, o, out_rows, lse):
    full, half = (CHIP_TOK, WIDTH), (TOK, WIDTH)
    return whole_call(
        mlp_kernel, "mlp",
        [
            (full, BF), (full, F32), (full, BF), ((8, WIDTH), F32), ((CHIP_TOK, HALF), BF),
            ((HALF, WIDTH), BF), ((3, 2, CHIP_TOK), F32), ((4, HALF, WIDTH), BF), (half, F32), (half, BF),
            ((2, WIDTH), F32),
        ]
        + [((4, 96, WIDTH), BF)] * 4,
        place, [a2, vec, weights, dy_own, dy_other, middle, o, out_rows, lse],
        scratch=[
            pltpu.VMEM(full, F32), pltpu.VMEM((4, WIDTH, WIDTH), BF), pltpu.VMEM((WIDTH, 4 * WIDTH), BF),
            pltpu.VMEM(half, F32), pltpu.VMEM(half, BF), pltpu.VMEM((2, WIDTH), F32),
            pltpu.VMEM(full, BF), pltpu.VMEM(full, BF), pltpu.SemaphoreType.DMA((56,)),
        ],
        flops=8 * 10**9, vmem=30, far=tuple(range(7, 15)), away=tuple(range(1, 9)),
    )


def branch_kernel(
    core_ref, da2_ref, got_ref, mid_ref, dy_ref, vec_ref, o_ref, w_ref, lse_ref,
    do_ref, delta_ref, back_ref, on_ref, own_ref, send_ref, sums_ref, dmid_hbm, scr_ref, sems,
):
    core = core_ref[0]
    mover = Mover(sems)
    mine = pl.ds(pl.multiple_of(core * TOK, TOK), TOK)
    unit, scale = centred(mid_ref[...])
    da2 = da2_ref[...].astype(F32) + got_ref[...].astype(F32)
    dy = dy_ref[...].astype(F32)
    dmid = centred_back(unit, scale, da2 * vec_ref[3:4, :]) + dy
    low = dmid.astype(BF)
    scr_ref[...] = dmid
    mover.put(scr_ref.at[mine, :], dmid_hbm)
    do = dot_nt(low, w_ref[...]).astype(BF)
    do_ref[...] = do
    heads = lax.broadcasted_iota(jnp.int32, (8, HALF), 0)
    lane = lax.broadcasted_iota(jnp.int32, (8, HALF), 1)
    hot = jnp.where(jnp.logical_and(lane >= 64 * heads, lane < 64 * heads + 64), 1.0, 0.0)
    delta = lax.dot_general(
        hot, do.astype(F32) * o_ref[...].astype(F32), (((1,), (1,)), ((), ())),
        precision=lax.Precision.HIGHEST, preferred_element_type=F32,
    )
    for i in range(3):
        delta_ref[i] = delta[2 * i : 2 * i + 2]
    lse = jnp.concatenate([lse_ref[i] for i in range(3)] + [jnp.zeros((2, CHIP_TOK), F32)], axis=0)
    tail = []
    for value in (delta, lse):
        high = value.astype(BF)
        tail += [high, (value - high.astype(F32)).astype(BF)]
    tail = jnp.concatenate(tail, axis=0)
    for ref, rows in ((back_ref, slice(0, TOK)), (on_ref, slice(TOK, CHIP_TOK))):
        ref[:TOK, :] = do[rows]
        ref[TOK:, :] = jnp.concatenate([tail[:, rows], jnp.zeros((32, 128), BF)], axis=1)
    grad = dot_tn(o_ref[...], low).astype(BF)
    own_ref[...] = pick(core, grad[:, :HALF], grad[:, HALF:])
    send_ref[...] = pick(core, grad[:, HALF:], grad[:, :HALF])
    row = lax.broadcasted_iota(jnp.int32, (CHIP_TOK, 1), 0)
    here = jnp.logical_and(row >= core * TOK, row < core * TOK + TOK)
    total = lambda v: jnp.sum(jnp.where(here, v, 0.0), axis=0, keepdims=True)
    sums_ref[0:1, :] = total(low.astype(F32))
    sums_ref[1:2, :] = total(da2 * unit)
    sums_ref[2:3, :] = total(da2)
    sums_ref[3:4, :] = total(dy)
    mover.finish()


def qkv_grad_kernel(
    place_ref, dq_ref, near_ref, before_ref, after_ref, own_ref, got_ref, sums_ref,
    q_ref, k_ref, v_ref, turn_ref, a1_ref, x_ref, w_ref, id_hbm, more_hbm,
    *refs,
):
    low_hbms, high_hbms, da1_own_hbm, da1_send_hbm = refs[:4], refs[4:8], refs[8], refs[9]
    da1_ref, da1_send_ref, full_ref, tail_ref, dkv_ref, kid_ref, id_ref, more_ref, sems, high_sems = refs[10:]
    core, x, y = place_ref[0], place_ref[4], place_ref[1]
    mover = Mover(sems)
    wait_all(mover.load(((id_hbm, id_ref), (more_hbm, more_ref))))
    kid_ref[...] = id_columns(id_ref)
    far_back(q_ref, k_ref, v_ref, before_ref, after_ref, id_ref, kid_ref, near_ref, dkv_ref)

    def high_copies(step, k):
        return [
            pltpu.make_async_copy(
                full_ref.at[step, pl.ds(192 * j + 96, 96), :], high_hbms[k].at[j], high_sems.at[k, j]
            )
            for j in range(4)
        ]

    def hand_out(step, full):
        full_ref[step] = full
        for k, ref in enumerate(low_hbms):
            row = pl.multiple_of(192 * lax.bitwise_and(x + 4 - k, 3), 96)
            mover.put(full_ref.at[step, pl.ds(row, 96), :], ref.at[step, pl.ds(0, 96), :])
        for k in range(4):

            @pl.when(lax.bitwise_and(y + 4 - k, 3) == step)
            def _():
                for copy in high_copies(step, k):
                    copy.start()

    tail = []
    angle = 0.0
    a1_turned = jnp.transpose(a1_ref[...])
    for step, grad in enumerate((dq_ref[...], dkv_ref[0], dkv_ref[1])):
        if step < 2:
            other = swap_halves(grad)
            turned = (q_ref, k_ref)[step][OWN, :].astype(F32)
            angle = angle + other * turned - grad * swap_halves(turned)
            grad = grad * turn_ref[0] - other * turn_ref[1]
        low = grad.astype(BF)
        tail.append(jnp.sum(low.astype(F32), axis=0, keepdims=True))
        hand_out(step, dot(a1_turned, low).astype(BF))
        term = dot_nt(low, w_ref[step])
        if step == 0:
            da1_ref[...] = term
        else:
            da1_ref[...] += term
    first = pick(core, own_ref[...], got_ref[...])
    second = pick(core, got_ref[...], own_ref[...])
    hand_out(3, jnp.concatenate([first, second], axis=0))
    da1 = da1_ref[...]
    mover.put(da1_ref.at[pl.ds(pl.multiple_of(core * TOK, TOK), TOK), :], da1_own_hbm)
    da1_send_ref[...] = da1_ref[pl.ds(pl.multiple_of((1 - core) * TOK, TOK), TOK), :].astype(BF)
    mover.put(da1_send_ref, da1_send_hbm)
    unit, _ = centred(x_ref[:, :WIDTH].astype(F32))
    spots = x_ref[:, WIDTH:].astype(F32)
    halves = lambda v: [v[:, :HALF], v[:, HALF:]]
    tail += halves(jnp.sum(da1 * unit, axis=0, keepdims=True))
    tail += halves(jnp.sum(da1, axis=0, keepdims=True))
    tail += [jnp.sum(angle * spots[:, f : f + 1], axis=0, keepdims=True) for f in range(2)]
    for i in range(4):
        tail += halves(sums_ref[i : i + 1, :])
    for h in range(2):
        tail += halves(more_ref[h : h + 1, :])
    tail += [jnp.zeros((11, HALF), F32)]
    tail_ref[...] = jnp.concatenate(tail, axis=0).astype(BF)
    for ref in low_hbms:
        for i in range(4):
            mover.put(tail_ref.at[pl.ds(16 * (i % 2), 16), :], ref.at[i, pl.ds(96, 16), :])
    mover.finish()
    for k in range(4):
        wait_all(high_copies(0, k))


def qkv_grad_call(place, near, kept, ids, more):
    return whole_call(
        qkv_grad_kernel, "qkv_grad",
        [((4, 112, HALF), BF)] * 4 + [((4, 96, HALF), BF)] * 4 + [((TOK, WIDTH), F32), ((TOK, WIDTH), BF)],
        place, [*near, *kept, ids, more],
        scratch=[
            pltpu.VMEM((CHIP_TOK, WIDTH), F32), pltpu.VMEM((TOK, WIDTH), BF),
            pltpu.VMEM((4, WIDTH, HALF), BF), pltpu.VMEM((32, HALF), BF),
            pltpu.VMEM((2, CHIP_TOK, HALF), F32), pltpu.VMEM((4 * TOK, 1), F32),
            pltpu.VMEM((1, 4 * TOK), F32), pltpu.VMEM((2, WIDTH), F32), pltpu.SemaphoreType.DMA((48,)),
            pltpu.SemaphoreType.DMA((4, 4)),
        ],
        flops=3 * 10**9, vmem=20, far=tuple(range(10)), away=(14, 15),
    )


def total_of(refs):
    total = refs[0][...].astype(F32)
    for ref in refs[1:]:
        total = total + ref[...].astype(F32)
    return total.astype(BF)


def four_kernel(core_ref, *refs):
    sources, out_ref, in_ref, sems = refs[:4], *refs[4:]
    wait_all(Mover(sems).load([(source, in_ref.at[i]) for i, source in enumerate(sources)]))
    out_ref[...] = total_of([in_ref.at[i] for i in range(4)])


def mid_kernel(place_ref, *refs):
    sources, out_low, out_high = refs[:10], refs[10:14], refs[14:18]
    low_ref, high_ref, mlp_ref, rest_ref, sems = refs[18:]
    targets = [r.at[i] for r in (high_ref, low_ref) for i in range(4)] + [mlp_ref, rest_ref]
    copies = Mover(sems).load(tuple(zip(sources, targets)))
    x, y = place_ref[4], place_ref[1]

    def total(ref):
        value = ref[0].astype(F32)
        for i in range(1, 4):
            value = value + ref[i].astype(F32)
        ref[0] = value.astype(BF)

    for i, ref in enumerate((high_ref, low_ref)):
        wait_all(copies[4 * i : 4 * i + 4])
        total(ref)
    wait_all(copies[8:])
    for k in range(4):
        to_y, to_x = lax.bitwise_and(y + 4 - k, 3), lax.bitwise_and(x + 4 - k, 3)
        out_low[k][:96, :WIDTH] = mlp_ref[to_y]
        out_low[k][:96, WIDTH:] = low_ref[0, to_y, :96, :]
        for i in range(3):
            first = 96 + 8 * (i % 2)
            out_low[k][96:, HALF * i : HALF * i + HALF] = low_ref[0, i // 2, first : first + 8, :]
        out_high[k][:, :WIDTH] = rest_ref[to_x]
        out_high[k][:, WIDTH:] = high_ref[0, to_x]


def join_kernel(core_ref, *refs):
    low, high, out_ref = total_of(refs[:4]), total_of(refs[4:8]), refs[8]
    for i in range(8):
        part = (low, high)[i // 4]
        out_ref[i, :24, :] = part[24 * (i % 4) : 24 * (i % 4) + 24]
        out_ref[i, 24:, :] = low[96:]


def total_kernel(core_ref, in_ref, out_ref):
    total = in_ref[0].astype(F32)
    for i in range(1, 8):
        total = total + in_ref[i].astype(F32)
    out_ref[...] = total.astype(BF)


def share_kernel(place_ref, own_ref, got_ref, out_ref):
    core, y = place_ref[0], place_ref[1]
    own, got = own_ref[...].astype(F32), got_ref[...].astype(F32)
    own_rows = pick(core, own[:12], own[12:24])
    got_rows = pick(core, got[:12], got[12:24])
    both = jnp.concatenate([pick(core, own_rows, got_rows), pick(core, got_rows, own_rows)], axis=0)
    out_ref[:24, WIDTH:] = both[:, WIDTH:].astype(BF)
    out_ref[:24, :WIDTH] = jnp.where(y < 2, both[:, :WIDTH], own[:24, :WIDTH]).astype(BF)
    out_ref[24:32, :] = pick(core, own[24:], got[24:]).astype(BF)
    out_ref[32:, :] = pick(core, got[24:], own[24:]).astype(BF)


def last_kernel(
    place_ref, part0_ref, part1_ref, part2_ref, part3_ref,
    qkv_ref, out_ref, up_ref, down_ref, *refs,
):
    small_refs, freq_ref, scr_ref = refs[:8], refs[8], refs[9]
    core, y, chip = place_ref[0], place_ref[1], place_ref[2]
    device = (2 * chip + core).astype(F32)
    for i, ref in enumerate((part0_ref, part1_ref, part2_ref, part3_ref)):
        scr_ref[i] = ref[...].astype(F32)
    ups = []
    for q in range(4):
        rows = scr_ref[lax.bitwise_and(q + 4 - y, 3)]
        for c in range(2):
            cols = rows[12 * c : 12 * c + 12, WIDTH:]
            if q < 3:
                qkv_ref[:, WIDTH * q + HALF * c : WIDTH * q + HALF * c + HALF] = cols
            else:
                out_ref[:, HALF * c : HALF * c + HALF] = cols
            if q < 2:
                ups.append((c, q, rows[12 * c : 12 * c + 12, :WIDTH]))
        if q > 1:
            down_ref[24 * (q - 2) : 24 * (q - 2) + 24, :] = rows[:24, :WIDTH]
    group, inner = split_index(lax.broadcasted_iota(jnp.int32, (HALF, 1), 0).astype(F32), 24)
    col = lax.broadcasted_iota(jnp.int32, (HALF, 4 * HALF), 1).astype(F32)
    spread_out = jnp.where(col == 96.0 * group + inner, 1.0, 0.0).astype(BF)
    stack = jnp.concatenate(
        [jnp.concatenate([piece, jnp.zeros((4, WIDTH), F32)], axis=0) for _, _, piece in ups], axis=0
    ).astype(BF)
    for g in range(2):
        parts = dot(stack[:, HALF * g : HALF * g + HALF], spread_out)
        total = parts[:12]
        for i, (c, q, _) in enumerate(ups):
            if i:
                total = total + pltpu.roll(parts[16 * i : 16 * i + 16], 48 * c + 24 * q, 1)[:12]
        up_ref[:, 4 * HALF * g : 4 * HALF * g + 4 * HALF] = total
    rows = scr_ref[lax.bitwise_and(7 - y, 3)]
    tails = [
        jnp.concatenate(
            [rows[24 + 8 * c : 32 + 8 * c, HALF * k : HALF * k + HALF] for k in range(3)], axis=0
        ).astype(BF)
        for c in range(2)
    ]
    sub = lax.broadcasted_iota(jnp.int32, (HALF, 128), 0).astype(F32)
    lane = lax.broadcasted_iota(jnp.int32, (HALF, 128), 1).astype(F32)

    def take(tail, want, limit):
        hot = jnp.where(jnp.logical_and(sub == want, lane < limit), 1.0, 0.0).astype(BF)
        return dot(tail, hot)

    entry = 12.0 * device + lane
    low = sum(take(tail, entry, 12) for tail in tails)
    high = sum(take(tail, entry - HALF, 12) for tail in tails)
    rows = [low[3 + i : 4 + i] + high[4 + i : 5 + i] for i in (0, 2, 6, 8, 10, 12)]
    entry = 36.0 * device + lane
    bias = 0.0
    for t in range(3):
        for c in range(2):
            bias = bias + take(tails[c], entry - (WIDTH * t + HALF * c), 36)[t : t + 1]
    rows.append(bias)
    own = pick(core, tails[0], tails[1])
    entry = 24.0 * chip.astype(F32) + lane
    bias = 0.0
    for h in range(2):
        shifted = entry - 24.0 * h
        fits = jnp.logical_and(lane >= 24.0 * h, lane < 24.0 * h + 24.0)
        for k in range(2):
            want = jnp.where(fits, shifted - HALF * k, -1.0)
            bias = bias + take(own, want, 48)[17 + 2 * h + k : 18 + 2 * h + k]
    rows.append(bias)
    side = jnp.where(chip < 16, 0.0, 1.0)
    source = jnp.where(chip < 16, tails[0], tails[1])
    head, inner = split_index(6.0 * device + lane - 192.0 * side, 32)
    freq = take(source, 64.0 * head + inner, 6)
    freq_ref[...] = freq[7:9, :6]
    for ref, row in zip(small_refs, rows):
        ref[...] = row[0, : ref.shape[0]]


def per_device(
    tokens, image_ids, patch_row, patch_col, cotangent,
    norm1_gain, norm1_bias, qkv_weight, qkv_bias, frequencies, out_weight, out_bias,
    norm2_gain, norm2_bias, up_weight, up_bias, down_weight, down_bias,
):
    x, y, z, core = (lax.axis_index(a) for a in ("x", "y", "z", "c"))
    place = jnp.stack([core, y, x * NZ + z, z, x]).astype(jnp.int32)
    chip = x * NZ + z
    core_arr = core.reshape(1).astype(jnp.int32)

    groups = [norm1_gain, norm1_bias, out_bias, norm2_gain, norm2_bias, down_bias, qkv_bias, up_bias]
    small = jnp.concatenate(groups + [frequencies[0], frequencies[1], jnp.zeros((216,), BF)])[None]
    pieces = []
    for c in range(2):
        cols = [qkv_weight[:, WIDTH * i + HALF * c : WIDTH * i + HALF * c + HALF] for i in range(3)]
        cols.append(out_weight[:, HALF * c : HALF * c + HALF])
        piece = cols[3]
        for i in range(3):
            piece = jnp.where(y == i, cols[i], piece)
        pieces.append(jnp.concatenate([piece, small, jnp.zeros((3, HALF), BF)], axis=0))
    block = jnp.broadcast_to(jnp.stack(pieces)[None], (NZ, 2, 16, HALF)).reshape(256, HALF)
    up_split = up_weight.reshape(12, 32, 2, 2, 24)
    up_halves = [up_split[:, :, c].transpose(0, 2, 1, 3).reshape(12, FF_HALF) for c in range(2)]
    up_own = jnp.where(core == 0, up_halves[0], up_halves[1])
    up_other = jnp.where(core == 0, up_halves[1], up_halves[0])
    up_pack = in_core_order(core, up_own, swap(up_other))
    mlp_pack = jnp.concatenate([up_pack, down_weight[:24], down_weight[24:]], axis=1)

    f = ("x", "z", "c")
    onward = [(i, i + 1) for i in range(2 * NX * NZ - 1)]
    backward = [(b, a) for a, b in onward]
    spots = jnp.stack([patch_row[0], patch_col[0]], axis=1).astype(BF)
    own = jnp.concatenate([tokens[0], jnp.pad(spots, ((0, 0), (0, 126)))], axis=1)
    lower, upper = lax.ppermute(own, f, onward), lax.ppermute(own, f, backward)
    near = lax.dynamic_slice_in_dim(jnp.pad(image_ids[0] + 1, (TOK, TOK)), chip * CHIP_TOK, 4 * TOK, 0)
    ids = near[None].astype(F32)

    mlp = lax.all_gather(mlp_pack, ("x", "z"), axis=0, tiled=True)
    block = lax.all_to_all(block, ("z", "c"), split_axis=0, concat_axis=0, tiled=True)
    block = block.reshape(16, 16, HALF)
    rows, lines = block[:, :12].reshape(192, HALF), block[:, 12]
    low = jnp.concatenate([rows[:96], lines[:8]], axis=0)
    high = jnp.concatenate([rows[96:], lines[8:]], axis=0)
    low = jnp.stack(around_axis(low, "x", NX))
    high = jnp.stack(around_axis(high, "y", NY))
    low, high, lower, upper, dy_own = lax.optimization_barrier((low, high, lower, upper, cotangent[0]))
    edge = jnp.where(core == 0, lower, upper)
    far = swap(edge)
    sources = [own, lower, upper, far]
    dy_other = swap(dy_own)
    by_y = around_axis(low, "y", NY)
    by_x = around_axis(high, "x", NX)

    wide, half, square = ((CHIP_TOK, WIDTH), BF), ((CHIP_TOK, HALF), BF), ((HALF, HALF), BF)
    ids, *parts = lax.optimization_barrier((ids, *by_y, *by_x))
    q, k, v, keep, send, *kept = qkv_call(place, sources, parts[:4], parts[4:])
    q_kept, k_kept, v_kept, vec, a1, turn, weights, inputs = kept
    got = swap(send)
    branch, o, lse, out_rows = attend(core_arr, q, k, v, ids, keep, got)

    a2, middle = norm_call(core_arr, branch, swap(branch), inputs, vec)
    da2, *held, high, result, result_send, du_sums, l0, l1, l2, l3 = mlp_call(
        place, a2, vec, mlp, dy_own, dy_other, middle, o, out_rows, lse
    )
    output = (result + swap(result_send).astype(F32)).astype(BF)[None]
    mlp_lows = [fetch(part, "x", NX, k) for k, part in enumerate((l0, l1, l2, l3))]

    do, delta, to_prev, to_next, out_own, out_send, sums, dmid = whole_call(
        branch_kernel, "branch",
        [((CHIP_TOK, HALF), BF), ((3, 2, CHIP_TOK), F32), ((288, HALF), BF), ((288, HALF), BF),
         ((HALF, HALF), BF), ((HALF, HALF), BF), ((4, WIDTH), F32), ((TOK, WIDTH), F32)],
        core_arr, [da2, swap(da2), *held],
        scratch=[pltpu.VMEM((CHIP_TOK, WIDTH), F32), pltpu.SemaphoreType.DMA((2,))],
        flops=10**9, vmem=14, far=(7,),
    )
    high, do = lax.optimization_barrier((high, do))
    mlp_high = scatter_sum(high, "y").reshape(4, 96, WIDTH)
    up_list = [(i, i + 1) for i in range(NX * NZ - 1)]
    down_list = [(b, a) for a, b in up_list]
    from_prev = lax.ppermute(to_next, ("x", "z"), up_list)
    from_next = lax.ppermute(to_prev, ("x", "z"), down_list)
    dq, dkv, *kept = near_back(
        core_arr, [q_kept, k_kept, v_kept, turn, a1, inputs, weights], do, lse, delta, ids
    )
    *parts, da1_own, da1_send = qkv_grad_call(
        place, [dq, dkv, from_prev, from_next, out_own, swap(out_send), sums], kept, ids, du_sums
    )
    highs = [fetch(part, "y", NY, k) for k, part in enumerate(parts[4:])]
    lows = [fetch(part, "x", NX, k) for k, part in enumerate(parts[:4])]
    da1 = da1_own + swap(da1_send).astype(F32)
    unit, scale = centred(tokens[0].astype(F32))
    input_grad = (centred_back(unit, scale, da1 * vec[0]) + dmid)[None]

    (mlp_low,) = whole_call(
        four_kernel, "four", [((4, 96, WIDTH), BF)], core_arr, mlp_lows,
        scratch=[pltpu.VMEM((4, 4, 96, WIDTH), BF), pltpu.SemaphoreType.DMA((4,))],
        away=tuple(range(4)),
    )
    seconds = whole_call(
        mid_kernel, "mid", [((104, 3 * HALF), BF)] * 4 + [((96, 3 * HALF), BF)] * 4, place,
        [*highs, *lows, mlp_low, mlp_high],
        scratch=[
            pltpu.VMEM((4, 4, 112, HALF), BF), pltpu.VMEM((4, 4, 96, HALF), BF),
            pltpu.VMEM((4, 96, WIDTH), BF), pltpu.VMEM((4, 96, WIDTH), BF),
            pltpu.SemaphoreType.DMA((16,)),
        ],
        vmem=16, away=tuple(range(10)),
    )
    lows = [fetch(part, "y", NY, k) for k, part in enumerate(seconds[:4])]
    highs = [fetch(part, "x", NX, k) for k, part in enumerate(seconds[4:])]
    (joined,) = whole_call(
        join_kernel, "join", [((8, 32, 3 * HALF), BF)], core_arr, lows + highs
    )
    joined = lax.all_to_all(
        joined.reshape(256, 3 * HALF), "z", split_axis=0, concat_axis=0, tiled=True
    )
    (mine,) = whole_call(
        total_kernel, "total", [((32, 3 * HALF), BF)],
        core_arr, [joined.reshape(8, 32, 3 * HALF)],
    )
    (part,) = whole_call(
        share_kernel, "share", [((40, 3 * HALF), BF)], place, [mine, swap(mine)]
    )
    parts = [fetch(part, "y", NY, k) for k in range(NY)]
    qkv_grad, out_weight_grad, up_grad, down_grad, *smalls, freq_grad = whole_call(
        last_kernel, "last",
        [((12, 3 * WIDTH), F32), ((12, WIDTH), F32), ((12, 4 * WIDTH), F32), ((48, WIDTH), F32)]
        + [((size,), F32) for size in (12, 12, 12, 12, 12, 12, 36, 48)]
        + [((2, 6), F32)],
        place, parts, scratch=[pltpu.VMEM((4, 40, 3 * HALF), F32)],
    )
    qkv_bias_grad, up_bias_grad = smalls[6:]
    return (
        output, input_grad,
        smalls[0], smalls[1], qkv_grad, qkv_bias_grad, freq_grad, out_weight_grad, smalls[2],
        smalls[3], smalls[4], up_grad, up_bias_grad, down_grad, smalls[5],
    )


def solution(mesh):
    fine = Mesh(mesh.devices.reshape(NY, NX, NZ, 2), ("y", "x", "z", "c"))
    f = ("x", "z", "c")
    return jax.shard_map(
        per_device,
        mesh=fine,
        in_specs=(
            P("y", f, None), P("y", None), P("y", f), P("y", f), P("y", f, None),
            P(f), P(f), P(f, None), P(f), P(None, f), P(f, None), P(f),
            P(f), P(f), P(f, None), P(f), P(f, None), P(f),
        ),
        out_specs=(
            P("y", f, None), P("y", f, None),
            P(f), P(f), P(f, None), P(f), P(None, f), P(f, None), P(f),
            P(f), P(f), P(f, None), P(f), P(f, None), P(f),
        ),
        check_vma=False,
    )
```
